256 devices in a mesh: sec: 64 (over z, x, core), blk: 4 (over y).
Axes of the slice: x: 4, y: 4, z: 8, core: 2. Of those that a mesh axis runs over, the one named last changes fastest.
Arguments:
- state: float32 [8, 16384, 2048], P(None, 'sec', 'blk'), may hold values from -6 to 6
- velocity: float32 [2, 16384, 2048], P(None, 'sec', 'blk'), may hold values from -1 to 1
- limiter: int32 [16384, 2048], P('sec', 'blk'), may hold values from 0 to 1
- footpoint_owner: int32 [64, 4, 1024, 1], P('sec', 'blk'), may hold values from 0 to 63; in each aligned block of 1024 rows (0 to 1023, 1024 to 2047, ..., all dimensions but the last counted through in order) at most 32 rows name the same one
- footpoint_slot: int32 [64, 4, 1024, 1], P('sec', 'blk'), may hold values from 0 to 63
- conductance: float32 [1024, 2048], P('sec', 'blk'), may hold values from 1 to 10
- potential_prior: float32 [1024, 2048], P('sec', 'blk'), may hold values from -6 to 6
Outputs:
- new_state: float32 [8, 16384, 2048], P(None, 'sec', 'blk')
- shell_potential: float32 [1024, 2048], P('sec', 'blk')
- foot_potential: float32 [16384, 2048], P('sec', 'blk')
The draws below stay inside these ranges and needn't reach their ends.
Inputs may be any that keep to these rules, and one draw needn't show every extreme that they name: `footpoint_owner`: among the 1024 blocks of one device no section is named more than 32 times, a bound that some block reaches.
All inputs are finite; a program needn't handle non-finite values.
Results may differ from the reference program's by a relative error of at most 0.0003.
Values sent between devices are 32-bit elements; how exact they have to be, the bound alone decides.
A program may use at most 128 MiB of HBM per device.

```python
import math
import jax
import jax.numpy as jnp
import numpy as np
from jax import lax

NV = 8
CX = 256
CY = 512
SLAT = 16
SLON = 512
ITERS = 4
NBLK = 1024
CAP = 32
SB = 64
NX = 16384
NY = 2048
NLAT = 1024
NLON = 2048
N_SEC = 64
N_BLK = 4


def plant(values, rng, least, largest):
    index_at = [jax.random.randint(jax.random.fold_in(rng, axis), (), 0, length) for axis, length in enumerate(values.shape)]
    main_axis = values.shape.index(max(values.shape))
    next_to = index_at[:main_axis] + [(index_at[main_axis] + 1) % values.shape[main_axis]] + index_at[main_axis + 1:]
    return values.at[tuple(index_at)].set(least).at[tuple(next_to)].set(largest)


def levels(rng, dims, cuts, low, high):
    def one(axis_at, shards_of):
        steps = jax.random.uniform(jax.random.fold_in(jax.random.fold_in(rng, 6), axis_at), (shards_of,), jnp.float32, low / len(cuts), high / len(cuts))
        return jnp.repeat(jnp.exp(steps), dims[axis_at] // shards_of).reshape((-1,) + (1,) * (len(dims) - axis_at - 1))

    loudness = one(*cuts[0])
    for cut in cuts[1:]:
        loudness = loudness * one(*cut)
    return loudness


def assign_block(stream_key, own, number, rows, number_of, top, bound, slope):
    sequence = jax.random.permutation(stream_key, number_of)
    heavy_load, ordinary = load_shares(number_of, rows * top, bound, slope, True), load_shares(number_of, rows * top, bound, slope, False)
    places = jnp.arange(number_of)

    def named(tallies, rotation):
        used = int((tallies > 0).sum())
        fixed = max(1, used // 4)
        passed = fixed + (places - fixed + rotation * (used - fixed)) % max(1, number_of - fixed)
        return jnp.zeros((number_of,), jnp.int32).at[sequence[jnp.where(places < fixed, places, passed)]].set(jnp.asarray(tallies, jnp.int32))

    tallies = jnp.where(number % 4 == 0, named(heavy_load, number // 4), named(ordinary, number - number // 4 - 1))
    mixed = jax.random.permutation(jax.random.fold_in(own, 3), number_of)
    donor, receiver = mixed[0:number_of // 2 * 2:2], mixed[1:number_of // 2 * 2:2]
    margin = jnp.minimum(tallies[donor] - 1, bound - tallies[receiver]) // 2
    margin = jnp.where((donor == sequence[0]) | (receiver == sequence[0]) | (tallies[receiver] == 0), 0, jnp.maximum(margin, 0))
    passed = jax.random.randint(jax.random.fold_in(own, 4), (number_of // 2,), 0, 1 << 20) % (margin + 1)
    tallies = tallies.at[donor].add(-passed).at[receiver].add(passed)
    items = jnp.searchsorted(jnp.cumsum(tallies), jnp.arange(rows * top), side="right").astype(jnp.int32)
    listing = items.reshape(top, rows).T
    listing = listing[jax.random.permutation(jax.random.fold_in(own, 1), rows)]
    rotation = jax.random.randint(jax.random.fold_in(own, 2), (rows, 1), 0, top)
    return jnp.take_along_axis(listing, (jnp.arange(top)[None, :] + rotation) % top, axis=1)


def load_shares(count, total, reach, lean, full):
    weights = [(1 << 20) // math.isqrt(standing ** lean) + 1 for standing in range(1, count + 1)]
    largest = reach if full else min(reach, max(-(-total // count), total * weights[0] // sum(weights)))
    least = 1 if total - largest >= count - 1 else 0
    counts, spare = [largest] + [least] * (count - 1), total - largest - least * (count - 1)
    while spare > 0:
        candidates = [i for i in range(1, count) if counts[i] < largest] or [i for i in range(1, count) if counts[i] < reach]
        pool, left = sum([weights[i] for i in candidates]), spare
        for i in candidates:
            extra = min(reach - counts[i], max(1, left * weights[i] // pool), spare)
            counts[i] = counts[i] + extra
            spare = spare - extra
    return np.array(counts)


def normal_values(rng, dims, scale, reach, split=(), kind=jnp.bfloat16):
    gain = levels(rng, dims, split, -0.22, 0.18) if split else 1.0
    values = jax.random.normal(rng, dims, jnp.float32) * scale * gain
    return jnp.minimum(jnp.maximum(values, -reach), reach).astype(kind)


def setup_inputs(seed: int = 0) -> dict:
    splits = jax.random.split(jax.random.key(seed), 8)
    state = normal_values(splits[0], (NV, NX, NY), 1.0, 6.0, ((1, 64), (2, 4)), jnp.float32)
    velocity = jnp.clip(jax.random.uniform(splits[1], (2, NX, NY), jnp.float32, -1.0, 1.0) * levels(splits[1], (2, NX, NY), ((1, 64), (2, 4)), -0.4, 0.0), -1.0, 1.0)
    limiter = plant(jax.random.randint(splits[2], (NX, NY), 0, 2), jax.random.fold_in(splits[2], 1), 0, 1).astype(jnp.int32)
    footpoint_owner_keys = jax.random.split(jax.random.fold_in(splits[3], 1), N_SEC * N_BLK * NBLK // NBLK)
    footpoint_owner_turns = jax.random.permutation(jax.random.fold_in(splits[3], 3), N_SEC * N_BLK * NBLK // NBLK)
    footpoint_owner = jax.vmap(lambda own, number: assign_block(jax.random.fold_in(splits[3], 2), own, number, NBLK, N_SEC, 1, CAP, 2))(footpoint_owner_keys, footpoint_owner_turns).reshape((N_SEC, N_BLK, NBLK, 1))
    footpoint_slot = plant(jax.random.randint(splits[4], (N_SEC, N_BLK, NBLK, 1), 0, SB), jax.random.fold_in(splits[4], 1), 0, SB - 1).astype(jnp.int32)
    conductance = jnp.clip(jnp.exp(math.log(10.0) - 2.3025851 * jax.random.uniform(splits[5], (NLAT, NLON), jnp.float32) ** levels(splits[5], (NLAT, NLON), ((0, 64), (1, 4)), -0.2, 0.2)), 1.0, 10.0)
    potential_prior = normal_values(splits[6], (NLAT, NLON), 1.0, 6.0, ((0, 64), (1, 4)), jnp.float32)
    return {"state": state, "velocity": velocity, "limiter": limiter, "footpoint_owner": footpoint_owner, "footpoint_slot": footpoint_slot, "conductance": conductance, "potential_prior": potential_prior}


courant = 0.4
leak = 1.0


def minmod(lower_diff, upper_diff):
    return jnp.where(lower_diff * upper_diff > 0.0, jnp.sign(lower_diff) * jnp.minimum(jnp.abs(lower_diff), jnp.abs(upper_diff)), 0.0)


def window(array, off_x, off_y):
    return array[..., 2 + off_x:array.shape[-2] - 2 + off_x, 2 + off_y:array.shape[-1] - 2 + off_y]


def flux_change(field, speed, weight, along_x):
    def shifted(array, offset):
        return window(array, offset, 0) if along_x else window(array, 0, offset)

    slopes = [shifted(weight, offset) * minmod(shifted(field, offset) - shifted(field, offset - 1), shifted(field, offset + 1) - shifted(field, offset)) for offset in (-1, 0, 1)]
    fluxes = []
    for offset in (-1, 0):
        left_value = shifted(field, offset) + 0.5 * slopes[offset + 1]
        right_value = shifted(field, offset + 1) - 0.5 * slopes[offset + 2]
        face_speed = 0.5 * (shifted(speed, offset) + shifted(speed, offset + 1))
        fluxes.append(jnp.where(face_speed > 0.0, face_speed * left_value, face_speed * right_value))
    return fluxes[1] - fluxes[0]


def advance(field, speed_x, speed_y, weight):
    return window(field, 0, 0) - courant * (flux_change(field, speed_x, weight, True) + flux_change(field, speed_y, weight, False))


def curl_field(padded):
    field_x = padded[0]
    field_y = padded[1]
    return 0.5 * (field_y[2:, 1:-1] - field_y[:-2, 1:-1]) - 0.5 * (field_x[1:-1, 2:] - field_x[1:-1, :-2])


def relax(potential_ext, sigma_ext, source):
    centre = sigma_ext[1:-1, 1:-1]
    north = 0.5 * (centre + sigma_ext[:-2, 1:-1])
    south = 0.5 * (centre + sigma_ext[2:, 1:-1])
    west = 0.5 * (centre + sigma_ext[1:-1, :-2])
    east = 0.5 * (centre + sigma_ext[1:-1, 2:])
    total = north * potential_ext[:-2, 1:-1] + south * potential_ext[2:, 1:-1] + west * potential_ext[1:-1, :-2] + east * potential_ext[1:-1, 2:] + source
    return total / (north + south + west + east + leak)


def reference(state, velocity, limiter, footpoint_owner, footpoint_slot, conductance, potential_prior):
    speed_x = jnp.pad(velocity[0], 2, mode="wrap")
    speed_y = jnp.pad(velocity[1], 2, mode="wrap")
    weight = jnp.pad(limiter.astype(jnp.float32), 2, mode="wrap")

    def one_quantity(field):
        return advance(jnp.pad(field, 2, mode="wrap"), speed_x, speed_y, weight)

    new_state = lax.map(one_quantity, state)
    fields = jnp.pad(new_state[NV - 2:], ((0, 0), (1, 1), (1, 1)), mode="wrap")
    current = curl_field(fields)
    blocks = current.reshape(N_SEC, CX, N_BLK, CY).transpose(0, 2, 1, 3).reshape(N_SEC * N_BLK * NBLK, 128)
    column = jnp.arange(N_BLK, dtype=jnp.int32)[None, :, None]
    target = ((footpoint_owner[..., 0] * N_BLK + column) * SB + footpoint_slot[..., 0]).reshape(-1).astype(jnp.int32)
    source_blocks = jax.ops.segment_sum(blocks, target, num_segments=N_SEC * N_BLK * SB)
    source = source_blocks.reshape(N_SEC, N_BLK, SLAT, SLON).transpose(0, 2, 1, 3).reshape(NLAT, NLON)
    sigma_ext = jnp.pad(conductance, 1)
    potential = potential_prior
    for step in range(ITERS):
        potential = relax(jnp.pad(potential, 1), sigma_ext, source)
    table = potential.reshape(N_SEC, SLAT, N_BLK, SLON).transpose(0, 2, 1, 3).reshape(N_SEC * N_BLK * SB, 128)
    foot_blocks = table[target]
    foot_potential = foot_blocks.reshape(N_SEC, N_BLK, CX, CY).transpose(0, 2, 1, 3).reshape(NX, NY)
    return new_state, potential, foot_potential
```

```python
import jax
import jax.numpy as jnp
from jax import lax
from jax.experimental import pallas as pl
from jax.experimental.pallas import tpu as pltpu
from jax.sharding import PartitionSpec as P

ITERS = 4
CORES = 2
TOP = 16
PAD = 40
GROUPS = 8
MESH = pl.DeviceIdType.MESH


def minmod(a, b):
    return jnp.maximum(jnp.minimum(a, b), jnp.minimum(jnp.maximum(a, b), 0.0))


def lane_next(tiles, lane):
    rolled = [pltpu.roll(t, 127, 1) for t in tiles]
    n = len(tiles)
    return [jnp.where(lane == 127, rolled[(j + 1) % n], rolled[j]) for j in range(n)]


def lane_prev(tiles, lane):
    rolled = [pltpu.roll(t, 1, 1) for t in tiles]
    return [jnp.where(lane == 0, rolled[j - 1], rolled[j]) for j in range(len(tiles))]


def kernel(
    dims,
    state,
    velocity,
    limiter,
    sigma,
    prior,
    row_target,
    target,
    out_state,
    out_phi,
    out_foot,
    grid,
    flags,
    fresh,
    face_x,
    face_y,
    packs,
    edges,
    corners,
    packs_o,
    edges_o,
    shell,
    weights,
    dense_sib,
    dense_own,
    got_sib,
    got_x,
    z_part,
    got_z,
    table,
    foot,
    load_sem,
    out_sem,
    send_sem,
    recv_sem,
):
    zs, xs, secs, blks, nq, cx, cy, lat, lon = dims
    nj = cy // 128
    sb = lat * lon // 128
    me = lax.axis_index("sec")
    col = lax.axis_index("blk")
    core = lax.rem(me, CORES)
    at_x = lax.rem(lax.div(me, CORES), xs)
    at_z = lax.div(me, CORES * xs)

    def sec_of(z, x, c):
        return (z * xs + x) * CORES + c

    up, down = lax.rem(me + secs - 1, secs), lax.rem(me + 1, secs)
    left, right = lax.rem(col + blks - 1, blks), lax.rem(col + 1, blks)
    sibling = (me + 1 - 2 * core, col)
    x_peer = {d: (sec_of(at_z, lax.rem(at_x + d, xs), core), col) for d in range(1, xs)}
    z_peer = {d: (sec_of(lax.rem(at_z + d, zs), at_x, core), col) for d in range(1, zs)}
    compass = {
        (-1, 0): (up, col),
        (1, 0): (down, col),
        (0, -1): (me, left),
        (0, 1): (me, right),
        (-1, -1): (up, left),
        (-1, 1): (up, right),
        (1, -1): (down, left),
        (1, 1): (down, right),
    }

    used = [0]
    sent = []

    def send(src, dst, device):
        n = used[0]
        used[0] += 1
        copy = pltpu.make_async_remote_copy(
            src_ref=src,
            dst_ref=dst,
            send_sem=send_sem.at[n],
            recv_sem=recv_sem.at[n],
            device_id=device,
            device_id_type=MESH,
        )
        copy.start()
        sent.append(copy)
        return copy

    loads = {}

    def load(name, src, dst):
        copy = pltpu.make_async_copy(src, dst, load_sem.at[len(loads)])
        copy.start()
        loads[name] = copy

    mid = slice(TOP, TOP + cx)
    for j in range(nj):
        lanes = slice(128 * j, 128 * j + 128)
        load(("f", j), state.at[nq - 2 : nq, :, lanes], grid.at[nq - 2 : nq, j, mid, :])
        load(("v", j), velocity.at[:, :, lanes], grid.at[nq : nq + 2, j, mid, :])
        load(("l", j), limiter.at[:, lanes], flags.at[j])
    load("sigma", sigma, shell.at[0, 8 : 8 + lat, 128 : 128 + lon])
    load("prior", prior, shell.at[1, 8 : 8 + lat, 128 : 128 + lon])
    for j in range(nj):
        lanes = slice(128 * j, 128 * j + 128)
        load(("o", j), state.at[: nq - 2, :, lanes], grid.at[: nq - 2, j, mid, :])

    barrier = pltpu.get_barrier_semaphore()
    partners = [*compass.values(), *x_peer.values(), *z_peer.values(), sibling]
    for device in partners:
        pl.semaphore_signal(barrier, inc=1, device_id=device, device_id_type=MESH)
    pl.semaphore_wait(barrier, len(partners))

    lane = lax.broadcasted_iota(jnp.int32, (8, 128), 1)
    sub = lax.broadcasted_iota(jnp.int32, (8, 128), 0)

    for j in range(nj):
        for name in ("f", "v", "l"):
            loads[(name, j)].wait()
    for j in range(nj):
        grid[nq + 2, j, mid, :] = 0.5 * flags[j].astype(jnp.float32)
    first = nq - 2
    fields = slice(first, first + 5)
    top, bottom = slice(TOP, TOP + 8), slice(TOP + cx - 8, TOP + cx)
    above, below = slice(TOP - 8, TOP), slice(TOP + cx, TOP + cx + 8)
    halo = []
    halo.append(send(grid.at[fields, 0:nj, bottom, :], grid.at[fields, 0:nj, above, :], (down, col)))
    halo.append(send(grid.at[fields, 0:nj, top, :], grid.at[fields, 0:nj, below, :], (up, col)))

    rows = cx // GROUPS
    wide = lax.broadcasted_iota(jnp.int32, (rows, 128), 1)

    def pack(base, count, width):
        at_left = jnp.zeros((rows, 128), jnp.float32)
        at_right = jnp.zeros((rows, 128), jnp.float32)
        for g in range(GROUPS):
            here = slice(TOP + g * rows, TOP + (g + 1) * rows)
            for a in range(count):
                at = 16 * g + width * a
                mask = (wide >= at) & (wide < at + width)
                at_left = jnp.where(mask, pltpu.roll(grid[base + a, 0, here, :], at, 1), at_left)
                moved = pltpu.roll(grid[base + a, nj - 1, here, :], (at + width) % 128, 1)
                at_right = jnp.where(mask, moved, at_right)
        return at_left, at_right

    def unpack(base, count, width, from_left, from_right, take, put, size, group):
        side = lax.broadcasted_iota(jnp.int32, (size, 128), 1) < 64
        for a in range(count):
            at = 16 * group + width * a
            r = pltpu.roll(from_right[take, :], (128 - at) % 128, 1)
            l = pltpu.roll(from_left[take, :], (256 - width - at) % 128, 1)
            grid[base + a, nj, put, :] = jnp.where(side, r, l)

    to_left, to_right = pack(first, 5, 3)
    packs[0] = to_left
    packs[1] = to_right
    halo.append(send(packs.at[1], edges.at[0], (me, right)))
    halo.append(send(packs.at[0], edges.at[1], (me, left)))
    halo.append(send(packs.at[1, rows - 8 : rows, :], corners.at[0], (down, right)))
    halo.append(send(packs.at[0, rows - 8 : rows, :], corners.at[1], (down, left)))
    halo.append(send(packs.at[1, 0:8, :], corners.at[2], (up, right)))
    halo.append(send(packs.at[0, 0:8, :], corners.at[3], (up, left)))

    row_src = {0: slice(8, 8 + lat), 1: slice(lat, lat + 8), -1: slice(8, 16)}
    row_dst = {0: slice(8, 8 + lat), 1: slice(0, 8), -1: slice(8 + lat, 16 + lat)}
    lane_src = {0: slice(128, 128 + lon), 1: slice(lon, lon + 128), -1: slice(128, 256)}
    lane_dst = {0: slice(128, 128 + lon), 1: slice(0, 128), -1: slice(128 + lon, 256 + lon)}

    def shell_halo(which):
        return [
            send(
                shell.at[which, row_src[dr], lane_src[dc]],
                shell.at[which, row_dst[dr], lane_dst[dc]],
                device,
            )
            for (dr, dc), device in compass.items()
        ]

    loads["sigma"].wait()
    loads["prior"].wait()
    shell_copies = shell_halo(slice(0, 2))

    for j in range(nj):
        loads[("o", j)].wait()
    others = slice(0, nq - 2)
    halo_o = [
        send(grid.at[others, 0:nj, bottom, :], grid.at[others, 0:nj, above, :], (down, col)),
        send(grid.at[others, 0:nj, top, :], grid.at[others, 0:nj, below, :], (up, col)),
    ]
    to_left, to_right = pack(0, nq - 2, 2)
    packs_o[0] = to_left
    packs_o[1] = to_right
    halo_o.append(send(packs_o.at[1], edges_o.at[0], (me, right)))
    halo_o.append(send(packs_o.at[0], edges_o.at[1], (me, left)))

    for copy in halo:
        copy.wait_recv()
    for g in range(GROUPS):
        here = slice(TOP + g * rows, TOP + (g + 1) * rows)
        unpack(first, 5, 3, edges.at[0], edges.at[1], slice(0, rows), here, rows, g)
    unpack(first, 5, 3, corners.at[0], corners.at[1], slice(0, 8), above, 8, GROUPS - 1)
    unpack(first, 5, 3, corners.at[2], corners.at[3], slice(0, 8), below, 8, 0)

    def tile(ref, *at):
        return ref[at]

    def faces(k, carry):
        b = pl.multiple_of(8 * k, 8)
        speed_y = [grid[nq + 1, j, pl.ds(b, 8), :] for j in range(nj + 1)]
        for j, (here, after) in enumerate(zip(speed_y, lane_next(speed_y, lane))):
            face_y[j, pl.ds(b, 8), :] = 0.2 * (here + after)
            face_x[j, pl.ds(b, 8), :] = 0.2 * (
                grid[nq, j, pl.ds(b, 8), :] + grid[nq, j, pl.ds(b + 1, 8), :]
            )
        return carry

    lax.fori_loop(1, TOP // 8 + cx // 8 + 1, faces, 0)

    def advect(q, tiles_x, last):
        def slopes(k):
            b = pl.multiple_of(8 * k, 8)
            lefts, rights = [], []
            for j in range(tiles_x):
                here = grid[q, j, pl.ds(b, 8), :]
                lower = here - grid[q, j, pl.ds(b - 1, 8), :]
                upper = grid[q, j, pl.ds(b + 1, 8), :] - here
                half = minmod(lower, upper) * grid[nq + 2, j, pl.ds(b, 8), :]
                lefts.append(here + half)
                rights.append(here - half)
            return tuple(lefts), tuple(pltpu.roll(r, 7, 0) for r in rights)

        def step(k, carry):
            lefts, rights, flux_before = carry
            lefts_k, rights_k = slopes(k)
            b = pl.multiple_of(8 * (k - 1), 8)
            here = [grid[q, j, pl.ds(b, 8), :] for j in range(nj + 1)]
            diff = [after - h for h, after in zip(here, lane_next(here, lane))]
            lim = [grid[nq + 2, j, pl.ds(b, 8), :] for j in range(nj + 1)]
            half = [
                minmod(lower, upper) * w
                for lower, upper, w in zip(lane_prev(diff, lane), diff, lim)
            ]
            after = lane_next([h - s for h, s in zip(here, half)], lane)
            flux_y = []
            for j in range(nj + 1):
                speed = face_y[j, pl.ds(b, 8), :]
                flux_y.append(speed * jnp.where(speed > 0.0, here[j] + half[j], after[j]))
            before_y = lane_prev(flux_y, lane)
            flux_rolled = []
            for j in range(tiles_x):
                speed = face_x[j, pl.ds(b, 8), :]
                follow = jnp.where(sub == 7, rights_k[j], rights[j])
                flux = speed * jnp.where(speed > 0.0, lefts[j], follow)
                rolled = pltpu.roll(flux, 1, 0)
                flux_rolled.append(rolled)
                change = (flux - jnp.where(sub == 0, flux_before[j], rolled)) + (
                    flux_y[j] - before_y[j]
                )
                fresh[q, j, pl.ds(b, 8), :] = here[j] - change
            return lefts_k, rights_k, tuple(flux_rolled)

        zero = tuple(jnp.zeros((8, 128), jnp.float32) for _ in range(tiles_x))
        lefts, rights = slopes(1)
        lax.fori_loop(2, last + 1, step, (lefts, rights, zero))

    end = TOP // 8 + cx // 8 + 1
    advect(nq - 2, nj + 1, end)
    advect(nq - 1, nj + 1, end)

    writes = []

    def write(src, dst):
        copy = pltpu.make_async_copy(src, dst, out_sem.at[len(writes)])
        copy.start()
        writes.append(copy)

    for j in range(nj):
        lanes = slice(128 * j, 128 * j + 128)
        write(fresh.at[nq - 2 : nq, j, mid, :], out_state.at[nq - 2 : nq, :, lanes])

    chunk = 16
    lane_c = lax.broadcasted_iota(jnp.int32, (chunk, 128), 1)

    def curl(k, carry):
        b = pl.multiple_of(TOP + chunk * k, 8)
        field_x = [fresh[nq - 2, j, pl.ds(b, chunk), :] for j in range(nj + 1)]
        after = lane_next(field_x, lane_c)
        before = lane_prev(field_x, lane_c)
        for j in range(nj):
            current = 0.5 * (
                fresh[nq - 1, j, pl.ds(b + 1, chunk), :] - fresh[nq - 1, j, pl.ds(b - 1, chunk), :]
            ) - 0.5 * (after[j] - before[j])
            high = current.astype(jnp.bfloat16)
            low = (current - high.astype(jnp.float32)).astype(jnp.bfloat16)
            r = pl.multiple_of(j * cx + chunk * k, chunk)
            weights[pl.ds(r, chunk), 0:128] = high
            weights[pl.ds(r, chunk), 128:256] = low
        return carry

    lax.fori_loop(0, cx // chunk, curl, 0)

    per_x = zs * sb
    size = min(256, per_x)

    def sums(base, store):
        def one(i, carry):
            at = pl.multiple_of(i * size, size)
            ids = lax.broadcasted_iota(jnp.int32, (size, nj * cx), 0) + (base + at)
            chosen = jnp.where(ids == row_target[...], 1.0, 0.0).astype(jnp.bfloat16)
            both = jnp.dot(chosen, weights[...], preferred_element_type=jnp.float32)
            store[pl.ds(at, size), :] = both[:, :128] + both[:, 128:]
            return carry

        lax.fori_loop(0, per_x // size, one, 0)

    order = sorted(range(1, xs), key=lambda d: -min(d, xs - d)) + [0]
    sib_copies, x_copies = {}, {}

    def for_sibling(d):
        base = ((1 - core) * xs + lax.rem(at_x + d, xs)) * per_x
        sums(base, dense_sib.at[d])
        sib_copies[d] = send(dense_sib.at[d], got_sib.at[d], sibling)

    def for_own(d):
        base = (core * xs + lax.rem(at_x + d, xs)) * per_x
        sums(base, dense_own.at[d])
        sib_copies[d].wait_recv()
        dense_own[d] = dense_own[d] + got_sib[d]
        if d:
            x_copies[d] = send(dense_own.at[d], got_x.at[d - 1], x_peer[d])

    for_sibling(order[0])
    for i, d in enumerate(order):
        if i + 1 < len(order):
            for_sibling(order[i + 1])
        for_own(d)

    for copy in halo_o:
        copy.wait_recv()
    for g in range(GROUPS):
        here = slice(TOP + g * rows, TOP + (g + 1) * rows)
        unpack(0, nq - 2, 2, edges_o.at[0], edges_o.at[1], slice(0, rows), here, rows, g)

    def other(q, carry):
        advect(q, nj, end - 1)
        return carry

    lax.fori_loop(0, nq - 2, other, 0)
    for j in range(nj):
        lanes = slice(128 * j, 128 * j + 128)
        write(fresh.at[0 : nq - 2, j, mid, :], out_state.at[0 : nq - 2, :, lanes])

    for copy in x_copies.values():
        copy.wait_recv()
    total = dense_own[0]
    for d in range(1, xs):
        total = total + got_x[d - 1]
    z_part[...] = total
    z_copies = []
    for d in range(1, zs):
        at = pl.multiple_of(lax.rem(at_z + d, zs) * sb, sb)
        z_copies.append(send(z_part.at[pl.ds(at, sb), :], got_z.at[d - 1], z_peer[d]))
    source = z_part[pl.ds(pl.multiple_of(at_z * sb, sb), sb), :]
    for d in range(1, zs):
        z_copies[d - 1].wait_recv()
        source = source + got_z[d - 1]
    for c in range(lon // 128):
        at = 128 + 128 * c
        shell[2, 8 : 8 + lat, at : at + 128] = source[c * lat : (c + 1) * lat, :]
    source_copies = shell_halo(slice(2, 3))

    for copy in shell_copies:
        copy.wait_recv()
    shape = (lat + 16, lon + 256)
    lat_at = lax.broadcasted_iota(jnp.int32, shape, 0) + (me * lat - 8)
    lon_at = lax.broadcasted_iota(jnp.int32, shape, 1) + (col * lon - 128)
    inside = (lat_at >= 0) & (lat_at < secs * lat) & (lon_at >= 0) & (lon_at < blks * lon)
    sig = jnp.where(inside, shell[0], 0.0)
    phi = jnp.where(inside, shell[1], 0.0)

    def around(a):
        return (
            pltpu.roll(a, 1, 0),
            pltpu.roll(a, lat + 15, 0),
            pltpu.roll(a, 1, 1),
            pltpu.roll(a, lon + 255, 1),
        )

    ways = [0.5 * (sig + other_sig) for other_sig in around(sig)]
    inverse = 1.0 / (ways[0] + ways[1] + ways[2] + ways[3] + 1.0)
    for copy in source_copies:
        copy.wait_recv()
    src = shell[2]
    for _ in range(ITERS):
        n, s, w, e = around(phi)
        total = ways[0] * n + ways[1] * s + ways[2] * w + ways[3] * e + src
        phi = jnp.where(inside, total * inverse, 0.0)
    phi = phi[8 : 8 + lat, 128 : 128 + lon]
    out_phi[...] = phi

    def piece(z, x, c):
        return table.at[pl.ds(pl.multiple_of(((c * xs + x) * zs + z) * sb, sb), sb), :]

    mine = ((core * xs + at_x) * zs + at_z) * sb
    for c in range(lon // 128):
        at = pl.multiple_of(mine + c * lat, lat)
        table[pl.ds(at, lat), :] = phi[:, c * 128 : (c + 1) * 128]

    from_z, from_x, from_sib = {}, {}, []
    own = piece(at_z, at_x, core)
    nearest = sorted(range(1, zs), key=lambda d: min(d, zs - d))
    for d in nearest:
        from_z[d] = send(own, own, z_peer[d])
    for dz in [0] + nearest:
        if dz:
            from_z[dz].wait_recv()
        z = lax.rem(at_z + zs - dz, zs)
        part = piece(z, at_x, core)
        for dx in range(1, xs):
            from_x[dz, dx] = send(part, part, x_peer[dx])
        from_sib.append(send(part, part, sibling))
    for dz in [0] + nearest:
        for dx in range(1, xs):
            from_x[dz, dx].wait_recv()
            z = lax.rem(at_z + zs - dz, zs)
            part = piece(z, lax.rem(at_x + xs - dx, xs), core)
            from_sib.append(send(part, part, sibling))
    for copy in from_sib:
        copy.wait_recv()

    def look_up(k, carry):
        b = pl.multiple_of(8 * k, 8)
        for r in range(8):
            for j in range(nj):
                at = target[(b + r) * nj + j]
                foot[j, pl.ds(b + r, 1), :] = table[pl.ds(at, 1), :]
        return carry

    lax.fori_loop(0, cx // 8, look_up, 0)
    for j in range(nj):
        write(foot.at[j], out_foot.at[:, 128 * j : 128 * j + 128])
    for copy in sent:
        copy.wait_send()
    for copy in writes:
        copy.wait()


def on_device(
    state, velocity, limiter, footpoint_owner, footpoint_slot, conductance, potential_prior
):
    secs, blks = lax.axis_size("sec"), lax.axis_size("blk")
    xs = 4 if secs % 8 == 0 and secs >= 32 else 2
    zs = secs // (CORES * xs)
    nq, cx, cy = state.shape
    lat, lon = conductance.shape
    nj = cy // 128
    sb = lat * lon // 128
    blocks = nj * cx
    owner = footpoint_owner.reshape(blocks)
    slot = footpoint_slot.reshape(blocks)
    per_row = lon // 128
    slot = (slot % per_row) * lat + slot // per_row
    core, x, z = owner % CORES, owner // CORES % xs, owner // (CORES * xs)
    target = ((core * xs + x) * zs + z) * sb + slot
    row_target = target.reshape(cx, nj).T.reshape(1, blocks)

    dims = (zs, xs, secs, blks, nq, cx, cy, lat, lon)
    f32 = jnp.float32
    rows = cx // GROUPS
    per_x = zs * sb
    messages = 12 + 8 + 8 + xs + (xs - 1) + (zs - 1) + (zs - 1) + zs * (xs - 1) + zs * xs
    any_space = pl.BlockSpec(memory_space=pl.ANY)
    vmem = pl.BlockSpec(memory_space=pltpu.VMEM)
    smem = pl.BlockSpec(memory_space=pltpu.SMEM)

    def body(*refs):
        kernel(dims, *refs)

    return pl.pallas_call(
        body,
        out_shape=(
            jax.ShapeDtypeStruct(state.shape, f32),
            jax.ShapeDtypeStruct(conductance.shape, f32),
            jax.ShapeDtypeStruct((cx, cy), f32),
        ),
        in_specs=[any_space] * 5 + [vmem, smem],
        out_specs=(any_space, vmem, any_space),
        scratch_shapes=[
            pltpu.VMEM((nq + 3, nj + 1, cx + PAD, 128), f32),
            pltpu.VMEM((nj, cx, 128), jnp.int32),
            pltpu.VMEM((nq, nj + 1, cx + PAD, 128), f32),
            pltpu.VMEM((nj + 1, cx + PAD, 128), f32),
            pltpu.VMEM((nj + 1, cx + PAD, 128), f32),
            pltpu.VMEM((2, rows, 128), f32),
            pltpu.VMEM((2, rows, 128), f32),
            pltpu.VMEM((4, 8, 128), f32),
            pltpu.VMEM((2, rows, 128), f32),
            pltpu.VMEM((2, rows, 128), f32),
            pltpu.VMEM((3, lat + 16, lon + 256), f32),
            pltpu.VMEM((blocks, 256), jnp.bfloat16),
            pltpu.VMEM((xs, per_x, 128), f32),
            pltpu.VMEM((xs, per_x, 128), f32),
            pltpu.VMEM((xs, per_x, 128), f32),
            pltpu.VMEM((xs - 1, per_x, 128), f32),
            pltpu.VMEM((per_x, 128), f32),
            pltpu.VMEM((zs - 1, sb, 128), f32),
            pltpu.VMEM((secs * sb, 128), f32),
            pltpu.VMEM((nj, cx, 128), f32),
            pltpu.SemaphoreType.DMA((4 * nj + 2,)),
            pltpu.SemaphoreType.DMA((3 * nj,)),
            pltpu.SemaphoreType.DMA((messages,)),
            pltpu.SemaphoreType.DMA((messages,)),
        ],
        compiler_params=pltpu.CompilerParams(
            collective_id=0, has_side_effects=True, vmem_limit_bytes=56 * 1024 * 1024
        ),
    )(state, velocity, limiter, conductance, potential_prior, row_target, target)


def solution(mesh):
    in_specs = (
        P(None, "sec", "blk"),
        P(None, "sec", "blk"),
        P("sec", "blk"),
        P("sec", "blk", None, None),
        P("sec", "blk", None, None),
        P("sec", "blk"),
        P("sec", "blk"),
    )
    out_specs = (P(None, "sec", "blk"), P("sec", "blk"), P("sec", "blk"))
    return jax.shard_map(
        on_device, mesh=mesh, in_specs=in_specs, out_specs=out_specs, check_vma=False
    )
```

```python
import jax
import jax.numpy as jnp
from jax import lax
from jax.experimental import pallas as pl
from jax.experimental.pallas import tpu as pltpu
from jax.sharding import PartitionSpec as P

ITERS = 4
CORES = 2
TOP = 16
PAD = 40
GROUPS = 8
MESH = pl.DeviceIdType.MESH


def minmod(a, b):
    return jnp.maximum(jnp.minimum(a, b), jnp.minimum(jnp.maximum(a, b), 0.0))


def lane_next(tiles, lane):
    rolled = [pltpu.roll(t, 127, 1) for t in tiles]
    n = len(tiles)
    return [jnp.where(lane == 127, rolled[(j + 1) % n], rolled[j]) for j in range(n)]


def lane_prev(tiles, lane):
    rolled = [pltpu.roll(t, 1, 1) for t in tiles]
    return [jnp.where(lane == 0, rolled[j - 1], rolled[j]) for j in range(len(tiles))]


def kernel(
    dims,
    state,
    velocity,
    limiter,
    sigma,
    prior,
    owner,
    slot,
    out_state,
    out_phi,
    out_foot,
    grid,
    flags,
    fresh,
    left_x,
    right_x,
    face_x,
    face_y,
    face_before,
    block_at,
    look_at,
    look_up_at,
    packs,
    edges,
    corners,
    packs_o,
    edges_o,
    shell,
    weights,
    dense_sib,
    dense_own,
    got_sib,
    got_half,
    got_x,
    z_part,
    got_z,
    table,
    foot,
    look_sem,
    load_sem,
    out_sem,
    send_sem,
    recv_sem,
):
    zs, xs, secs, blks, nq, cx, cy, lat, lon = dims
    nj = cy // 128
    sb = lat * lon // 128
    me = lax.axis_index("sec")
    col = lax.axis_index("blk")
    core = lax.rem(me, CORES)
    at_x = lax.rem(lax.div(me, CORES), xs)
    at_z = lax.div(me, CORES * xs)

    def sec_of(z, x, c):
        return (z * xs + x) * CORES + c

    up, down = lax.rem(me + secs - 1, secs), lax.rem(me + 1, secs)
    left, right = lax.rem(col + blks - 1, blks), lax.rem(col + 1, blks)
    sibling = (me + 1 - 2 * core, col)
    x_peer = {d: (sec_of(at_z, lax.rem(at_x + d, xs), core), col) for d in range(1, xs)}
    z_peer = {d: (sec_of(lax.rem(at_z + d, zs), at_x, core), col) for d in range(1, zs)}
    compass = {
        (-1, 0): (up, col),
        (1, 0): (down, col),
        (0, -1): (me, left),
        (0, 1): (me, right),
        (-1, -1): (up, left),
        (-1, 1): (up, right),
        (1, -1): (down, left),
        (1, 1): (down, right),
    }

    used = [0]
    sent = []

    def send(src, dst, device):
        n = used[0]
        used[0] += 1
        copy = pltpu.make_async_remote_copy(
            src_ref=src,
            dst_ref=dst,
            send_sem=send_sem.at[n],
            recv_sem=recv_sem.at[n],
            device_id=device,
            device_id_type=MESH,
        )
        copy.start()
        sent.append(copy)
        return copy

    loads = {}

    def load(name, src, dst):
        copy = pltpu.make_async_copy(src, dst, load_sem.at[len(loads)])
        copy.start()
        loads[name] = copy

    mid = slice(TOP, TOP + cx)
    for j in range(nj):
        lanes = slice(128 * j, 128 * j + 128)
        load(("f", j), state.at[nq - 2 : nq, :, lanes], grid.at[nq - 2 : nq, j, mid, :])
        load(("v", j), velocity.at[:, :, lanes], grid.at[nq : nq + 2, j, mid, :])
        load(("l", j), limiter.at[:, lanes], flags.at[j])
    load("sigma", sigma, shell.at[0, 8 : 8 + lat, 128 : 128 + lon])
    load("prior", prior, shell.at[1, 8 : 8 + lat, 128 : 128 + lon])
    for j in range(nj):
        lanes = slice(128 * j, 128 * j + 128)
        load(("o", j), state.at[: nq - 2, :, lanes], grid.at[: nq - 2, j, mid, :])

    per_row = lon // 128
    at_owner, at_slot = owner[...], slot[...]
    look_at[...] = at_owner * sb + at_slot
    look_load = pltpu.make_async_copy(look_at, look_up_at, look_sem)
    look_load.start()
    ordered = (
        ((at_owner % CORES) * xs + (at_owner // CORES) % xs) * zs + at_owner // (CORES * xs)
    ) * sb
    ordered = ordered + (at_slot % per_row) * lat + at_slot // per_row
    to_lane = lax.broadcasted_iota(jnp.int32, (128, 128), 1)
    from_lane = lax.broadcasted_iota(jnp.int32, (128, 128), 0)
    each = 128 // nj
    moved = ((from_lane % nj) * each + from_lane // nj == to_lane).astype(jnp.float32)

    def move(a):
        return jnp.dot(a.astype(jnp.float32), moved, preferred_element_type=jnp.float32).astype(jnp.int32)

    block_at[...] = move(ordered // 64) * 64 + move(ordered % 64)

    barrier = pltpu.get_barrier_semaphore()
    partners = [*compass.values(), *x_peer.values(), *z_peer.values(), sibling]
    for device in partners:
        pl.semaphore_signal(barrier, inc=1, device_id=device, device_id_type=MESH)
    pl.semaphore_wait(barrier, len(partners))


    for j in range(nj):
        for name in ("f", "v", "l"):
            loads[(name, j)].wait()
    for j in range(nj):
        grid[nq + 2, j, mid, :] = 0.5 * flags[j].astype(jnp.float32)
    first = nq - 2
    fields = slice(first, first + 5)
    top, bottom = slice(TOP, TOP + 8), slice(TOP + cx - 8, TOP + cx)
    above, below = slice(TOP - 8, TOP), slice(TOP + cx, TOP + cx + 8)
    halo = []
    halo.append(send(grid.at[fields, 0:nj, bottom, :], grid.at[fields, 0:nj, above, :], (down, col)))
    halo.append(send(grid.at[fields, 0:nj, top, :], grid.at[fields, 0:nj, below, :], (up, col)))

    rows = cx // GROUPS
    wide = lax.broadcasted_iota(jnp.int32, (rows, 128), 1)

    def pack(base, count, width):
        at_left = jnp.zeros((rows, 128), jnp.float32)
        at_right = jnp.zeros((rows, 128), jnp.float32)
        for g in range(GROUPS):
            here = slice(TOP + g * rows, TOP + (g + 1) * rows)
            for a in range(count):
                at = 16 * g + width * a
                mask = (wide >= at) & (wide < at + width)
                at_left = jnp.where(mask, pltpu.roll(grid[base + a, 0, here, :], at, 1), at_left)
                moved = pltpu.roll(grid[base + a, nj - 1, here, :], (at + width) % 128, 1)
                at_right = jnp.where(mask, moved, at_right)
        return at_left, at_right

    def unpack(base, count, width, from_left, from_right, take, put, size, group):
        side = lax.broadcasted_iota(jnp.int32, (size, 128), 1) < 64
        for a in range(count):
            at = 16 * group + width * a
            r = pltpu.roll(from_right[take, :], (128 - at) % 128, 1)
            l = pltpu.roll(from_left[take, :], (256 - width - at) % 128, 1)
            grid[base + a, nj, put, :] = jnp.where(side, r, l)

    to_left, to_right = pack(first, 5, 3)
    packs[0] = to_left
    packs[1] = to_right
    halo.append(send(packs.at[1], edges.at[0], (me, right)))
    halo.append(send(packs.at[0], edges.at[1], (me, left)))
    halo.append(send(packs.at[1, rows - 8 : rows, :], corners.at[0], (down, right)))
    halo.append(send(packs.at[0, rows - 8 : rows, :], corners.at[1], (down, left)))
    halo.append(send(packs.at[1, 0:8, :], corners.at[2], (up, right)))
    halo.append(send(packs.at[0, 0:8, :], corners.at[3], (up, left)))

    row_src = {0: slice(8, 8 + lat), 1: slice(lat, lat + 8), -1: slice(8, 16)}
    row_dst = {0: slice(8, 8 + lat), 1: slice(0, 8), -1: slice(8 + lat, 16 + lat)}
    lane_src = {0: slice(128, 128 + lon), 1: slice(lon, lon + 128), -1: slice(128, 256)}
    lane_dst = {0: slice(128, 128 + lon), 1: slice(0, 128), -1: slice(128 + lon, 256 + lon)}

    def shell_halo(which):
        return [
            send(
                shell.at[which, row_src[dr], lane_src[dc]],
                shell.at[which, row_dst[dr], lane_dst[dc]],
                device,
            )
            for (dr, dc), device in compass.items()
        ]

    loads["sigma"].wait()
    loads["prior"].wait()
    shell_copies = shell_halo(slice(0, 2))

    for j in range(nj):
        loads[("o", j)].wait()
    others = slice(0, nq - 2)
    halo_o = [
        send(grid.at[others, 0:nj, bottom, :], grid.at[others, 0:nj, above, :], (down, col)),
        send(grid.at[others, 0:nj, top, :], grid.at[others, 0:nj, below, :], (up, col)),
    ]
    to_left, to_right = pack(0, nq - 2, 2)
    packs_o[0] = to_left
    packs_o[1] = to_right
    halo_o.append(send(packs_o.at[1], edges_o.at[0], (me, right)))
    halo_o.append(send(packs_o.at[0], edges_o.at[1], (me, left)))

    for copy in halo:
        copy.wait_recv()
    for g in range(GROUPS):
        here = slice(TOP + g * rows, TOP + (g + 1) * rows)
        unpack(first, 5, 3, edges.at[0], edges.at[1], slice(0, rows), here, rows, g)
    unpack(first, 5, 3, corners.at[0], corners.at[1], slice(0, 8), above, 8, GROUPS - 1)
    unpack(first, 5, 3, corners.at[2], corners.at[3], slice(0, 8), below, 8, 0)

    deep = 16
    lane_d = lax.broadcasted_iota(jnp.int32, (deep, 128), 1)

    def faces(k, carry):
        b = pl.multiple_of(TOP - 8 + deep * k, 8)
        speed_y = [grid[nq + 1, j, pl.ds(b, deep), :] for j in range(nj + 1)]
        faces_y = [0.2 * (here + after) for here, after in zip(speed_y, lane_next(speed_y, lane_d))]
        faces_before = lane_prev(faces_y, lane_d)
        for j in range(nj + 1):
            face_y[j, pl.ds(b, deep), :] = faces_y[j]
            face_before[j, pl.ds(b, deep), :] = faces_before[j]
            face_x[j, pl.ds(b, deep), :] = 0.2 * (
                grid[nq, j, pl.ds(b, deep), :] + grid[nq, j, pl.ds(b + 1, deep), :]
            )
        return carry

    lax.fori_loop(0, (cx + 16) // deep, faces, 0)

    def advect(first_q, tiles_x, start, high, steps):
        lane_h = lax.broadcasted_iota(jnp.int32, (high, 128), 1)

        def along_x(k, carry):
            b = pl.multiple_of(TOP - 8 + deep * k, 8)
            for n in range(2):
                for j in range(tiles_x):
                    here = grid[first_q + n, j, pl.ds(b, deep), :]
                    lower = here - grid[first_q + n, j, pl.ds(b - 1, deep), :]
                    upper = grid[first_q + n, j, pl.ds(b + 1, deep), :] - here
                    half = minmod(lower, upper) * grid[nq + 2, j, pl.ds(b, deep), :]
                    left_x[n, j, pl.ds(b, deep), :] = here + half
                    right_x[n, j, pl.ds(b, deep), :] = here - half
            return carry

        def step(k, carry):
            b = pl.multiple_of(start + high * k, 8)
            for n in range(2):
                here = [grid[first_q + n, j, pl.ds(b, high), :] for j in range(nj + 1)]
                nexts, befores = lane_next(here, lane_h), lane_prev(here, lane_h)
                half = [
                    minmod(h - before, after - h) * grid[nq + 2, j, pl.ds(b, high), :]
                    for j, (h, before, after) in enumerate(zip(here, befores, nexts))
                ]
                left_y = [h + m for h, m in zip(here, half)]
                right_y = [h - m for h, m in zip(here, half)]
                right_next, left_before = lane_next(right_y, lane_h), lane_prev(left_y, lane_h)
                for j in range(tiles_x):
                    speed = face_y[j, pl.ds(b, high), :]
                    flux_y = speed * jnp.where(speed > 0.0, left_y[j], right_next[j])
                    speed = face_before[j, pl.ds(b, high), :]
                    flux_before = speed * jnp.where(speed > 0.0, left_before[j], right_y[j])
                    speed = face_x[j, pl.ds(b, high), :]
                    flux_x = speed * jnp.where(
                        speed > 0.0,
                        left_x[n, j, pl.ds(b, high), :],
                        right_x[n, j, pl.ds(b + 1, high), :],
                    )
                    speed = face_x[j, pl.ds(b - 1, high), :]
                    flux_above = speed * jnp.where(
                        speed > 0.0,
                        left_x[n, j, pl.ds(b - 1, high), :],
                        right_x[n, j, pl.ds(b, high), :],
                    )
                    fresh[first_q + n, j, pl.ds(b, high), :] = here[j] - (
                        (flux_x - flux_above) + (flux_y - flux_before)
                    )
            return carry

        lax.fori_loop(0, (cx + 16) // deep, along_x, 0)
        lax.fori_loop(0, steps, step, 0)

    advect(nq - 2, nj + 1, TOP - 8, deep, (cx + 16) // deep)
    writes = []

    def write(src, dst):
        copy = pltpu.make_async_copy(src, dst, out_sem.at[len(writes)])
        copy.start()
        writes.append(copy)

    for j in range(nj):
        lanes = slice(128 * j, 128 * j + 128)
        write(fresh.at[nq - 2 : nq, j, mid, :], out_state.at[nq - 2 : nq, :, lanes])

    chunk = each
    lane_c = lax.broadcasted_iota(jnp.int32, (chunk, 128), 1)

    def curl(k, carry):
        b = pl.multiple_of(TOP + chunk * k, 8)
        field_x = [fresh[nq - 2, j, pl.ds(b, chunk), :] for j in range(nj + 1)]
        after = lane_next(field_x, lane_c)
        before = lane_prev(field_x, lane_c)
        for j in range(nj):
            current = 0.5 * (
                fresh[nq - 1, j, pl.ds(b + 1, chunk), :] - fresh[nq - 1, j, pl.ds(b - 1, chunk), :]
            ) - 0.5 * (after[j] - before[j])
            high = current.astype(jnp.bfloat16)
            low = (current - high.astype(jnp.float32)).astype(jnp.bfloat16)
            r = pl.multiple_of((k * nj + j) * chunk, chunk)
            weights[pl.ds(r, chunk), 0:128] = high
            weights[pl.ds(r, chunk), 128:256] = low
        return carry

    lax.fori_loop(0, cx // chunk, curl, 0)

    per_x = zs * sb
    half = per_x // 2
    groups = nj * cx // 128

    def sums(base, store):
        ids = lax.broadcasted_iota(jnp.int32, (per_x, 128), 0) + base
        chosen = [
            jnp.where(ids == block_at[k : k + 1, :], 1.0, 0.0).astype(jnp.bfloat16)
            for k in range(groups)
        ]
        both = jnp.dot(
            jnp.concatenate(chosen, axis=1), weights[...], preferred_element_type=jnp.float32
        )
        store[...] = both[:, :128] + both[:, 128:]

    sib_copies = {}

    def for_sibling(d):
        sums(((1 - core) * xs + lax.rem(at_x + d, xs)) * per_x, dense_sib.at[d])
        sib_copies[d] = send(dense_sib.at[d], got_sib.at[d], sibling)

    def for_own(d):
        sums((core * xs + lax.rem(at_x + d, xs)) * per_x, dense_own.at[d])
        sib_copies[d].wait_recv()
        dense_own[d] = dense_own[d] + got_sib[d]

    def to_x(d, n, part):
        return send(dense_own.at[d, part, :], got_x.at[n, part, :], x_peer[d])

    first_part, last_part = slice(0, half), slice(half, per_x)
    if xs == 4:
        for_sibling(2)
        for_sibling(1)
        for_own(2)
        across_up = send(dense_own.at[2, first_part, :], got_half.at[0], x_peer[1])
        across_down = send(dense_own.at[2, last_part, :], got_half.at[1], x_peer[3])
        for_sibling(3)
        for_own(1)
        last_in = to_x(1, 0, last_part)
        for_sibling(0)
        for_own(3)
        first_in = to_x(3, 1, first_part)
        across_up.wait_recv()
        dense_own[1, first_part, :] = dense_own[1, first_part, :] + got_half[0]
        x_first = [first_in, to_x(1, 0, first_part)]
        across_down.wait_recv()
        dense_own[3, last_part, :] = dense_own[3, last_part, :] + got_half[1]
        x_last = [last_in, to_x(3, 1, last_part)]
        for_own(0)
        terms = 2
    else:
        for_sibling(1)
        for_own(1)
        x_first = [to_x(1, 0, first_part)]
        x_last = [to_x(1, 0, last_part)]
        for_sibling(0)
        for_own(0)
        terms = 1
    for copy in halo_o:
        copy.wait_recv()
    for g in range(GROUPS):
        here = slice(TOP + g * rows, TOP + (g + 1) * rows)
        unpack(0, nq - 2, 2, edges_o.at[0], edges_o.at[1], slice(0, rows), here, rows, g)

    def other(n, carry):
        advect(2 * n, nj, TOP, 32, cx // 32)
        return carry

    pairs = (nq - 2) // 2
    lax.fori_loop(0, pairs - 1, other, 0)
    for copy in x_first + x_last:
        copy.wait_recv()
    total = dense_own[0]
    for n in range(terms):
        total = total + got_x[n]
    z_part[...] = total
    z_copies = []
    for d in range(1, zs):
        at = pl.multiple_of(lax.rem(at_z + d, zs) * sb, sb)
        z_copies.append(send(z_part.at[pl.ds(at, sb), :], got_z.at[d - 1], z_peer[d]))
    lax.fori_loop(pairs - 1, pairs, other, 0)
    for j in range(nj):
        lanes = slice(128 * j, 128 * j + 128)
        write(fresh.at[0 : nq - 2, j, mid, :], out_state.at[0 : nq - 2, :, lanes])
    source = z_part[pl.ds(pl.multiple_of(at_z * sb, sb), sb), :]
    for d in range(1, zs):
        z_copies[d - 1].wait_recv()
        source = source + got_z[d - 1]
    for c in range(lon // 128):
        at = 128 + 128 * c
        shell[2, 8 : 8 + lat, at : at + 128] = source[c * lat : (c + 1) * lat, :]
    source_copies = shell_halo(slice(2, 3))

    for copy in shell_copies:
        copy.wait_recv()
    shape = (lat + 16, lon + 256)
    lat_at = lax.broadcasted_iota(jnp.int32, shape, 0) + (me * lat - 8)
    lon_at = lax.broadcasted_iota(jnp.int32, shape, 1) + (col * lon - 128)
    inside = (lat_at >= 0) & (lat_at < secs * lat) & (lon_at >= 0) & (lon_at < blks * lon)
    sig = jnp.where(inside, shell[0], 0.0)
    phi = jnp.where(inside, shell[1], 0.0)

    def around(a):
        return (
            pltpu.roll(a, 1, 0),
            pltpu.roll(a, lat + 15, 0),
            pltpu.roll(a, 1, 1),
            pltpu.roll(a, lon + 255, 1),
        )

    ways = [0.5 * (sig + other_sig) for other_sig in around(sig)]
    inverse = 1.0 / (ways[0] + ways[1] + ways[2] + ways[3] + 1.0)
    for copy in source_copies:
        copy.wait_recv()
    src = shell[2]
    for _ in range(ITERS):
        n, s, w, e = around(phi)
        total = ways[0] * n + ways[1] * s + ways[2] * w + ways[3] * e + src
        phi = jnp.where(inside, total * inverse, 0.0)
    phi = phi[8 : 8 + lat, 128 : 128 + lon]
    out_phi[...] = phi

    def piece(z, x, c):
        return table.at[pl.ds(pl.multiple_of(sec_of(z, x, c) * sb, sb), sb), :]

    mine = pl.multiple_of(me * sb, sb)
    for c in range(per_row):
        table[pl.ds(mine + c, lat, stride=per_row), :] = phi[:, c * 128 : (c + 1) * 128]

    from_z, from_x, from_sib = {}, {}, []
    own = piece(at_z, at_x, core)
    nearest = sorted(range(1, zs), key=lambda d: min(d, zs - d))
    for d in nearest:
        from_z[d] = send(own, own, z_peer[d])
    steps = [0] + nearest
    beside = sorted({1, xs - 1})

    def along_x(i):
        dz = steps[i]
        if dz:
            from_z[dz].wait_recv()
        part = piece(lax.rem(at_z + zs - dz, zs), at_x, core)
        for dx in beside:
            from_x[i, dx] = send(part, part, x_peer[dx])
        from_sib.append(send(part, part, sibling))

    def arrived(i, dx):
        from_x[i, dx].wait_recv()
        z = lax.rem(at_z + zs - steps[i], zs)
        part = piece(z, lax.rem(at_x + xs - dx, xs), core)
        if xs == 4 and dx == (1, 3)[i % 2]:
            from_x[i, 2] = send(part, part, x_peer[dx])
        from_sib.append(send(part, part, sibling))

    for i in range(zs + 2):
        if i < zs:
            along_x(i)
        if i >= 2:
            for dx in beside:
                arrived(i - 2, dx)
    if xs == 4:
        for i in range(zs):
            arrived(i, 2)
    for copy in from_sib:
        copy.wait_recv()
    look_load.wait()

    def look_up(k, carry):
        b = pl.multiple_of(8 * k, 8)
        for r in range(8):
            for j in range(nj):
                at = look_up_at[lax.div(b, 128 // nj), lax.rem(b, 128 // nj) * nj + r * nj + j]
                foot[j, pl.ds(b + r, 1), :] = table[pl.ds(at, 1), :]
        return carry

    lax.fori_loop(0, cx // 8, look_up, 0)
    for j in range(nj):
        write(foot.at[j], out_foot.at[:, 128 * j : 128 * j + 128])
    for copy in sent:
        copy.wait_send()
    for copy in writes:
        copy.wait()


def on_device(
    state, velocity, limiter, footpoint_owner, footpoint_slot, conductance, potential_prior
):
    secs, blks = lax.axis_size("sec"), lax.axis_size("blk")
    xs = 4 if secs % 16 == 0 else 2
    zs = secs // (CORES * xs)
    nq, cx, cy = state.shape
    lat, lon = conductance.shape
    nj = cy // 128
    sb = lat * lon // 128
    blocks = nj * cx
    owner = footpoint_owner.reshape(blocks // 128, 128)
    slot = footpoint_slot.reshape(blocks // 128, 128)
    dims = (zs, xs, secs, blks, nq, cx, cy, lat, lon)
    f32 = jnp.float32
    rows = cx // GROUPS
    per_x = zs * sb
    messages = 12 + 8 + 8 + xs + 6 + 2 * (zs - 1) + zs * (xs - 1) + zs * xs
    any_space = pl.BlockSpec(memory_space=pl.ANY)
    vmem = pl.BlockSpec(memory_space=pltpu.VMEM)

    def body(*refs):
        kernel(dims, *refs)

    return pl.pallas_call(
        body,
        out_shape=(
            jax.ShapeDtypeStruct(state.shape, f32),
            jax.ShapeDtypeStruct(conductance.shape, f32),
            jax.ShapeDtypeStruct((cx, cy), f32),
        ),
        in_specs=[any_space] * 5 + [vmem, vmem],
        out_specs=(any_space, vmem, any_space),
        scratch_shapes=[
            pltpu.VMEM((nq + 3, nj + 1, cx + PAD, 128), f32),
            pltpu.VMEM((nj, cx, 128), jnp.int32),
            pltpu.VMEM((nq, nj + 1, cx + PAD, 128), f32),
            pltpu.VMEM((2, nj + 1, cx + PAD, 128), f32),
            pltpu.VMEM((2, nj + 1, cx + PAD, 128), f32),
            pltpu.VMEM((nj + 1, cx + PAD, 128), f32),
            pltpu.VMEM((nj + 1, cx + PAD, 128), f32),
            pltpu.VMEM((nj + 1, cx + PAD, 128), f32),
            pltpu.VMEM((blocks // 128, 128), jnp.int32),
            pltpu.VMEM((blocks // 128, 128), jnp.int32),
            pltpu.SMEM((blocks // 128, 128), jnp.int32),
            pltpu.VMEM((2, rows, 128), f32),
            pltpu.VMEM((2, rows, 128), f32),
            pltpu.VMEM((4, 8, 128), f32),
            pltpu.VMEM((2, rows, 128), f32),
            pltpu.VMEM((2, rows, 128), f32),
            pltpu.VMEM((3, lat + 16, lon + 256), f32),
            pltpu.VMEM((blocks, 256), jnp.bfloat16),
            pltpu.VMEM((xs, per_x, 128), f32),
            pltpu.VMEM((xs, per_x, 128), f32),
            pltpu.VMEM((xs, per_x, 128), f32),
            pltpu.VMEM((2, per_x // 2, 128), f32),
            pltpu.VMEM((2, per_x, 128), f32),
            pltpu.VMEM((per_x, 128), f32),
            pltpu.VMEM((zs - 1, sb, 128), f32),
            pltpu.VMEM((secs * sb, 128), f32),
            pltpu.VMEM((nj, cx, 128), f32),
            pltpu.SemaphoreType.DMA(()),
            pltpu.SemaphoreType.DMA((4 * nj + 2,)),
            pltpu.SemaphoreType.DMA((3 * nj,)),
            pltpu.SemaphoreType.DMA((messages,)),
            pltpu.SemaphoreType.DMA((messages,)),
        ],
        compiler_params=pltpu.CompilerParams(
            collective_id=0, has_side_effects=True, vmem_limit_bytes=56 * 1024 * 1024
        ),
    )(state, velocity, limiter, conductance, potential_prior, owner, slot)


def solution(mesh):
    in_specs = (
        P(None, "sec", "blk"),
        P(None, "sec", "blk"),
        P("sec", "blk"),
        P("sec", "blk", None, None),
        P("sec", "blk", None, None),
        P("sec", "blk"),
        P("sec", "blk"),
    )
    out_specs = (P(None, "sec", "blk"), P("sec", "blk"), P("sec", "blk"))
    return jax.shard_map(
        on_device, mesh=mesh, in_specs=in_specs, out_specs=out_specs, check_vma=False
    )
```

```python
import jax
import jax.numpy as jnp
from jax import lax
from jax.experimental import pallas as pl
from jax.experimental.pallas import tpu as pltpu
from jax.sharding import PartitionSpec as P

ITERS = 4
CORES = 2
TOP = 16
PAD = 40
GROUPS = 8
MESH = pl.DeviceIdType.MESH


def minmod(a, b):
    return jnp.maximum(jnp.minimum(a, b), jnp.minimum(jnp.maximum(a, b), 0.0))


def lane_next(tiles, lane):
    rolled = [pltpu.roll(t, 127, 1) for t in tiles]
    n = len(tiles)
    return [jnp.where(lane == 127, rolled[(j + 1) % n], rolled[j]) for j in range(n)]


def lane_prev(tiles, lane):
    rolled = [pltpu.roll(t, 1, 1) for t in tiles]
    return [jnp.where(lane == 0, rolled[j - 1], rolled[j]) for j in range(len(tiles))]


def kernel(
    dims,
    state,
    velocity,
    limiter,
    sigma,
    prior,
    owner,
    slot,
    out_state,
    out_phi,
    out_foot,
    grid,
    flags,
    fresh,
    left_x,
    right_x,
    face_x,
    face_y,
    face_before,
    block_at,
    look_at,
    look_up_at,
    packs,
    edges,
    corners,
    packs_o,
    edges_o,
    shell,
    weights,
    dense_sib,
    dense_own,
    got_sib,
    got_x,
    z_part,
    got_z,
    table,
    foot,
    look_sem,
    load_sem,
    out_sem,
    send_sem,
    recv_sem,
):
    zs, xs, secs, blks, nq, cx, cy, lat, lon = dims
    nj = cy // 128
    sb = lat * lon // 128
    me = lax.axis_index("sec")
    col = lax.axis_index("blk")
    core = lax.rem(me, CORES)
    at_x = lax.rem(lax.div(me, CORES), xs)
    at_z = lax.div(me, CORES * xs)

    def sec_of(z, x, c):
        return (z * xs + x) * CORES + c

    up, down = lax.rem(me + secs - 1, secs), lax.rem(me + 1, secs)
    left, right = lax.rem(col + blks - 1, blks), lax.rem(col + 1, blks)
    sibling = (me + 1 - 2 * core, col)
    x_peer = {d: (sec_of(at_z, lax.rem(at_x + d, xs), core), col) for d in range(1, xs)}
    z_peer = {d: (sec_of(lax.rem(at_z + d, zs), at_x, core), col) for d in range(1, zs)}
    compass = {
        (-1, 0): (up, col),
        (1, 0): (down, col),
        (0, -1): (me, left),
        (0, 1): (me, right),
        (-1, -1): (up, left),
        (-1, 1): (up, right),
        (1, -1): (down, left),
        (1, 1): (down, right),
    }

    used = [0]
    sent = []

    def send(src, dst, device):
        n = used[0]
        used[0] += 1
        copy = pltpu.make_async_remote_copy(
            src_ref=src,
            dst_ref=dst,
            send_sem=send_sem.at[n],
            recv_sem=recv_sem.at[n],
            device_id=device,
            device_id_type=MESH,
        )
        copy.start()
        sent.append(copy)
        return copy

    loads = {}

    def load(name, src, dst):
        copy = pltpu.make_async_copy(src, dst, load_sem.at[len(loads)])
        copy.start()
        loads[name] = copy

    mid = slice(TOP, TOP + cx)
    for j in range(nj):
        lanes = slice(128 * j, 128 * j + 128)
        load(("f", j), state.at[nq - 2 : nq, :, lanes], grid.at[nq - 2 : nq, j, mid, :])
        load(("v", j), velocity.at[:, :, lanes], grid.at[nq : nq + 2, j, mid, :])
        load(("l", j), limiter.at[:, lanes], flags.at[j])
    load("sigma", sigma, shell.at[0, 8 : 8 + lat, 128 : 128 + lon])
    load("prior", prior, shell.at[1, 8 : 8 + lat, 128 : 128 + lon])
    for j in range(nj):
        lanes = slice(128 * j, 128 * j + 128)
        load(("o", j), state.at[: nq - 2, :, lanes], grid.at[: nq - 2, j, mid, :])

    per_row = lon // 128
    at_owner, at_slot = owner[...], slot[...]
    look_at[...] = at_owner * sb + at_slot
    look_load = pltpu.make_async_copy(look_at, look_up_at, look_sem)
    look_load.start()
    ordered = (
        ((at_owner % CORES) * zs + at_owner // (CORES * xs)) * xs + (at_owner // CORES) % xs
    ) * sb
    ordered = ordered + (at_slot % per_row) * lat + at_slot // per_row
    to_lane = lax.broadcasted_iota(jnp.int32, (128, 128), 1)
    from_lane = lax.broadcasted_iota(jnp.int32, (128, 128), 0)
    each = 128 // nj
    moved = ((from_lane % nj) * each + from_lane // nj == to_lane).astype(jnp.float32)

    def move(a):
        return jnp.dot(a.astype(jnp.float32), moved, preferred_element_type=jnp.float32).astype(jnp.int32)

    block_at[...] = move(ordered // 64) * 64 + move(ordered % 64)

    barrier = pltpu.get_barrier_semaphore()
    partners = [*compass.values(), *x_peer.values(), *z_peer.values(), sibling]
    for device in partners:
        pl.semaphore_signal(barrier, inc=1, device_id=device, device_id_type=MESH)

    for j in range(nj):
        for name in ("f", "v", "l"):
            loads[(name, j)].wait()
    for j in range(nj):
        grid[nq + 2, j, mid, :] = 0.5 * flags[j].astype(jnp.float32)
    first = nq - 2
    fields = slice(first, first + 5)
    top, bottom = slice(TOP, TOP + 8), slice(TOP + cx - 8, TOP + cx)
    above, below = slice(TOP - 8, TOP), slice(TOP + cx, TOP + cx + 8)
    rows = cx // GROUPS
    wide = lax.broadcasted_iota(jnp.int32, (rows, 128), 1)

    def pack(base, count, width):
        at_left = jnp.zeros((rows, 128), jnp.float32)
        at_right = jnp.zeros((rows, 128), jnp.float32)
        for g in range(GROUPS):
            here = slice(TOP + g * rows, TOP + (g + 1) * rows)
            for a in range(count):
                at = 16 * g + width * a
                mask = (wide >= at) & (wide < at + width)
                at_left = jnp.where(mask, pltpu.roll(grid[base + a, 0, here, :], at, 1), at_left)
                moved = pltpu.roll(grid[base + a, nj - 1, here, :], (at + width) % 128, 1)
                at_right = jnp.where(mask, moved, at_right)
        return at_left, at_right

    def unpack(base, count, width, from_left, from_right, take, put, size, group):
        side = lax.broadcasted_iota(jnp.int32, (size, 128), 1) < 64
        for a in range(count):
            at = 16 * group + width * a
            r = pltpu.roll(from_right[take, :], (128 - at) % 128, 1)
            l = pltpu.roll(from_left[take, :], (256 - width - at) % 128, 1)
            grid[base + a, nj, put, :] = jnp.where(side, r, l)

    to_left, to_right = pack(first, 5, 3)
    packs[0] = to_left
    packs[1] = to_right
    pl.semaphore_wait(barrier, len(partners))
    halo = []
    halo.append(send(grid.at[fields, 0:nj, bottom, :], grid.at[fields, 0:nj, above, :], (down, col)))
    halo.append(send(grid.at[fields, 0:nj, top, :], grid.at[fields, 0:nj, below, :], (up, col)))
    halo.append(send(packs.at[1], edges.at[0], (me, right)))
    halo.append(send(packs.at[0], edges.at[1], (me, left)))
    halo.append(send(packs.at[1, rows - 8 : rows, :], corners.at[0], (down, right)))
    halo.append(send(packs.at[0, rows - 8 : rows, :], corners.at[1], (down, left)))
    halo.append(send(packs.at[1, 0:8, :], corners.at[2], (up, right)))
    halo.append(send(packs.at[0, 0:8, :], corners.at[3], (up, left)))

    row_src = {0: slice(8, 8 + lat), 1: slice(lat, lat + 8), -1: slice(8, 16)}
    row_dst = {0: slice(8, 8 + lat), 1: slice(0, 8), -1: slice(8 + lat, 16 + lat)}
    lane_src = {0: slice(128, 128 + lon), 1: slice(lon, lon + 128), -1: slice(128, 256)}
    lane_dst = {0: slice(128, 128 + lon), 1: slice(0, 128), -1: slice(128 + lon, 256 + lon)}

    def shell_halo(which):
        return [
            send(
                shell.at[which, row_src[dr], lane_src[dc]],
                shell.at[which, row_dst[dr], lane_dst[dc]],
                device,
            )
            for (dr, dc), device in compass.items()
        ]

    loads["sigma"].wait()
    loads["prior"].wait()
    shell_copies = shell_halo(slice(0, 2))

    for j in range(nj):
        loads[("o", j)].wait()
    others = slice(0, nq - 2)
    halo_o = [
        send(grid.at[others, 0:nj, bottom, :], grid.at[others, 0:nj, above, :], (down, col)),
        send(grid.at[others, 0:nj, top, :], grid.at[others, 0:nj, below, :], (up, col)),
    ]
    to_left, to_right = pack(0, nq - 2, 2)
    packs_o[0] = to_left
    packs_o[1] = to_right
    halo_o.append(send(packs_o.at[1], edges_o.at[0], (me, right)))
    halo_o.append(send(packs_o.at[0], edges_o.at[1], (me, left)))

    for copy in halo:
        copy.wait_recv()
    for g in range(GROUPS):
        here = slice(TOP + g * rows, TOP + (g + 1) * rows)
        unpack(first, 5, 3, edges.at[0], edges.at[1], slice(0, rows), here, rows, g)
    unpack(first, 5, 3, corners.at[0], corners.at[1], slice(0, 8), above, 8, GROUPS - 1)
    unpack(first, 5, 3, corners.at[2], corners.at[3], slice(0, 8), below, 8, 0)

    around_rows = cx + 16
    ring = slice(TOP - 8, TOP + cx + 8)
    lane_r = lax.broadcasted_iota(jnp.int32, (around_rows, 128), 1)
    speed_y = [grid[nq + 1, j, ring, :] for j in range(nj + 1)]
    faces_y = [0.2 * (here + after) for here, after in zip(speed_y, lane_next(speed_y, lane_r))]
    faces_before = lane_prev(faces_y, lane_r)
    for j in range(nj + 1):
        face_y[j, ring, :] = faces_y[j]
        face_before[j, ring, :] = faces_before[j]
        face_x[j, ring, :] = 0.2 * (grid[nq, j, ring, :] + grid[nq, j, TOP - 7 : TOP + cx + 9, :])

    def advect(q, tiles_x, start, high):
        lane_h = lax.broadcasted_iota(jnp.int32, (high, 128), 1)
        deep = 16

        def along_x(k, carry):
            b = pl.multiple_of(TOP - 8 + deep * k, 8)
            for j in range(tiles_x):
                here = grid[q, j, pl.ds(b, deep), :]
                lower = here - grid[q, j, pl.ds(b - 1, deep), :]
                upper = grid[q, j, pl.ds(b + 1, deep), :] - here
                half = minmod(lower, upper) * grid[nq + 2, j, pl.ds(b, deep), :]
                left_x[j, pl.ds(b, deep), :] = here + half
                right_x[j, pl.ds(b, deep), :] = here - half
            return carry

        lax.fori_loop(0, (cx + 16) // deep, along_x, 0)
        at, above, below = (slice(start + n, start + n + high) for n in (0, -1, 1))
        here = [grid[q, j, at, :] for j in range(nj + 1)]
        nexts, befores = lane_next(here, lane_h), lane_prev(here, lane_h)
        half = [
            minmod(h - before, after - h) * grid[nq + 2, j, at, :]
            for j, (h, before, after) in enumerate(zip(here, befores, nexts))
        ]
        left_y = [h + m for h, m in zip(here, half)]
        right_y = [h - m for h, m in zip(here, half)]
        right_next, left_before = lane_next(right_y, lane_h), lane_prev(left_y, lane_h)
        for j in range(tiles_x):
            speed = face_y[j, at, :]
            flux_y = speed * jnp.where(speed > 0.0, left_y[j], right_next[j])
            speed = face_before[j, at, :]
            flux_before = speed * jnp.where(speed > 0.0, left_before[j], right_y[j])
            speed = face_x[j, at, :]
            flux_x = speed * jnp.where(speed > 0.0, left_x[j, at, :], right_x[j, below, :])
            speed = face_x[j, above, :]
            flux_above = speed * jnp.where(speed > 0.0, left_x[j, above, :], right_x[j, at, :])
            fresh[q, j, at, :] = here[j] - ((flux_x - flux_above) + (flux_y - flux_before))

    def field(q, carry):
        advect(q, nj + 1, TOP - 8, cx + 16)
        return carry

    lax.fori_loop(nq - 2, nq, field, 0)
    writes = []

    def write(src, dst):
        copy = pltpu.make_async_copy(src, dst, out_sem.at[len(writes)])
        copy.start()
        writes.append(copy)

    for j in range(nj):
        lanes = slice(128 * j, 128 * j + 128)
        write(fresh.at[nq - 2 : nq, j, mid, :], out_state.at[nq - 2 : nq, :, lanes])

    lane_c = lax.broadcasted_iota(jnp.int32, (cx, 128), 1)
    field_x = [fresh[nq - 2, j, mid, :] for j in range(nj + 1)]
    after, before = lane_next(field_x, lane_c), lane_prev(field_x, lane_c)
    for j in range(nj):
        current = 0.5 * (
            fresh[nq - 1, j, TOP + 1 : TOP + cx + 1, :] - fresh[nq - 1, j, TOP - 1 : TOP + cx - 1, :]
        ) - 0.5 * (after[j] - before[j])
        high = current.astype(jnp.bfloat16)
        low = (current - high.astype(jnp.float32)).astype(jnp.bfloat16)
        for k in range(cx // each):
            part = slice((k * nj + j) * each, (k * nj + j + 1) * each)
            weights[part, 0:128] = high[k * each : (k + 1) * each, :]
            weights[part, 128:256] = low[k * each : (k + 1) * each, :]

    order = sorted(range(zs), key=lambda d: -min(d, zs - d))
    duos = [order[n : n + 2] for n in range(0, zs, 2)]
    per_z = xs * sb
    groups = nj * cx // 128

    def sums(duo, to_core):
        ids = jnp.concatenate(
            [
                lax.broadcasted_iota(jnp.int32, (per_z, 128), 0)
                + (to_core * zs + lax.rem(at_z + d, zs)) * per_z
                for d in duo
            ],
            axis=0,
        )
        chosen = [
            jnp.where(ids == block_at[k : k + 1, :], 1.0, 0.0).astype(jnp.bfloat16)
            for k in range(groups)
        ]
        both = jnp.dot(
            jnp.concatenate(chosen, axis=1), weights[...], preferred_element_type=jnp.float32
        )
        return (both[:, :128] + both[:, 128:]).reshape(2, xs, sb, 128)

    sib_copies, x_copies, z_copies = {}, {}, {}

    def for_sibling(n):
        dense_sib[n] = sums(duos[n], 1 - core)
        sib_copies[n] = send(dense_sib.at[n], got_sib.at[n], sibling)

    def for_own(n):
        dense_own[n] = sums(duos[n], core)
        sib_copies[n].wait_recv()
        dense_own[n] = dense_own[n] + got_sib[n]
        for d in sorted(x_peer, key=lambda d: -min(d, xs - d)):
            part = dense_own.at[n, :, lax.rem(at_x + d, xs)]
            x_copies[n, d] = send(part, got_x.at[n, d - 1], x_peer[d])

    for_sibling(0)
    for n in range(len(duos)):
        if n + 1 < len(duos):
            for_sibling(n + 1)
        for_own(n)
    for copy in halo_o:
        copy.wait_recv()
    for g in range(GROUPS):
        here = slice(TOP + g * rows, TOP + (g + 1) * rows)
        unpack(0, nq - 2, 2, edges_o.at[0], edges_o.at[1], slice(0, rows), here, rows, g)

    def other(q, carry):
        advect(q, nj, TOP, cx)
        return carry

    def along_z(n):
        for d in x_peer:
            x_copies[n, d].wait_recv()
        for h, d in enumerate(duos[n]):
            part = dense_own[n, h, at_x]
            for e in x_peer:
                part = part + got_x[n, e - 1, h]
            z_part[n, h] = part
            if d:
                z_copies[d] = send(z_part.at[n, h], got_z.at[d - 1], z_peer[d])

    done = (nq - 2) // 2
    lax.fori_loop(0, done, other, 0)
    for n in range(len(duos)):
        if n == len(duos) - 1:
            lax.fori_loop(done, nq - 2, other, 0)
        along_z(n)
    for j in range(nj):
        lanes = slice(128 * j, 128 * j + 128)
        write(fresh.at[0 : nq - 2, j, mid, :], out_state.at[0 : nq - 2, :, lanes])
    source = z_part[len(duos) - 1, 1]
    for d in order[:-1]:
        z_copies[d].wait_recv()
        source = source + got_z[d - 1]
    for c in range(lon // 128):
        at = 128 + 128 * c
        shell[2, 8 : 8 + lat, at : at + 128] = source[c * lat : (c + 1) * lat, :]
    source_copies = shell_halo(slice(2, 3))

    for copy in shell_copies:
        copy.wait_recv()
    shape = (lat + 16, lon + 256)
    lat_at = lax.broadcasted_iota(jnp.int32, shape, 0) + (me * lat - 8)
    lon_at = lax.broadcasted_iota(jnp.int32, shape, 1) + (col * lon - 128)
    inside = (lat_at >= 0) & (lat_at < secs * lat) & (lon_at >= 0) & (lon_at < blks * lon)
    sig = jnp.where(inside, shell[0], 0.0)
    phi = jnp.where(inside, shell[1], 0.0)

    def around(a):
        return (
            pltpu.roll(a, 1, 0),
            pltpu.roll(a, lat + 15, 0),
            pltpu.roll(a, 1, 1),
            pltpu.roll(a, lon + 255, 1),
        )

    ways = [0.5 * (sig + other_sig) for other_sig in around(sig)]
    inverse = 1.0 / (ways[0] + ways[1] + ways[2] + ways[3] + 1.0)
    for copy in source_copies:
        copy.wait_recv()
    src = shell[2]
    for _ in range(ITERS):
        n, s, w, e = around(phi)
        total = ways[0] * n + ways[1] * s + ways[2] * w + ways[3] * e + src
        phi = jnp.where(inside, total * inverse, 0.0)
    phi = phi[8 : 8 + lat, 128 : 128 + lon]
    out_phi[...] = phi

    def piece(z, x, c):
        return table.at[pl.ds(pl.multiple_of(sec_of(z, x, c) * sb, sb), sb), :]

    mine = pl.multiple_of(me * sb, sb)
    for c in range(per_row):
        table[pl.ds(mine + c, lat, stride=per_row), :] = phi[:, c * 128 : (c + 1) * 128]

    from_z, from_x, from_sib = {}, {}, []
    own = piece(at_z, at_x, core)
    nearest = sorted(range(1, zs), key=lambda d: min(d, zs - d))
    for d in nearest:
        from_z[d] = send(own, own, z_peer[d])
    steps = [0] + nearest
    order_x = sorted(x_peer, key=lambda d: -min(d, xs - d))

    def along_x(i):
        dz = steps[i]
        if dz:
            from_z[dz].wait_recv()
        part = piece(lax.rem(at_z + zs - dz, zs), at_x, core)
        for dx in order_x:
            from_x[i, dx] = send(part, part, x_peer[dx])
        from_sib.append(send(part, part, sibling))

    for i in range(zs):
        along_x(i)
    for i in range(zs):
        for dx in order_x:
            from_x[i, dx].wait_recv()
            z = lax.rem(at_z + zs - steps[i], zs)
            part = piece(z, lax.rem(at_x + xs - dx, xs), core)
            from_sib.append(send(part, part, sibling))
    for copy in from_sib:
        copy.wait_recv()
    look_load.wait()

    def look_up(k, carry):
        b = pl.multiple_of(8 * k, 8)
        for r in range(8):
            for j in range(nj):
                at = look_up_at[lax.div(b, 128 // nj), lax.rem(b, 128 // nj) * nj + r * nj + j]
                foot[j, pl.ds(b + r, 1), :] = table[pl.ds(at, 1), :]
        return carry

    lax.fori_loop(0, cx // 8, look_up, 0)
    for j in range(nj):
        write(foot.at[j], out_foot.at[:, 128 * j : 128 * j + 128])
    for copy in sent:
        copy.wait_send()
    for copy in writes:
        copy.wait()


def on_device(
    state, velocity, limiter, footpoint_owner, footpoint_slot, conductance, potential_prior
):
    secs, blks = lax.axis_size("sec"), lax.axis_size("blk")
    xs = 4 if secs % 16 == 0 else 2
    zs = secs // (CORES * xs)
    nq, cx, cy = state.shape
    lat, lon = conductance.shape
    nj = cy // 128
    sb = lat * lon // 128
    blocks = nj * cx
    owner = footpoint_owner.reshape(blocks // 128, 128)
    slot = footpoint_slot.reshape(blocks // 128, 128)
    dims = (zs, xs, secs, blks, nq, cx, cy, lat, lon)
    f32 = jnp.float32
    rows = cx // GROUPS
    messages = 12 + 8 + 8 + zs // 2 + zs // 2 * (xs - 1) + 2 * (zs - 1) + zs * (xs - 1) + zs * xs
    any_space = pl.BlockSpec(memory_space=pl.ANY)
    vmem = pl.BlockSpec(memory_space=pltpu.VMEM)

    def body(*refs):
        kernel(dims, *refs)

    return pl.pallas_call(
        body,
        out_shape=(
            jax.ShapeDtypeStruct(state.shape, f32),
            jax.ShapeDtypeStruct(conductance.shape, f32),
            jax.ShapeDtypeStruct((cx, cy), f32),
        ),
        in_specs=[any_space] * 5 + [vmem, vmem],
        out_specs=(any_space, vmem, any_space),
        scratch_shapes=[
            pltpu.VMEM((nq + 3, nj + 1, cx + PAD, 128), f32),
            pltpu.VMEM((nj, cx, 128), jnp.int32),
            pltpu.VMEM((nq, nj + 1, cx + PAD, 128), f32),
            pltpu.VMEM((nj + 1, cx + PAD, 128), f32),
            pltpu.VMEM((nj + 1, cx + PAD, 128), f32),
            pltpu.VMEM((nj + 1, cx + PAD, 128), f32),
            pltpu.VMEM((nj + 1, cx + PAD, 128), f32),
            pltpu.VMEM((nj + 1, cx + PAD, 128), f32),
            pltpu.VMEM((blocks // 128, 128), jnp.int32),
            pltpu.VMEM((blocks // 128, 128), jnp.int32),
            pltpu.SMEM((blocks // 128, 128), jnp.int32),
            pltpu.VMEM((2, rows, 128), f32),
            pltpu.VMEM((2, rows, 128), f32),
            pltpu.VMEM((4, 8, 128), f32),
            pltpu.VMEM((2, rows, 128), f32),
            pltpu.VMEM((2, rows, 128), f32),
            pltpu.VMEM((3, lat + 16, lon + 256), f32),
            pltpu.VMEM((blocks, 256), jnp.bfloat16),
            pltpu.VMEM((zs // 2, 2, xs, sb, 128), f32),
            pltpu.VMEM((zs // 2, 2, xs, sb, 128), f32),
            pltpu.VMEM((zs // 2, 2, xs, sb, 128), f32),
            pltpu.VMEM((zs // 2, xs - 1, 2, sb, 128), f32),
            pltpu.VMEM((zs // 2, 2, sb, 128), f32),
            pltpu.VMEM((zs - 1, sb, 128), f32),
            pltpu.VMEM((secs * sb, 128), f32),
            pltpu.VMEM((nj, cx, 128), f32),
            pltpu.SemaphoreType.DMA(()),
            pltpu.SemaphoreType.DMA((4 * nj + 2,)),
            pltpu.SemaphoreType.DMA((3 * nj,)),
            pltpu.SemaphoreType.DMA((messages,)),
            pltpu.SemaphoreType.DMA((messages,)),
        ],
        compiler_params=pltpu.CompilerParams(
            collective_id=0, has_side_effects=True, vmem_limit_bytes=56 * 1024 * 1024
        ),
    )(state, velocity, limiter, conductance, potential_prior, owner, slot)


def solution(mesh):
    in_specs = (
        P(None, "sec", "blk"),
        P(None, "sec", "blk"),
        P("sec", "blk"),
        P("sec", "blk", None, None),
        P("sec", "blk", None, None),
        P("sec", "blk"),
        P("sec", "blk"),
    )
    out_specs = (P(None, "sec", "blk"), P("sec", "blk"), P("sec", "blk"))
    return jax.shard_map(
        on_device, mesh=mesh, in_specs=in_specs, out_specs=out_specs, check_vma=False
    )
```

```python
import jax
import jax.numpy as jnp
from jax import lax
from jax.experimental import pallas as pl
from jax.experimental.pallas import tpu as pltpu
from jax.sharding import PartitionSpec as P

ITERS = 4
CORES = 2
TOP = 16
PAD = 40
GROUPS = 8
MESH = pl.DeviceIdType.MESH


def minmod(a, b):
    return jnp.maximum(jnp.minimum(a, b), jnp.minimum(jnp.maximum(a, b), 0.0))


def lane_next(tiles, lane):
    rolled = [pltpu.roll(t, 127, 1) for t in tiles]
    n = len(tiles)
    return [jnp.where(lane == 127, rolled[(j + 1) % n], rolled[j]) for j in range(n)]


def lane_prev(tiles, lane):
    rolled = [pltpu.roll(t, 1, 1) for t in tiles]
    return [jnp.where(lane == 0, rolled[j - 1], rolled[j]) for j in range(len(tiles))]


def kernel(
    dims,
    state,
    velocity,
    limiter,
    sigma,
    prior,
    owner,
    slot,
    fresh,
    out_phi,
    foot,
    grid,
    flags,
    left_x,
    right_x,
    face_x,
    face_y,
    face_before,
    blocks_to,
    block_at,
    look_at,
    look_up_at,
    packs,
    edges,
    corners,
    packs_o,
    edges_o,
    shell,
    weights,
    dense_sib,
    dense_own,
    got_sib,
    got_x,
    z_part,
    got_z,
    table,
    look_sem,
    load_sem,
    send_sem,
    recv_sem,
):
    zs, xs, secs, blks, nq, cx, cy, lat, lon = dims
    nj = cy // 128
    sb = lat * lon // 128
    me = lax.axis_index("sec")
    col = lax.axis_index("blk")
    core = lax.rem(me, CORES)
    at_x = lax.rem(lax.div(me, CORES), xs)
    at_z = lax.div(me, CORES * xs)

    def sec_of(z, x, c):
        return (z * xs + x) * CORES + c

    up, down = lax.rem(me + secs - 1, secs), lax.rem(me + 1, secs)
    left, right = lax.rem(col + blks - 1, blks), lax.rem(col + 1, blks)
    sibling = (me + 1 - 2 * core, col)
    x_peer = {d: (sec_of(at_z, lax.rem(at_x + d, xs), core), col) for d in range(1, xs)}
    z_peer = {d: (sec_of(lax.rem(at_z + d, zs), at_x, core), col) for d in range(1, zs)}
    compass = {
        (-1, 0): (up, col),
        (1, 0): (down, col),
        (0, -1): (me, left),
        (0, 1): (me, right),
        (-1, -1): (up, left),
        (-1, 1): (up, right),
        (1, -1): (down, left),
        (1, 1): (down, right),
    }

    used = [0]
    sent = []

    def send(src, dst, device):
        n = used[0]
        used[0] += 1
        copy = pltpu.make_async_remote_copy(
            src_ref=src,
            dst_ref=dst,
            send_sem=send_sem.at[n],
            recv_sem=recv_sem.at[n],
            device_id=device,
            device_id_type=MESH,
        )
        copy.start()
        sent.append(copy)
        return copy

    barrier = pltpu.get_barrier_semaphore()
    partners = [*compass.values(), *x_peer.values(), *z_peer.values(), sibling]
    for device in partners:
        pl.semaphore_signal(barrier, inc=1, device_id=device, device_id_type=MESH)

    loads = {}

    def load(name, src, dst):
        copy = pltpu.make_async_copy(src, dst, load_sem.at[len(loads)])
        copy.start()
        loads[name] = copy

    load("owner", owner, blocks_to.at[0])
    load("slot", slot, blocks_to.at[1])
    mid = slice(TOP, TOP + cx)
    for j in range(nj):
        lanes = slice(128 * j, 128 * j + 128)
        load(("f", j), state.at[nq - 2 : nq, :, lanes], grid.at[nq - 2 : nq, j, mid, :])
        load(("v", j), velocity.at[:, :, lanes], grid.at[nq : nq + 2, j, mid, :])
        load(("l", j), limiter.at[:, lanes], flags.at[j])
    load("sigma", sigma, shell.at[0, 8 : 8 + lat, 128 : 128 + lon])
    load("prior", prior, shell.at[1, 8 : 8 + lat, 128 : 128 + lon])
    for j in range(nj):
        lanes = slice(128 * j, 128 * j + 128)
        load(("o", j), state.at[: nq - 2, :, lanes], grid.at[: nq - 2, j, mid, :])

    per_row = lon // 128
    loads["owner"].wait()
    loads["slot"].wait()
    at_owner, at_slot = blocks_to[0], blocks_to[1]
    look_at[...] = at_owner * sb + at_slot
    look_load = pltpu.make_async_copy(look_at, look_up_at, look_sem)
    look_load.start()
    ordered = (
        ((at_owner % CORES) * zs + at_owner // (CORES * xs)) * xs + (at_owner // CORES) % xs
    ) * sb
    ordered = ordered + (at_slot % per_row) * lat + at_slot // per_row
    to_lane = lax.broadcasted_iota(jnp.int32, (128, 128), 1)
    from_lane = lax.broadcasted_iota(jnp.int32, (128, 128), 0)
    each = 128 // nj
    moved = ((from_lane % nj) * each + from_lane // nj == to_lane).astype(jnp.float32)

    def move(a):
        return jnp.dot(a.astype(jnp.float32), moved, preferred_element_type=jnp.float32).astype(jnp.int32)

    block_at[...] = move(ordered // 64) * 64 + move(ordered % 64)

    for j in range(nj):
        for name in ("f", "v", "l"):
            loads[(name, j)].wait()
    for j in range(nj):
        grid[nq + 2, j, mid, :] = 0.5 * flags[j].astype(jnp.float32)
    first = nq - 2
    fields = slice(first, first + 5)
    top, bottom = slice(TOP, TOP + 8), slice(TOP + cx - 8, TOP + cx)
    above, below = slice(TOP - 8, TOP), slice(TOP + cx, TOP + cx + 8)
    rows = cx // GROUPS
    wide = lax.broadcasted_iota(jnp.int32, (rows, 128), 1)

    def pack(base, count, width):
        at_left = jnp.zeros((rows, 128), jnp.float32)
        at_right = jnp.zeros((rows, 128), jnp.float32)
        for g in range(GROUPS):
            here = slice(TOP + g * rows, TOP + (g + 1) * rows)
            for a in range(count):
                at = 16 * g + width * a
                mask = (wide >= at) & (wide < at + width)
                at_left = jnp.where(mask, pltpu.roll(grid[base + a, 0, here, :], at, 1), at_left)
                moved = pltpu.roll(grid[base + a, nj - 1, here, :], (at + width) % 128, 1)
                at_right = jnp.where(mask, moved, at_right)
        return at_left, at_right

    def unpack(base, count, width, from_left, from_right, take, put, size, group):
        side = lax.broadcasted_iota(jnp.int32, (size, 128), 1) < 64
        for a in range(count):
            at = 16 * group + width * a
            r = pltpu.roll(from_right[take, :], (128 - at) % 128, 1)
            l = pltpu.roll(from_left[take, :], (256 - width - at) % 128, 1)
            grid[base + a, nj, put, :] = jnp.where(side, r, l)

    to_left, to_right = pack(first, 5, 3)
    packs[0] = to_left
    packs[1] = to_right
    pl.semaphore_wait(barrier, len(partners))
    halo = []
    halo.append(send(grid.at[fields, 0:nj, bottom, :], grid.at[fields, 0:nj, above, :], (down, col)))
    halo.append(send(grid.at[fields, 0:nj, top, :], grid.at[fields, 0:nj, below, :], (up, col)))
    halo.append(send(packs.at[1], edges.at[0], (me, right)))
    halo.append(send(packs.at[0], edges.at[1], (me, left)))
    halo.append(send(packs.at[1, rows - 8 : rows, :], corners.at[0], (down, right)))
    halo.append(send(packs.at[0, rows - 8 : rows, :], corners.at[1], (down, left)))
    halo.append(send(packs.at[1, 0:8, :], corners.at[2], (up, right)))
    halo.append(send(packs.at[0, 0:8, :], corners.at[3], (up, left)))

    row_src = {0: slice(8, 8 + lat), 1: slice(lat, lat + 8), -1: slice(8, 16)}
    row_dst = {0: slice(8, 8 + lat), 1: slice(0, 8), -1: slice(8 + lat, 16 + lat)}
    lane_src = {0: slice(128, 128 + lon), 1: slice(lon, lon + 128), -1: slice(128, 256)}
    lane_dst = {0: slice(128, 128 + lon), 1: slice(0, 128), -1: slice(128 + lon, 256 + lon)}

    def shell_halo(which):
        return [
            send(
                shell.at[which, row_src[dr], lane_src[dc]],
                shell.at[which, row_dst[dr], lane_dst[dc]],
                device,
            )
            for (dr, dc), device in compass.items()
        ]

    loads["sigma"].wait()
    loads["prior"].wait()
    shell_copies = shell_halo(slice(0, 2))

    for j in range(nj):
        loads[("o", j)].wait()
    others = slice(0, nq - 2)
    halo_o = [
        send(grid.at[others, 0:nj, bottom, :], grid.at[others, 0:nj, above, :], (down, col)),
        send(grid.at[others, 0:nj, top, :], grid.at[others, 0:nj, below, :], (up, col)),
    ]
    to_left, to_right = pack(0, nq - 2, 2)
    packs_o[0] = to_left
    packs_o[1] = to_right
    halo_o.append(send(packs_o.at[1], edges_o.at[0], (me, right)))
    halo_o.append(send(packs_o.at[0], edges_o.at[1], (me, left)))

    for copy in halo:
        copy.wait_recv()
    for g in range(GROUPS):
        here = slice(TOP + g * rows, TOP + (g + 1) * rows)
        unpack(first, 5, 3, edges.at[0], edges.at[1], slice(0, rows), here, rows, g)
    unpack(first, 5, 3, corners.at[0], corners.at[1], slice(0, 8), above, 8, GROUPS - 1)
    unpack(first, 5, 3, corners.at[2], corners.at[3], slice(0, 8), below, 8, 0)

    around_rows = cx + 16
    ring = slice(TOP - 8, TOP + cx + 8)
    lane_r = lax.broadcasted_iota(jnp.int32, (around_rows, 128), 1)
    speed_y = [grid[nq + 1, j, ring, :] for j in range(nj + 1)]
    faces_y = [0.2 * (here + after) for here, after in zip(speed_y, lane_next(speed_y, lane_r))]
    faces_before = lane_prev(faces_y, lane_r)
    for j in range(nj + 1):
        face_y[j, ring, :] = faces_y[j]
        face_before[j, ring, :] = faces_before[j]
        face_x[j, ring, :] = 0.2 * (grid[nq, j, ring, :] + grid[nq, j, TOP - 7 : TOP + cx + 9, :])

    def advect(q, tiles_x, start, high):
        lane_h = lax.broadcasted_iota(jnp.int32, (high, 128), 1)
        deep = 16

        def along_x(k, carry):
            b = pl.multiple_of(TOP - 8 + deep * k, 8)
            for j in range(tiles_x):
                here = grid[q, j, pl.ds(b, deep), :]
                lower = here - grid[q, j, pl.ds(b - 1, deep), :]
                upper = grid[q, j, pl.ds(b + 1, deep), :] - here
                half = minmod(lower, upper) * grid[nq + 2, j, pl.ds(b, deep), :]
                left_x[j, pl.ds(b, deep), :] = here + half
                right_x[j, pl.ds(b, deep), :] = here - half
            return carry

        lax.fori_loop(0, (cx + 16) // deep, along_x, 0)
        at, above, below = (slice(start + n, start + n + high) for n in (0, -1, 1))
        here = [grid[q, j, at, :] for j in range(nj + 1)]
        nexts, befores = lane_next(here, lane_h), lane_prev(here, lane_h)
        half = [
            minmod(h - before, after - h) * grid[nq + 2, j, at, :]
            for j, (h, before, after) in enumerate(zip(here, befores, nexts))
        ]
        left_y = [h + m for h, m in zip(here, half)]
        right_y = [h - m for h, m in zip(here, half)]
        right_next, left_before = lane_next(right_y, lane_h), lane_prev(left_y, lane_h)
        for j in range(tiles_x):
            speed = face_y[j, at, :]
            flux_y = speed * jnp.where(speed > 0.0, left_y[j], right_next[j])
            speed = face_before[j, at, :]
            flux_before = speed * jnp.where(speed > 0.0, left_before[j], right_y[j])
            speed = face_x[j, at, :]
            flux_x = speed * jnp.where(speed > 0.0, left_x[j, at, :], right_x[j, below, :])
            speed = face_x[j, above, :]
            flux_above = speed * jnp.where(speed > 0.0, left_x[j, above, :], right_x[j, at, :])
            fresh[q, j, at, :] = here[j] - ((flux_x - flux_above) + (flux_y - flux_before))

    def field(q, carry):
        advect(q, nj + 1, TOP - 8, cx + 16)
        return carry

    lax.fori_loop(nq - 2, nq, field, 0)
    lane_c = lax.broadcasted_iota(jnp.int32, (cx, 128), 1)
    field_x = [fresh[nq - 2, j, mid, :] for j in range(nj + 1)]
    after, before = lane_next(field_x, lane_c), lane_prev(field_x, lane_c)
    for j in range(nj):
        current = 0.5 * (
            fresh[nq - 1, j, TOP + 1 : TOP + cx + 1, :] - fresh[nq - 1, j, TOP - 1 : TOP + cx - 1, :]
        ) - 0.5 * (after[j] - before[j])
        high = current.astype(jnp.bfloat16)
        low = (current - high.astype(jnp.float32)).astype(jnp.bfloat16)
        for k in range(cx // each):
            part = slice((k * nj + j) * each, (k * nj + j + 1) * each)
            weights[part, 0:128] = high[k * each : (k + 1) * each, :]
            weights[part, 128:256] = low[k * each : (k + 1) * each, :]

    order = sorted(range(zs), key=lambda d: -min(d, zs - d))
    duos = [order[n : n + 2] for n in range(0, zs, 2)]
    per_z = xs * sb
    groups = nj * cx // 128

    def sums(duo, to_core):
        ids = jnp.concatenate(
            [
                lax.broadcasted_iota(jnp.int32, (per_z, 128), 0)
                + (to_core * zs + lax.rem(at_z + d, zs)) * per_z
                for d in duo
            ],
            axis=0,
        )
        chosen = [
            jnp.where(ids == block_at[k : k + 1, :], 1.0, 0.0).astype(jnp.bfloat16)
            for k in range(groups)
        ]
        both = jnp.dot(
            jnp.concatenate(chosen, axis=1), weights[...], preferred_element_type=jnp.float32
        )
        return (both[:, :128] + both[:, 128:]).reshape(2, xs, sb, 128)

    sib_copies, x_copies, z_copies = {}, {}, {}

    def for_sibling(n):
        dense_sib[n] = sums(duos[n], 1 - core)
        sib_copies[n] = send(dense_sib.at[n], got_sib.at[n], sibling)

    def for_own(n):
        dense_own[n] = sums(duos[n], core)
        sib_copies[n].wait_recv()
        dense_own[n] = dense_own[n] + got_sib[n]
        for d in sorted(x_peer, key=lambda d: -min(d, xs - d)):
            part = dense_own.at[n, :, lax.rem(at_x + d, xs)]
            x_copies[n, d] = send(part, got_x.at[n, d - 1], x_peer[d])

    for_sibling(0)
    for n in range(len(duos)):
        if n + 1 < len(duos):
            for_sibling(n + 1)
        for_own(n)
    for copy in halo_o:
        copy.wait_recv()
    for g in range(GROUPS):
        here = slice(TOP + g * rows, TOP + (g + 1) * rows)
        unpack(0, nq - 2, 2, edges_o.at[0], edges_o.at[1], slice(0, rows), here, rows, g)

    def other(q, carry):
        advect(q, nj, TOP, cx)
        return carry

    def along_z(n):
        for d in x_peer:
            x_copies[n, d].wait_recv()
        for h, d in enumerate(duos[n]):
            part = dense_own[n, h, at_x]
            for e in x_peer:
                part = part + got_x[n, e - 1, h]
            z_part[n, h] = part
            if d:
                z_copies[d] = send(z_part.at[n, h], got_z.at[d - 1], z_peer[d])

    done = (nq - 2) // 2
    lax.fori_loop(0, done, other, 0)
    for n in range(len(duos)):
        if n == len(duos) - 1:
            lax.fori_loop(done, nq - 2, other, 0)
        along_z(n)
    source = z_part[len(duos) - 1, 1]
    for d in order[:-1]:
        z_copies[d].wait_recv()
        source = source + got_z[d - 1]
    for c in range(lon // 128):
        at = 128 + 128 * c
        shell[2, 8 : 8 + lat, at : at + 128] = source[c * lat : (c + 1) * lat, :]
    source_copies = shell_halo(slice(2, 3))

    for copy in shell_copies:
        copy.wait_recv()
    shape = (lat + 16, lon + 256)
    lat_at = lax.broadcasted_iota(jnp.int32, shape, 0) + (me * lat - 8)
    lon_at = lax.broadcasted_iota(jnp.int32, shape, 1) + (col * lon - 128)
    inside = (lat_at >= 0) & (lat_at < secs * lat) & (lon_at >= 0) & (lon_at < blks * lon)
    sig = jnp.where(inside, shell[0], 0.0)
    phi = jnp.where(inside, shell[1], 0.0)

    def around(a):
        return (
            pltpu.roll(a, 1, 0),
            pltpu.roll(a, lat + 15, 0),
            pltpu.roll(a, 1, 1),
            pltpu.roll(a, lon + 255, 1),
        )

    ways = [0.5 * (sig + other_sig) for other_sig in around(sig)]
    inverse = 1.0 / (ways[0] + ways[1] + ways[2] + ways[3] + 1.0)
    for copy in source_copies:
        copy.wait_recv()
    src = shell[2]
    for _ in range(ITERS):
        n, s, w, e = around(phi)
        total = ways[0] * n + ways[1] * s + ways[2] * w + ways[3] * e + src
        phi = jnp.where(inside, total * inverse, 0.0)
    phi = phi[8 : 8 + lat, 128 : 128 + lon]
    out_phi[...] = phi

    def piece(z, x, c):
        return table.at[pl.ds(pl.multiple_of(sec_of(z, x, c) * sb, sb), sb), :]

    mine = pl.multiple_of(me * sb, sb)
    for c in range(per_row):
        table[pl.ds(mine + c, lat, stride=per_row), :] = phi[:, c * 128 : (c + 1) * 128]

    from_z, from_x, from_sib = {}, {}, []
    own = piece(at_z, at_x, core)
    nearest = sorted(range(1, zs), key=lambda d: min(d, zs - d))
    for d in nearest:
        from_z[d] = send(own, own, z_peer[d])
    steps = [0] + nearest
    order_x = sorted(x_peer, key=lambda d: -min(d, xs - d))

    def along_x(i):
        dz = steps[i]
        if dz:
            from_z[dz].wait_recv()
        part = piece(lax.rem(at_z + zs - dz, zs), at_x, core)
        for dx in order_x:
            from_x[i, dx] = send(part, part, x_peer[dx])
        from_sib.append(send(part, part, sibling))

    for i in range(zs):
        along_x(i)
    for i in range(zs):
        for dx in order_x:
            from_x[i, dx].wait_recv()
            z = lax.rem(at_z + zs - steps[i], zs)
            part = piece(z, lax.rem(at_x + xs - dx, xs), core)
            from_sib.append(send(part, part, sibling))
    for copy in from_sib:
        copy.wait_recv()
    look_load.wait()

    def look_up(k, carry):
        b = pl.multiple_of(8 * k, 8)
        for r in range(8):
            for j in range(nj):
                at = look_up_at[lax.div(b, 128 // nj), lax.rem(b, 128 // nj) * nj + r * nj + j]
                foot[j, pl.ds(b + r, 1), :] = table[pl.ds(at, 1), :]
        return carry

    lax.fori_loop(0, cx // 8, look_up, 0)
    for copy in sent:
        copy.wait_send()


def write_out(fresh, phi, foot, out_state, out_phi, out_foot, sem):
    cx = foot.shape[1]
    copies = [pltpu.make_async_copy(phi, out_phi, sem.at[0])]
    for j in range(foot.shape[0]):
        lanes = slice(128 * j, 128 * j + 128)
        mid = fresh.at[:, j, TOP : TOP + cx, :]
        copies.append(pltpu.make_async_copy(mid, out_state.at[:, :, lanes], sem.at[2 * j + 1]))
        copies.append(pltpu.make_async_copy(foot.at[j], out_foot.at[:, lanes], sem.at[2 * j + 2]))
    for copy in copies:
        copy.start()
    for copy in copies:
        copy.wait()


def on_device(
    state, velocity, limiter, footpoint_owner, footpoint_slot, conductance, potential_prior
):
    secs, blks = lax.axis_size("sec"), lax.axis_size("blk")
    xs = 4 if secs % 16 == 0 else 2
    zs = secs // (CORES * xs)
    nq, cx, cy = state.shape
    lat, lon = conductance.shape
    nj = cy // 128
    sb = lat * lon // 128
    blocks = nj * cx
    owner = footpoint_owner.reshape(blocks // 128, 128)
    slot = footpoint_slot.reshape(blocks // 128, 128)
    dims = (zs, xs, secs, blks, nq, cx, cy, lat, lon)
    f32 = jnp.float32
    rows = cx // GROUPS
    messages = 12 + 8 + 8 + zs // 2 + zs // 2 * (xs - 1) + 2 * (zs - 1) + zs * (xs - 1) + zs * xs
    any_space = pl.BlockSpec(memory_space=pl.ANY)
    vmem = pl.BlockSpec(memory_space=pltpu.VMEM)

    def body(*refs):
        kernel(dims, *refs)

    results = pl.pallas_call(
        body,
        out_shape=(
            pltpu.VMEM((nq, nj + 1, cx + PAD, 128), f32),
            pltpu.VMEM(conductance.shape, f32),
            pltpu.VMEM((nj, cx, 128), f32),
        ),
        in_specs=[pl.BlockSpec(memory_space=pltpu.HBM)] * 7,
        out_specs=(vmem, vmem, vmem),
        scratch_shapes=[
            pltpu.VMEM((nq + 3, nj + 1, cx + PAD, 128), f32),
            pltpu.VMEM((nj, cx, 128), jnp.int32),
            pltpu.VMEM((nj + 1, cx + PAD, 128), f32),
            pltpu.VMEM((nj + 1, cx + PAD, 128), f32),
            pltpu.VMEM((nj + 1, cx + PAD, 128), f32),
            pltpu.VMEM((nj + 1, cx + PAD, 128), f32),
            pltpu.VMEM((nj + 1, cx + PAD, 128), f32),
            pltpu.VMEM((2, blocks // 128, 128), jnp.int32),
            pltpu.VMEM((blocks // 128, 128), jnp.int32),
            pltpu.VMEM((blocks // 128, 128), jnp.int32),
            pltpu.SMEM((blocks // 128, 128), jnp.int32),
            pltpu.VMEM((2, rows, 128), f32),
            pltpu.VMEM((2, rows, 128), f32),
            pltpu.VMEM((4, 8, 128), f32),
            pltpu.VMEM((2, rows, 128), f32),
            pltpu.VMEM((2, rows, 128), f32),
            pltpu.VMEM((3, lat + 16, lon + 256), f32),
            pltpu.VMEM((blocks, 256), jnp.bfloat16),
            pltpu.VMEM((zs // 2, 2, xs, sb, 128), f32),
            pltpu.VMEM((zs // 2, 2, xs, sb, 128), f32),
            pltpu.VMEM((zs // 2, 2, xs, sb, 128), f32),
            pltpu.VMEM((zs // 2, xs - 1, 2, sb, 128), f32),
            pltpu.VMEM((zs // 2, 2, sb, 128), f32),
            pltpu.VMEM((zs - 1, sb, 128), f32),
            pltpu.VMEM((secs * sb, 128), f32),
            pltpu.SemaphoreType.DMA(()),
            pltpu.SemaphoreType.DMA((4 * nj + 4,)),
            pltpu.SemaphoreType.DMA((messages,)),
            pltpu.SemaphoreType.DMA((messages,)),
        ],
        compiler_params=pltpu.CompilerParams(
            collective_id=0, has_side_effects=True, vmem_limit_bytes=40 * 1024 * 1024
        ),
    )(
        *[
            pltpu.with_memory_space_constraint(a, pltpu.HBM)
            for a in (state, velocity, limiter, conductance, potential_prior, owner, slot)
        ],
    )
    return pl.pallas_call(
        write_out,
        out_shape=(
            jax.ShapeDtypeStruct(state.shape, f32),
            jax.ShapeDtypeStruct(conductance.shape, f32),
            jax.ShapeDtypeStruct((cx, cy), f32),
        ),
        in_specs=[vmem] * 3,
        out_specs=(any_space,) * 3,
        scratch_shapes=[pltpu.SemaphoreType.DMA((2 * nj + 1,))],
        compiler_params=pltpu.CompilerParams(vmem_limit_bytes=16 * 1024 * 1024),
    )(*[pltpu.with_memory_space_constraint(r, pltpu.VMEM) for r in results])


def solution(mesh):
    in_specs = (
        P(None, "sec", "blk"),
        P(None, "sec", "blk"),
        P("sec", "blk"),
        P("sec", "blk", None, None),
        P("sec", "blk", None, None),
        P("sec", "blk"),
        P("sec", "blk"),
    )
    out_specs = (P(None, "sec", "blk"), P("sec", "blk"), P("sec", "blk"))
    return jax.shard_map(
        on_device, mesh=mesh, in_specs=in_specs, out_specs=out_specs, check_vma=False
    )
```

```python
import jax
import jax.numpy as jnp
from jax import lax
from jax.experimental import pallas as pl
from jax.experimental.pallas import tpu as pltpu
from jax.sharding import PartitionSpec as P

ITERS = 4
CORES = 2
TOP = 16
PAD = 40
GROUPS = 8
MESH = pl.DeviceIdType.MESH


def minmod(a, b):
    return jnp.maximum(jnp.minimum(a, b), jnp.minimum(jnp.maximum(a, b), 0.0))


def lane_next(tiles, lane):
    rolled = [pltpu.roll(t, 127, 1) for t in tiles]
    n = len(tiles)
    return [jnp.where(lane == 127, rolled[(j + 1) % n], rolled[j]) for j in range(n)]


def lane_prev(tiles, lane):
    rolled = [pltpu.roll(t, 1, 1) for t in tiles]
    return [jnp.where(lane == 0, rolled[j - 1], rolled[j]) for j in range(len(tiles))]


def kernel(
    dims,
    state,
    velocity,
    limiter,
    sigma,
    prior,
    owner,
    slot,
    fresh,
    out_phi,
    foot,
    grid,
    flags,
    left_x,
    right_x,
    face_x,
    face_y,
    face_before,
    blocks_to,
    block_at,
    look_at,
    look_up_at,
    packs,
    edges,
    corners,
    packs_o,
    edges_o,
    shell,
    weights,
    dense_sib,
    dense_own,
    got_sib,
    got_x,
    z_part,
    got_z,
    table,
    look_sem,
    load_sem,
    send_sem,
    recv_sem,
):
    zs, xs, secs, blks, nq, cx, cy, lat, lon = dims
    nj = cy // 128
    sb = lat * lon // 128
    me = lax.axis_index("sec")
    col = lax.axis_index("blk")
    core = lax.rem(me, CORES)
    at_x = lax.rem(lax.div(me, CORES), xs)
    at_z = lax.div(me, CORES * xs)

    def sec_of(z, x, c):
        return (z * xs + x) * CORES + c

    up, down = lax.rem(me + secs - 1, secs), lax.rem(me + 1, secs)
    left, right = lax.rem(col + blks - 1, blks), lax.rem(col + 1, blks)
    sibling = (me + 1 - 2 * core, col)
    x_peer = {d: (sec_of(at_z, lax.rem(at_x + d, xs), core), col) for d in range(1, xs)}
    z_peer = {d: (sec_of(lax.rem(at_z + d, zs), at_x, core), col) for d in range(1, zs)}
    compass = {
        (-1, 0): (up, col),
        (1, 0): (down, col),
        (0, -1): (me, left),
        (0, 1): (me, right),
        (-1, -1): (up, left),
        (-1, 1): (up, right),
        (1, -1): (down, left),
        (1, 1): (down, right),
    }

    used = [0]
    sent = []

    def send(src, dst, device):
        n = used[0]
        used[0] += 1
        copy = pltpu.make_async_remote_copy(
            src_ref=src,
            dst_ref=dst,
            send_sem=send_sem.at[n],
            recv_sem=recv_sem.at[n],
            device_id=device,
            device_id_type=MESH,
        )
        copy.start()
        sent.append(copy)
        return copy

    barrier = pltpu.get_barrier_semaphore()
    partners = [*compass.values(), *x_peer.values(), *z_peer.values(), sibling]
    for device in partners:
        pl.semaphore_signal(barrier, inc=1, device_id=device, device_id_type=MESH)

    loads = {}

    def load(name, src, dst):
        copy = pltpu.make_async_copy(src, dst, load_sem.at[len(loads)])
        copy.start()
        loads[name] = copy

    mid = slice(TOP, TOP + cx)
    for j in range(nj):
        lanes = slice(128 * j, 128 * j + 128)
        load(("f", j), state.at[nq - 2 : nq, :, lanes], grid.at[nq - 2 : nq, j, mid, :])
        load(("v", j), velocity.at[:, :, lanes], grid.at[nq : nq + 2, j, mid, :])
        load(("l", j), limiter.at[:, lanes], flags.at[j])
    load("owner", owner, blocks_to.at[0])
    load("slot", slot, blocks_to.at[1])
    load("sigma", sigma, shell.at[0, 8 : 8 + lat, 128 : 128 + lon])
    load("prior", prior, shell.at[1, 8 : 8 + lat, 128 : 128 + lon])
    for j in range(nj):
        lanes = slice(128 * j, 128 * j + 128)
        load(("o", j), state.at[: nq - 2, :, lanes], grid.at[: nq - 2, j, mid, :])

    for j in range(nj):
        for name in ("f", "v", "l"):
            loads[(name, j)].wait()
    for j in range(nj):
        grid[nq + 2, j, mid, :] = 0.5 * flags[j].astype(jnp.float32)
    first = nq - 2
    fields = slice(first, first + 5)
    top, bottom = slice(TOP, TOP + 8), slice(TOP + cx - 8, TOP + cx)
    above, below = slice(TOP - 8, TOP), slice(TOP + cx, TOP + cx + 8)
    rows = cx // GROUPS
    wide = lax.broadcasted_iota(jnp.int32, (rows, 128), 1)

    def pack(base, count, width):
        at_left = jnp.zeros((rows, 128), jnp.float32)
        at_right = jnp.zeros((rows, 128), jnp.float32)
        for g in range(GROUPS):
            here = slice(TOP + g * rows, TOP + (g + 1) * rows)
            for a in range(count):
                at = 16 * g + width * a
                mask = (wide >= at) & (wide < at + width)
                at_left = jnp.where(mask, pltpu.roll(grid[base + a, 0, here, :], at, 1), at_left)
                moved = pltpu.roll(grid[base + a, nj - 1, here, :], (at + width) % 128, 1)
                at_right = jnp.where(mask, moved, at_right)
        return at_left, at_right

    def unpack(base, count, width, from_left, from_right, take, put, size, group):
        side = lax.broadcasted_iota(jnp.int32, (size, 128), 1) < 64
        for a in range(count):
            at = 16 * group + width * a
            r = pltpu.roll(from_right[take, :], (128 - at) % 128, 1)
            l = pltpu.roll(from_left[take, :], (256 - width - at) % 128, 1)
            grid[base + a, nj, put, :] = jnp.where(side, r, l)

    to_left, to_right = pack(first, 5, 3)
    packs[0] = to_left
    packs[1] = to_right
    pl.semaphore_wait(barrier, len(partners))
    halo = []
    halo.append(send(grid.at[fields, 0:nj, bottom, :], grid.at[fields, 0:nj, above, :], (down, col)))
    halo.append(send(grid.at[fields, 0:nj, top, :], grid.at[fields, 0:nj, below, :], (up, col)))
    halo.append(send(packs.at[1], edges.at[0], (me, right)))
    halo.append(send(packs.at[0], edges.at[1], (me, left)))
    halo.append(send(packs.at[1, rows - 8 : rows, :], corners.at[0], (down, right)))
    halo.append(send(packs.at[0, rows - 8 : rows, :], corners.at[1], (down, left)))
    halo.append(send(packs.at[1, 0:8, :], corners.at[2], (up, right)))
    halo.append(send(packs.at[0, 0:8, :], corners.at[3], (up, left)))

    row_src = {0: slice(8, 8 + lat), 1: slice(lat, lat + 8), -1: slice(8, 16)}
    row_dst = {0: slice(8, 8 + lat), 1: slice(0, 8), -1: slice(8 + lat, 16 + lat)}
    lane_src = {0: slice(128, 128 + lon), 1: slice(lon, lon + 128), -1: slice(128, 256)}
    lane_dst = {0: slice(128, 128 + lon), 1: slice(0, 128), -1: slice(128 + lon, 256 + lon)}

    def shell_halo(which):
        return [
            send(
                shell.at[which, row_src[dr], lane_src[dc]],
                shell.at[which, row_dst[dr], lane_dst[dc]],
                device,
            )
            for (dr, dc), device in compass.items()
        ]

    loads["sigma"].wait()
    loads["prior"].wait()
    shell_copies = shell_halo(slice(0, 2))

    per_row = lon // 128
    loads["owner"].wait()
    loads["slot"].wait()
    at_owner, at_slot = blocks_to[0], blocks_to[1]
    look_at[...] = at_owner * sb + at_slot
    look_load = pltpu.make_async_copy(look_at, look_up_at, look_sem)
    look_load.start()
    ordered = (
        ((at_owner % CORES) * zs + at_owner // (CORES * xs)) * xs + (at_owner // CORES) % xs
    ) * sb
    ordered = ordered + (at_slot % per_row) * lat + at_slot // per_row
    to_lane = lax.broadcasted_iota(jnp.int32, (128, 128), 1)
    from_lane = lax.broadcasted_iota(jnp.int32, (128, 128), 0)
    each = 128 // nj
    moved = ((from_lane % nj) * each + from_lane // nj == to_lane).astype(jnp.float32)

    def move(a):
        return jnp.dot(a.astype(jnp.float32), moved, preferred_element_type=jnp.float32).astype(jnp.int32)

    block_at[...] = move(ordered // 64) * 64 + move(ordered % 64)

    for j in range(nj):
        loads[("o", j)].wait()
    others = slice(0, nq - 2)
    halo_o = [
        send(grid.at[others, 0:nj, bottom, :], grid.at[others, 0:nj, above, :], (down, col)),
        send(grid.at[others, 0:nj, top, :], grid.at[others, 0:nj, below, :], (up, col)),
    ]
    to_left, to_right = pack(0, nq - 2, 2)
    packs_o[0] = to_left
    packs_o[1] = to_right
    halo_o.append(send(packs_o.at[1], edges_o.at[0], (me, right)))
    halo_o.append(send(packs_o.at[0], edges_o.at[1], (me, left)))

    for copy in halo:
        copy.wait_recv()
    for g in range(GROUPS):
        here = slice(TOP + g * rows, TOP + (g + 1) * rows)
        unpack(first, 5, 3, edges.at[0], edges.at[1], slice(0, rows), here, rows, g)
    unpack(first, 5, 3, corners.at[0], corners.at[1], slice(0, 8), above, 8, GROUPS - 1)
    unpack(first, 5, 3, corners.at[2], corners.at[3], slice(0, 8), below, 8, 0)

    around_rows = cx + 16
    ring = slice(TOP - 8, TOP + cx + 8)
    lane_r = lax.broadcasted_iota(jnp.int32, (around_rows, 128), 1)
    speed_y = [grid[nq + 1, j, ring, :] for j in range(nj + 1)]
    faces_y = [0.2 * (here + after) for here, after in zip(speed_y, lane_next(speed_y, lane_r))]
    faces_before = lane_prev(faces_y, lane_r)
    for j in range(nj + 1):
        face_y[j, ring, :] = faces_y[j]
        face_before[j, ring, :] = faces_before[j]
        face_x[j, ring, :] = 0.2 * (grid[nq, j, ring, :] + grid[nq, j, TOP - 7 : TOP + cx + 9, :])

    def advect(q, tiles_x, start, high):
        lane_h = lax.broadcasted_iota(jnp.int32, (high, 128), 1)
        deep = 16

        def along_x(k, carry):
            b = pl.multiple_of(TOP - 8 + deep * k, 8)
            for j in range(tiles_x):
                here = grid[q, j, pl.ds(b, deep), :]
                lower = here - grid[q, j, pl.ds(b - 1, deep), :]
                upper = grid[q, j, pl.ds(b + 1, deep), :] - here
                half = minmod(lower, upper) * grid[nq + 2, j, pl.ds(b, deep), :]
                left_x[j, pl.ds(b, deep), :] = here + half
                right_x[j, pl.ds(b, deep), :] = here - half
            return carry

        lax.fori_loop(0, (cx + 16) // deep, along_x, 0)
        at, above, below = (slice(start + n, start + n + high) for n in (0, -1, 1))
        here = [grid[q, j, at, :] for j in range(nj + 1)]
        nexts, befores = lane_next(here, lane_h), lane_prev(here, lane_h)
        half = [
            minmod(h - before, after - h) * grid[nq + 2, j, at, :]
            for j, (h, before, after) in enumerate(zip(here, befores, nexts))
        ]
        left_y = [h + m for h, m in zip(here, half)]
        right_y = [h - m for h, m in zip(here, half)]
        right_next, left_before = lane_next(right_y, lane_h), lane_prev(left_y, lane_h)
        for j in range(tiles_x):
            speed = face_y[j, at, :]
            flux_y = speed * jnp.where(speed > 0.0, left_y[j], right_next[j])
            speed = face_before[j, at, :]
            flux_before = speed * jnp.where(speed > 0.0, left_before[j], right_y[j])
            speed = face_x[j, at, :]
            flux_x = speed * jnp.where(speed > 0.0, left_x[j, at, :], right_x[j, below, :])
            speed = face_x[j, above, :]
            flux_above = speed * jnp.where(speed > 0.0, left_x[j, above, :], right_x[j, at, :])
            fresh[q, j, at, :] = here[j] - ((flux_x - flux_above) + (flux_y - flux_before))

    def field(q, carry):
        advect(q, nj + 1, TOP - 8, cx + 16)
        return carry

    lax.fori_loop(nq - 2, nq, field, 0)
    lane_c = lax.broadcasted_iota(jnp.int32, (cx, 128), 1)
    field_x = [fresh[nq - 2, j, mid, :] for j in range(nj + 1)]
    after, before = lane_next(field_x, lane_c), lane_prev(field_x, lane_c)
    for j in range(nj):
        current = 0.5 * (
            fresh[nq - 1, j, TOP + 1 : TOP + cx + 1, :] - fresh[nq - 1, j, TOP - 1 : TOP + cx - 1, :]
        ) - 0.5 * (after[j] - before[j])
        high = current.astype(jnp.bfloat16)
        low = (current - high.astype(jnp.float32)).astype(jnp.bfloat16)
        for k in range(cx // each):
            part = slice((k * nj + j) * each, (k * nj + j + 1) * each)
            weights[part, 0:128] = high[k * each : (k + 1) * each, :]
            weights[part, 128:256] = low[k * each : (k + 1) * each, :]

    order = sorted(range(zs), key=lambda d: -min(d, zs - d))
    duos = [order[n : n + 2] for n in range(0, zs, 2)]
    per_z = xs * sb
    groups = nj * cx // 128

    def sums(duo, to_core):
        ids = jnp.concatenate(
            [
                lax.broadcasted_iota(jnp.int32, (per_z, 128), 0)
                + (to_core * zs + lax.rem(at_z + d, zs)) * per_z
                for d in duo
            ],
            axis=0,
        )
        chosen = [
            jnp.where(ids == block_at[k : k + 1, :], 1.0, 0.0).astype(jnp.bfloat16)
            for k in range(groups)
        ]
        both = jnp.dot(
            jnp.concatenate(chosen, axis=1), weights[...], preferred_element_type=jnp.float32
        )
        return (both[:, :128] + both[:, 128:]).reshape(2, xs, sb, 128)

    sib_copies, x_copies, z_copies = {}, {}, {}
    order_x = sorted(x_peer, key=lambda d: -min(d, xs - d))

    def for_sibling(n):
        dense_sib[n] = sums(duos[n], 1 - core)
        sib_copies[n] = send(dense_sib.at[n], got_sib.at[n], sibling)

    def for_own(n):
        dense_own[n] = sums(duos[n], core)
        sib_copies[n].wait_recv()
        dense_own[n] = dense_own[n] + got_sib[n]
        last = n == len(duos) - 1
        for h in (slice(0, 1), slice(1, 2)) if last else (slice(0, 2),):
            for d in order_x:
                part = dense_own.at[n, h, lax.rem(at_x + d, xs)]
                copy = send(part, got_x.at[n, d - 1, h], x_peer[d])
                x_copies.setdefault((n, h.start), []).append(copy)

    for_sibling(0)
    for n in range(len(duos)):
        if n + 1 < len(duos):
            for_sibling(n + 1)
        for_own(n)
    for copy in halo_o:
        copy.wait_recv()
    for g in range(GROUPS):
        here = slice(TOP + g * rows, TOP + (g + 1) * rows)
        unpack(0, nq - 2, 2, edges_o.at[0], edges_o.at[1], slice(0, rows), here, rows, g)

    def other(q, carry):
        advect(q, nj, TOP, cx)
        return carry

    def along_z(n):
        for h, d in enumerate(duos[n]):
            for copy in x_copies.get((n, h), []):
                copy.wait_recv()
            part = dense_own[n, h, at_x]
            for e in x_peer:
                part = part + got_x[n, e - 1, h]
            z_part[n, h] = part
            if d:
                z_copies[d] = send(z_part.at[n, h], got_z.at[d - 1], z_peer[d])

    done = (nq - 2) // 2
    lax.fori_loop(0, done, other, 0)
    for n in range(len(duos)):
        if n == len(duos) - 1:
            lax.fori_loop(done, nq - 2, other, 0)
        along_z(n)
    source = z_part[len(duos) - 1, 1]
    for d in order[:-1]:
        z_copies[d].wait_recv()
        source = source + got_z[d - 1]
    for c in range(lon // 128):
        at = 128 + 128 * c
        shell[2, 8 : 8 + lat, at : at + 128] = source[c * lat : (c + 1) * lat, :]
    source_copies = shell_halo(slice(2, 3))

    for copy in shell_copies:
        copy.wait_recv()
    shape = (lat + 16, lon + 256)
    lat_at = lax.broadcasted_iota(jnp.int32, shape, 0) + (me * lat - 8)
    lon_at = lax.broadcasted_iota(jnp.int32, shape, 1) + (col * lon - 128)
    inside = (lat_at >= 0) & (lat_at < secs * lat) & (lon_at >= 0) & (lon_at < blks * lon)
    sig = jnp.where(inside, shell[0], 0.0)
    phi = jnp.where(inside, shell[1], 0.0)

    def around(a):
        return (
            pltpu.roll(a, 1, 0),
            pltpu.roll(a, lat + 15, 0),
            pltpu.roll(a, 1, 1),
            pltpu.roll(a, lon + 255, 1),
        )

    ways = [0.5 * (sig + other_sig) for other_sig in around(sig)]
    inverse = 1.0 / (ways[0] + ways[1] + ways[2] + ways[3] + 1.0)
    for copy in source_copies:
        copy.wait_recv()
    src = shell[2]
    for _ in range(ITERS):
        n, s, w, e = around(phi)
        total = ways[0] * n + ways[1] * s + ways[2] * w + ways[3] * e + src
        phi = jnp.where(inside, total * inverse, 0.0)
    phi = phi[8 : 8 + lat, 128 : 128 + lon]
    out_phi[...] = phi

    split = sb // 4 * 3

    def piece(z, x, start=0, size=sb):
        at = sec_of(z, x, core) * sb + start
        return table.at[pl.ds(pl.multiple_of(at, sb // 4), size), :]

    mine = pl.multiple_of(me * sb, sb)
    for c in range(per_row):
        table[pl.ds(mine + c, lat, stride=per_row), :] = phi[:, c * 128 : (c + 1) * 128]

    from_z, from_x, first_rows, last_rows, from_sib = {}, {}, {}, {}, []
    own = piece(at_z, at_x)
    nearest = sorted(range(1, zs), key=lambda d: min(d, zs - d))
    for d in nearest[:2]:
        from_z[d] = send(own, own, z_peer[d])
    for d in order_x:
        from_x[d] = send(own, own, x_peer[d])
    for d in nearest[2:]:
        from_z[d] = send(own, own, z_peer[d])

    def share(part):
        from_sib.append(send(part, part, sibling))

    def z_back(d):
        return lax.rem(at_z + zs - d, zs)

    def x_back(d):
        return lax.rem(at_x + xs - d, xs)

    share(own)

    def along_x(d):
        from_z[d].wait_recv()
        part = piece(z_back(d), at_x, 0, split)
        for e in order_x:
            first_rows[d, e] = send(part, part, x_peer[e])
        share(piece(z_back(d), at_x))

    for d in nearest[:2]:
        along_x(d)
    for e in order_x[::-1]:
        from_x[e].wait_recv()
        part = piece(at_z, x_back(e), split, sb - split)
        for d in nearest[::-1]:
            last_rows[d, e] = send(part, part, z_peer[d])
        share(piece(at_z, x_back(e)))
    for d in nearest[2:]:
        along_x(d)
    for d in nearest:
        for e in order_x:
            first_rows[d, e].wait_recv()
            last_rows[d, e].wait_recv()
            share(piece(z_back(d), x_back(e)))
    for copy in from_sib:
        copy.wait_recv()
    look_load.wait()

    def look_up(k, carry):
        b = pl.multiple_of(8 * k, 8)
        for r in range(8):
            for j in range(nj):
                at = look_up_at[lax.div(b, 128 // nj), lax.rem(b, 128 // nj) * nj + r * nj + j]
                foot[j, pl.ds(b + r, 1), :] = table[pl.ds(at, 1), :]
        return carry

    lax.fori_loop(0, cx // 8, look_up, 0)
    for copy in sent:
        copy.wait_send()


def write_out(fresh, phi, foot, out_state, out_phi, out_foot, sem):
    cx = foot.shape[1]
    copies = [pltpu.make_async_copy(phi, out_phi, sem.at[0])]
    for j in range(foot.shape[0]):
        lanes = slice(128 * j, 128 * j + 128)
        mid = fresh.at[:, j, TOP : TOP + cx, :]
        copies.append(pltpu.make_async_copy(mid, out_state.at[:, :, lanes], sem.at[2 * j + 1]))
        copies.append(pltpu.make_async_copy(foot.at[j], out_foot.at[:, lanes], sem.at[2 * j + 2]))
    for copy in copies:
        copy.start()
    for copy in copies:
        copy.wait()


def on_device(
    state, velocity, limiter, footpoint_owner, footpoint_slot, conductance, potential_prior
):
    secs, blks = lax.axis_size("sec"), lax.axis_size("blk")
    xs = 4 if secs % 16 == 0 else 2
    zs = secs // (CORES * xs)
    nq, cx, cy = state.shape
    lat, lon = conductance.shape
    nj = cy // 128
    sb = lat * lon // 128
    blocks = nj * cx
    owner = footpoint_owner.reshape(blocks // 128, 128)
    slot = footpoint_slot.reshape(blocks // 128, 128)
    dims = (zs, xs, secs, blks, nq, cx, cy, lat, lon)
    f32 = jnp.float32
    rows = cx // GROUPS
    messages = 12 + 8 + 8 + zs // 2 + zs // 2 * (xs - 1) + (xs - 1) + 2 * (zs - 1) + (xs - 1) + 2 * (zs - 1) * (xs - 1) + zs * xs
    any_space = pl.BlockSpec(memory_space=pl.ANY)
    vmem = pl.BlockSpec(memory_space=pltpu.VMEM)

    def body(*refs):
        kernel(dims, *refs)

    results = pl.pallas_call(
        body,
        out_shape=(
            pltpu.VMEM((nq, nj + 1, cx + PAD, 128), f32),
            pltpu.VMEM(conductance.shape, f32),
            pltpu.VMEM((nj, cx, 128), f32),
        ),
        in_specs=[pl.BlockSpec(memory_space=pltpu.HBM)] * 7,
        out_specs=(vmem, vmem, vmem),
        scratch_shapes=[
            pltpu.VMEM((nq + 3, nj + 1, cx + PAD, 128), f32),
            pltpu.VMEM((nj, cx, 128), jnp.int32),
            pltpu.VMEM((nj + 1, cx + PAD, 128), f32),
            pltpu.VMEM((nj + 1, cx + PAD, 128), f32),
            pltpu.VMEM((nj + 1, cx + PAD, 128), f32),
            pltpu.VMEM((nj + 1, cx + PAD, 128), f32),
            pltpu.VMEM((nj + 1, cx + PAD, 128), f32),
            pltpu.VMEM((2, blocks // 128, 128), jnp.int32),
            pltpu.VMEM((blocks // 128, 128), jnp.int32),
            pltpu.VMEM((blocks // 128, 128), jnp.int32),
            pltpu.SMEM((blocks // 128, 128), jnp.int32),
            pltpu.VMEM((2, rows, 128), f32),
            pltpu.VMEM((2, rows, 128), f32),
            pltpu.VMEM((4, 8, 128), f32),
            pltpu.VMEM((2, rows, 128), f32),
            pltpu.VMEM((2, rows, 128), f32),
            pltpu.VMEM((3, lat + 16, lon + 256), f32),
            pltpu.VMEM((blocks, 256), jnp.bfloat16),
            pltpu.VMEM((zs // 2, 2, xs, sb, 128), f32),
            pltpu.VMEM((zs // 2, 2, xs, sb, 128), f32),
            pltpu.VMEM((zs // 2, 2, xs, sb, 128), f32),
            pltpu.VMEM((zs // 2, xs - 1, 2, sb, 128), f32),
            pltpu.VMEM((zs // 2, 2, sb, 128), f32),
            pltpu.VMEM((zs - 1, sb, 128), f32),
            pltpu.VMEM((secs * sb, 128), f32),
            pltpu.SemaphoreType.DMA(()),
            pltpu.SemaphoreType.DMA((4 * nj + 4,)),
            pltpu.SemaphoreType.DMA((messages,)),
            pltpu.SemaphoreType.DMA((messages,)),
        ],
        compiler_params=pltpu.CompilerParams(
            collective_id=0, has_side_effects=True, vmem_limit_bytes=40 * 1024 * 1024
        ),
    )(
        *[
            pltpu.with_memory_space_constraint(a, pltpu.HBM)
            for a in (state, velocity, limiter, conductance, potential_prior, owner, slot)
        ],
    )
    return pl.pallas_call(
        write_out,
        out_shape=(
            jax.ShapeDtypeStruct(state.shape, f32),
            jax.ShapeDtypeStruct(conductance.shape, f32),
            jax.ShapeDtypeStruct((cx, cy), f32),
        ),
        in_specs=[vmem] * 3,
        out_specs=(any_space,) * 3,
        scratch_shapes=[pltpu.SemaphoreType.DMA((2 * nj + 1,))],
        compiler_params=pltpu.CompilerParams(vmem_limit_bytes=16 * 1024 * 1024),
    )(*[pltpu.with_memory_space_constraint(r, pltpu.VMEM) for r in results])


def solution(mesh):
    in_specs = (
        P(None, "sec", "blk"),
        P(None, "sec", "blk"),
        P("sec", "blk"),
        P("sec", "blk", None, None),
        P("sec", "blk", None, None),
        P("sec", "blk"),
        P("sec", "blk"),
    )
    out_specs = (P(None, "sec", "blk"), P("sec", "blk"), P("sec", "blk"))
    return jax.shard_map(
        on_device, mesh=mesh, in_specs=in_specs, out_specs=out_specs, check_vma=False
    )
```

```python
import jax
import jax.numpy as jnp
from jax import lax
from jax.experimental import pallas as pl
from jax.experimental.pallas import tpu as pltpu
from jax.sharding import PartitionSpec as P

ITERS = 4
CORES = 2
TOP = 16
PAD = 40
GROUPS = 8
MESH = pl.DeviceIdType.MESH


def minmod(a, b):
    return jnp.maximum(jnp.minimum(a, b), jnp.minimum(jnp.maximum(a, b), 0.0))


def lane_next(tiles, lane):
    rolled = [pltpu.roll(t, 127, 1) for t in tiles]
    n = len(tiles)
    return [jnp.where(lane == 127, rolled[(j + 1) % n], rolled[j]) for j in range(n)]


def lane_prev(tiles, lane):
    rolled = [pltpu.roll(t, 1, 1) for t in tiles]
    return [jnp.where(lane == 0, rolled[j - 1], rolled[j]) for j in range(len(tiles))]


def kernel(
    dims,
    state,
    velocity,
    limiter,
    sigma,
    prior,
    owner,
    slot,
    fresh,
    out_phi,
    foot,
    grid,
    flags,
    left_x,
    right_x,
    face_x,
    face_y,
    face_before,
    blocks_to,
    block_at,
    look_at,
    look_up_at,
    packs,
    edges,
    corners,
    packs_o,
    edges_o,
    shell,
    weights,
    dense_sib,
    dense_own,
    got_sib,
    got_x,
    z_part,
    got_z,
    table,
    look_sem,
    load_sem,
    send_sem,
    recv_sem,
):
    zs, xs, secs, blks, nq, cx, cy, lat, lon = dims
    nj = cy // 128
    sb = lat * lon // 128
    me = lax.axis_index("sec")
    col = lax.axis_index("blk")
    core = lax.rem(me, CORES)
    at_x = lax.rem(lax.div(me, CORES), xs)
    at_z = lax.div(me, CORES * xs)

    def sec_of(z, x, c):
        return (z * xs + x) * CORES + c

    up, down = lax.rem(me + secs - 1, secs), lax.rem(me + 1, secs)
    left, right = lax.rem(col + blks - 1, blks), lax.rem(col + 1, blks)
    sibling = (me + 1 - 2 * core, col)
    x_peer = {d: (sec_of(at_z, lax.rem(at_x + d, xs), core), col) for d in range(1, xs)}
    z_peer = {d: (sec_of(lax.rem(at_z + d, zs), at_x, core), col) for d in range(1, zs)}
    compass = {
        (-1, 0): (up, col),
        (1, 0): (down, col),
        (0, -1): (me, left),
        (0, 1): (me, right),
        (-1, -1): (up, left),
        (-1, 1): (up, right),
        (1, -1): (down, left),
        (1, 1): (down, right),
    }

    used = [0]
    sent = []

    def send(src, dst, device):
        n = used[0]
        used[0] += 1
        copy = pltpu.make_async_remote_copy(
            src_ref=src,
            dst_ref=dst,
            send_sem=send_sem.at[n],
            recv_sem=recv_sem.at[n],
            device_id=device,
            device_id_type=MESH,
        )
        copy.start()
        sent.append(copy)
        return copy

    barrier = pltpu.get_barrier_semaphore()
    partners = [*compass.values(), *x_peer.values(), *z_peer.values(), sibling]
    for device in partners:
        pl.semaphore_signal(barrier, inc=1, device_id=device, device_id_type=MESH)

    loads = {}

    def load(name, src, dst):
        copy = pltpu.make_async_copy(src, dst, load_sem.at[len(loads)])
        copy.start()
        loads[name] = copy

    mid = slice(TOP, TOP + cx)
    for j in range(nj):
        lanes = slice(128 * j, 128 * j + 128)
        load(("f", j), state.at[nq - 2 : nq, :, lanes], grid.at[nq - 2 : nq, j, mid, :])
        load(("v", j), velocity.at[:, :, lanes], grid.at[nq : nq + 2, j, mid, :])
        load(("l", j), limiter.at[:, lanes], flags.at[j])
    load("owner", owner, blocks_to.at[0])
    load("slot", slot, blocks_to.at[1])
    load("sigma", sigma, shell.at[0, 8 : 8 + lat, 128 : 128 + lon])
    load("prior", prior, shell.at[1, 8 : 8 + lat, 128 : 128 + lon])
    for j in range(nj):
        lanes = slice(128 * j, 128 * j + 128)
        load(("o", j), state.at[: nq - 2, :, lanes], grid.at[: nq - 2, j, mid, :])

    for j in range(nj):
        for name in ("f", "v", "l"):
            loads[(name, j)].wait()
    for j in range(nj):
        grid[nq + 2, j, mid, :] = 0.5 * flags[j].astype(jnp.float32)
    first = nq - 2
    fields = slice(first, first + 5)
    top, bottom = slice(TOP, TOP + 8), slice(TOP + cx - 8, TOP + cx)
    above, below = slice(TOP - 8, TOP), slice(TOP + cx, TOP + cx + 8)
    rows = cx // GROUPS
    wide = lax.broadcasted_iota(jnp.int32, (rows, 128), 1)

    def pack(base, count, width):
        at_left = jnp.zeros((rows, 128), jnp.float32)
        at_right = jnp.zeros((rows, 128), jnp.float32)
        for g in range(GROUPS):
            here = slice(TOP + g * rows, TOP + (g + 1) * rows)
            for a in range(count):
                at = 16 * g + width * a
                mask = (wide >= at) & (wide < at + width)
                at_left = jnp.where(mask, pltpu.roll(grid[base + a, 0, here, :], at, 1), at_left)
                moved = pltpu.roll(grid[base + a, nj - 1, here, :], (at + width) % 128, 1)
                at_right = jnp.where(mask, moved, at_right)
        return at_left, at_right

    def unpack(base, count, width, from_left, from_right, take, put, size, group):
        side = lax.broadcasted_iota(jnp.int32, (size, 128), 1) < 64
        for a in range(count):
            at = 16 * group + width * a
            r = pltpu.roll(from_right[take, :], (128 - at) % 128, 1)
            l = pltpu.roll(from_left[take, :], (256 - width - at) % 128, 1)
            grid[base + a, nj, put, :] = jnp.where(side, r, l)

    to_left, to_right = pack(first, 5, 3)
    packs[0] = to_left
    packs[1] = to_right
    pl.semaphore_wait(barrier, len(partners))
    halo = []
    halo.append(send(grid.at[fields, 0:nj, bottom, :], grid.at[fields, 0:nj, above, :], (down, col)))
    halo.append(send(grid.at[fields, 0:nj, top, :], grid.at[fields, 0:nj, below, :], (up, col)))
    halo.append(send(packs.at[1], edges.at[0], (me, right)))
    halo.append(send(packs.at[0], edges.at[1], (me, left)))
    halo.append(send(packs.at[1, rows - 8 : rows, :], corners.at[0], (down, right)))
    halo.append(send(packs.at[0, rows - 8 : rows, :], corners.at[1], (down, left)))
    halo.append(send(packs.at[1, 0:8, :], corners.at[2], (up, right)))
    halo.append(send(packs.at[0, 0:8, :], corners.at[3], (up, left)))

    row_src = {0: slice(8, 8 + lat), 1: slice(lat, lat + 8), -1: slice(8, 16)}
    row_dst = {0: slice(8, 8 + lat), 1: slice(0, 8), -1: slice(8 + lat, 16 + lat)}
    lane_src = {0: slice(128, 128 + lon), 1: slice(lon, lon + 128), -1: slice(128, 256)}
    lane_dst = {0: slice(128, 128 + lon), 1: slice(0, 128), -1: slice(128 + lon, 256 + lon)}

    def shell_halo(which):
        return [
            send(
                shell.at[which, row_src[dr], lane_src[dc]],
                shell.at[which, row_dst[dr], lane_dst[dc]],
                device,
            )
            for (dr, dc), device in compass.items()
        ]

    loads["sigma"].wait()
    loads["prior"].wait()
    shell_copies = shell_halo(slice(0, 2))

    per_row = lon // 128
    loads["owner"].wait()
    loads["slot"].wait()
    at_owner, at_slot = blocks_to[0], blocks_to[1]
    look_at[...] = at_owner * sb + at_slot
    look_load = pltpu.make_async_copy(look_at, look_up_at, look_sem)
    look_load.start()
    ordered = (
        ((at_owner % CORES) * zs + at_owner // (CORES * xs)) * xs + (at_owner // CORES) % xs
    ) * sb
    ordered = ordered + (at_slot % per_row) * lat + at_slot // per_row
    to_lane = lax.broadcasted_iota(jnp.int32, (128, 128), 1)
    from_lane = lax.broadcasted_iota(jnp.int32, (128, 128), 0)
    each = 128 // nj
    moved = ((from_lane % nj) * each + from_lane // nj == to_lane).astype(jnp.float32)

    def move(a):
        return jnp.dot(a.astype(jnp.float32), moved, preferred_element_type=jnp.float32).astype(jnp.int32)

    block_at[...] = move(ordered // 64) * 64 + move(ordered % 64)

    for j in range(nj):
        loads[("o", j)].wait()
    others = slice(0, nq - 2)
    halo_o = [
        send(grid.at[others, 0:nj, bottom, :], grid.at[others, 0:nj, above, :], (down, col)),
        send(grid.at[others, 0:nj, top, :], grid.at[others, 0:nj, below, :], (up, col)),
    ]
    to_left, to_right = pack(0, nq - 2, 2)
    packs_o[0] = to_left
    packs_o[1] = to_right
    halo_o.append(send(packs_o.at[1], edges_o.at[0], (me, right)))
    halo_o.append(send(packs_o.at[0], edges_o.at[1], (me, left)))

    for copy in halo:
        copy.wait_recv()
    for g in range(GROUPS):
        here = slice(TOP + g * rows, TOP + (g + 1) * rows)
        unpack(first, 5, 3, edges.at[0], edges.at[1], slice(0, rows), here, rows, g)
    unpack(first, 5, 3, corners.at[0], corners.at[1], slice(0, 8), above, 8, GROUPS - 1)
    unpack(first, 5, 3, corners.at[2], corners.at[3], slice(0, 8), below, 8, 0)

    around_rows = cx + 16
    ring = slice(TOP - 8, TOP + cx + 8)
    lane_r = lax.broadcasted_iota(jnp.int32, (around_rows, 128), 1)
    speed_y = [grid[nq + 1, j, ring, :] for j in range(nj + 1)]
    faces_y = [0.2 * (here + after) for here, after in zip(speed_y, lane_next(speed_y, lane_r))]
    faces_before = lane_prev(faces_y, lane_r)
    for j in range(nj + 1):
        face_y[j, ring, :] = faces_y[j]
        face_before[j, ring, :] = faces_before[j]
        face_x[j, ring, :] = 0.2 * (grid[nq, j, ring, :] + grid[nq, j, TOP - 7 : TOP + cx + 9, :])

    def advect(q, tiles_x, start, high):
        lane_h = lax.broadcasted_iota(jnp.int32, (high, 128), 1)
        deep = 16

        def along_x(k, carry):
            b = pl.multiple_of(TOP - 8 + deep * k, 8)
            for j in range(tiles_x):
                here = grid[q, j, pl.ds(b, deep), :]
                lower = here - grid[q, j, pl.ds(b - 1, deep), :]
                upper = grid[q, j, pl.ds(b + 1, deep), :] - here
                half = minmod(lower, upper) * grid[nq + 2, j, pl.ds(b, deep), :]
                left_x[j, pl.ds(b, deep), :] = here + half
                right_x[j, pl.ds(b, deep), :] = here - half
            return carry

        lax.fori_loop(0, (cx + 16) // deep, along_x, 0)
        at, above, below = (slice(start + n, start + n + high) for n in (0, -1, 1))
        here = [grid[q, j, at, :] for j in range(nj + 1)]
        nexts, befores = lane_next(here, lane_h), lane_prev(here, lane_h)
        half = [
            minmod(h - before, after - h) * grid[nq + 2, j, at, :]
            for j, (h, before, after) in enumerate(zip(here, befores, nexts))
        ]
        left_y = [h + m for h, m in zip(here, half)]
        right_y = [h - m for h, m in zip(here, half)]
        right_next, left_before = lane_next(right_y, lane_h), lane_prev(left_y, lane_h)
        for j in range(tiles_x):
            speed = face_y[j, at, :]
            flux_y = speed * jnp.where(speed > 0.0, left_y[j], right_next[j])
            speed = face_before[j, at, :]
            flux_before = speed * jnp.where(speed > 0.0, left_before[j], right_y[j])
            speed = face_x[j, at, :]
            flux_x = speed * jnp.where(speed > 0.0, left_x[j, at, :], right_x[j, below, :])
            speed = face_x[j, above, :]
            flux_above = speed * jnp.where(speed > 0.0, left_x[j, above, :], right_x[j, at, :])
            fresh[q, j, at, :] = here[j] - ((flux_x - flux_above) + (flux_y - flux_before))

    def field(q, carry):
        advect(q, nj + 1, TOP - 8, cx + 16)
        return carry

    lax.fori_loop(nq - 2, nq, field, 0)
    lane_c = lax.broadcasted_iota(jnp.int32, (cx, 128), 1)
    field_x = [fresh[nq - 2, j, mid, :] for j in range(nj + 1)]
    after, before = lane_next(field_x, lane_c), lane_prev(field_x, lane_c)
    for j in range(nj):
        current = 0.5 * (
            fresh[nq - 1, j, TOP + 1 : TOP + cx + 1, :] - fresh[nq - 1, j, TOP - 1 : TOP + cx - 1, :]
        ) - 0.5 * (after[j] - before[j])
        high = current.astype(jnp.bfloat16)
        low = (current - high.astype(jnp.float32)).astype(jnp.bfloat16)
        for k in range(cx // each):
            part = slice((k * nj + j) * each, (k * nj + j + 1) * each)
            weights[part, 0:128] = high[k * each : (k + 1) * each, :]
            weights[part, 128:256] = low[k * each : (k + 1) * each, :]

    order = sorted(range(zs), key=lambda d: -min(d, zs - d))
    duos = [order[n : n + 2] for n in range(0, zs, 2)]
    per_z = xs * sb
    groups = nj * cx // 128

    def sums(duo, to_core):
        ids = jnp.concatenate(
            [
                lax.broadcasted_iota(jnp.int32, (per_z, 128), 0)
                + (to_core * zs + lax.rem(at_z + d, zs)) * per_z
                for d in duo
            ],
            axis=0,
        )
        chosen = [
            jnp.where(ids == block_at[k : k + 1, :], 1.0, 0.0).astype(jnp.bfloat16)
            for k in range(groups)
        ]
        both = jnp.dot(
            jnp.concatenate(chosen, axis=1), weights[...], preferred_element_type=jnp.float32
        )
        return (both[:, :128] + both[:, 128:]).reshape(2, xs, sb, 128)

    sib_copies, x_copies, z_copies = {}, {}, {}
    order_x = sorted(x_peer, key=lambda d: -min(d, xs - d))

    def for_sibling(n):
        dense_sib[n] = sums(duos[n], 1 - core)
        sib_copies[n] = send(dense_sib.at[n], got_sib.at[n], sibling)

    def for_own(n):
        dense_own[n] = sums(duos[n], core)
        sib_copies[n].wait_recv()
        dense_own[n] = dense_own[n] + got_sib[n]
        last = n == len(duos) - 1
        for h in (slice(0, 1), slice(1, 2)) if last else (slice(0, 2),):
            for d in order_x:
                part = dense_own.at[n, h, lax.rem(at_x + d, xs)]
                copy = send(part, got_x.at[n, d - 1, h], x_peer[d])
                x_copies.setdefault((n, h.start), []).append(copy)

    for_sibling(0)
    for n in range(len(duos)):
        if n + 1 < len(duos):
            for_sibling(n + 1)
        for_own(n)
    for copy in halo_o:
        copy.wait_recv()
    for g in range(GROUPS):
        here = slice(TOP + g * rows, TOP + (g + 1) * rows)
        unpack(0, nq - 2, 2, edges_o.at[0], edges_o.at[1], slice(0, rows), here, rows, g)

    def other(q, carry):
        advect(q, nj, TOP, cx)
        return carry

    def along_z(n):
        for h, d in enumerate(duos[n]):
            for copy in x_copies.get((n, h), []):
                copy.wait_recv()
            part = dense_own[n, h, at_x]
            for e in x_peer:
                part = part + got_x[n, e - 1, h]
            z_part[n, h] = part
            if d:
                z_copies[d] = send(z_part.at[n, h], got_z.at[d - 1], z_peer[d])

    lax.fori_loop(0, nq - 2, other, 0)
    for n in range(len(duos)):
        along_z(n)
    source = z_part[len(duos) - 1, 1]
    for d in order[:-1]:
        z_copies[d].wait_recv()
        source = source + got_z[d - 1]
    for c in range(lon // 128):
        at = 128 + 128 * c
        shell[2, 8 : 8 + lat, at : at + 128] = source[c * lat : (c + 1) * lat, :]
    source_copies = shell_halo(slice(2, 3))

    for copy in shell_copies:
        copy.wait_recv()
    shape = (lat + 16, lon + 256)
    lat_at = lax.broadcasted_iota(jnp.int32, shape, 0) + (me * lat - 8)
    lon_at = lax.broadcasted_iota(jnp.int32, shape, 1) + (col * lon - 128)
    inside = (lat_at >= 0) & (lat_at < secs * lat) & (lon_at >= 0) & (lon_at < blks * lon)
    sig = jnp.where(inside, shell[0], 0.0)
    phi = jnp.where(inside, shell[1], 0.0)

    def around(a):
        return (
            pltpu.roll(a, 1, 0),
            pltpu.roll(a, lat + 15, 0),
            pltpu.roll(a, 1, 1),
            pltpu.roll(a, lon + 255, 1),
        )

    ways = [0.5 * (sig + other_sig) for other_sig in around(sig)]
    inverse = 1.0 / (ways[0] + ways[1] + ways[2] + ways[3] + 1.0)
    for copy in source_copies:
        copy.wait_recv()
    src = shell[2]
    for _ in range(ITERS):
        n, s, w, e = around(phi)
        total = ways[0] * n + ways[1] * s + ways[2] * w + ways[3] * e + src
        phi = jnp.where(inside, total * inverse, 0.0)
    phi = phi[8 : 8 + lat, 128 : 128 + lon]
    out_phi[...] = phi

    split = sb // 8 * 7

    def piece(z, x, start=0, size=sb):
        at = sec_of(z, x, core) * sb + start
        return table.at[pl.ds(pl.multiple_of(at, 8), size), :]

    mine = pl.multiple_of(me * sb, sb)
    for c in range(per_row):
        table[pl.ds(mine + c, lat, stride=per_row), :] = phi[:, c * 128 : (c + 1) * 128]

    from_z, from_x, first_rows, last_rows, from_sib = {}, {}, {}, {}, []
    own = piece(at_z, at_x)
    nearest = sorted(range(1, zs), key=lambda d: min(d, zs - d))
    for d in nearest[:2]:
        from_z[d] = send(own, own, z_peer[d])
    for d in order_x:
        from_x[d] = send(own, own, x_peer[d])
    for d in nearest[2:]:
        from_z[d] = send(own, own, z_peer[d])

    def share(part):
        from_sib.append(send(part, part, sibling))

    def z_back(d):
        return lax.rem(at_z + zs - d, zs)

    def x_back(d):
        return lax.rem(at_x + xs - d, xs)

    share(own)

    def along_x(d):
        from_z[d].wait_recv()
        part = piece(z_back(d), at_x, 0, split)
        for e in order_x:
            first_rows[d, e] = send(part, part, x_peer[e])
        share(piece(z_back(d), at_x))

    for d in nearest[:2]:
        along_x(d)
    for e in order_x[::-1]:
        from_x[e].wait_recv()
        part = piece(at_z, x_back(e), split, sb - split)
        for d in nearest[::-1]:
            last_rows[d, e] = send(part, part, z_peer[d])
        share(piece(at_z, x_back(e)))
    for d in nearest[2:]:
        along_x(d)
    for d in nearest:
        for e in order_x:
            first_rows[d, e].wait_recv()
            last_rows[d, e].wait_recv()
            share(piece(z_back(d), x_back(e)))
    for copy in from_sib:
        copy.wait_recv()
    look_load.wait()

    def look_up(k, carry):
        b = pl.multiple_of(2 * each * k, 8)
        for n in range(2):
            for r in range(each):
                for j in range(nj):
                    at = look_up_at[2 * k + n, r * nj + j]
                    foot[j, pl.ds(b + n * each + r, 1), :] = table[pl.ds(at, 1), :]
        return carry

    lax.fori_loop(0, cx // (2 * each), look_up, 0)
    for copy in sent:
        copy.wait_send()


def write_out(fresh, phi, foot, out_state, out_phi, out_foot, sem):
    cx = foot.shape[1]
    copies = [pltpu.make_async_copy(phi, out_phi, sem.at[0])]
    for j in range(foot.shape[0]):
        lanes = slice(128 * j, 128 * j + 128)
        mid = fresh.at[:, j, TOP : TOP + cx, :]
        copies.append(pltpu.make_async_copy(mid, out_state.at[:, :, lanes], sem.at[2 * j + 1]))
        copies.append(pltpu.make_async_copy(foot.at[j], out_foot.at[:, lanes], sem.at[2 * j + 2]))
    for copy in copies:
        copy.start()
    for copy in copies:
        copy.wait()


def on_device(
    state, velocity, limiter, footpoint_owner, footpoint_slot, conductance, potential_prior
):
    secs, blks = lax.axis_size("sec"), lax.axis_size("blk")
    xs = 4 if secs % 16 == 0 else 2
    zs = secs // (CORES * xs)
    nq, cx, cy = state.shape
    lat, lon = conductance.shape
    nj = cy // 128
    sb = lat * lon // 128
    blocks = nj * cx
    owner = footpoint_owner.reshape(blocks // 128, 128)
    slot = footpoint_slot.reshape(blocks // 128, 128)
    dims = (zs, xs, secs, blks, nq, cx, cy, lat, lon)
    f32 = jnp.float32
    rows = cx // GROUPS
    messages = 12 + 8 + 8 + zs // 2 + zs // 2 * (xs - 1) + (xs - 1) + 2 * (zs - 1) + (xs - 1) + 2 * (zs - 1) * (xs - 1) + zs * xs
    any_space = pl.BlockSpec(memory_space=pl.ANY)
    vmem = pl.BlockSpec(memory_space=pltpu.VMEM)

    def body(*refs):
        kernel(dims, *refs)

    results = pl.pallas_call(
        body,
        out_shape=(
            pltpu.VMEM((nq, nj + 1, cx + PAD, 128), f32),
            pltpu.VMEM(conductance.shape, f32),
            pltpu.VMEM((nj, cx, 128), f32),
        ),
        in_specs=[pl.BlockSpec(memory_space=pltpu.HBM)] * 7,
        out_specs=(vmem, vmem, vmem),
        scratch_shapes=[
            pltpu.VMEM((nq + 3, nj + 1, cx + PAD, 128), f32),
            pltpu.VMEM((nj, cx, 128), jnp.int32),
            pltpu.VMEM((nj + 1, cx + PAD, 128), f32),
            pltpu.VMEM((nj + 1, cx + PAD, 128), f32),
            pltpu.VMEM((nj + 1, cx + PAD, 128), f32),
            pltpu.VMEM((nj + 1, cx + PAD, 128), f32),
            pltpu.VMEM((nj + 1, cx + PAD, 128), f32),
            pltpu.VMEM((2, blocks // 128, 128), jnp.int32),
            pltpu.VMEM((blocks // 128, 128), jnp.int32),
            pltpu.VMEM((blocks // 128, 128), jnp.int32),
            pltpu.SMEM((blocks // 128, 128), jnp.int32),
            pltpu.VMEM((2, rows, 128), f32),
            pltpu.VMEM((2, rows, 128), f32),
            pltpu.VMEM((4, 8, 128), f32),
            pltpu.VMEM((2, rows, 128), f32),
            pltpu.VMEM((2, rows, 128), f32),
            pltpu.VMEM((3, lat + 16, lon + 256), f32),
            pltpu.VMEM((blocks, 256), jnp.bfloat16),
            pltpu.VMEM((zs // 2, 2, xs, sb, 128), f32),
            pltpu.VMEM((zs // 2, 2, xs, sb, 128), f32),
            pltpu.VMEM((zs // 2, 2, xs, sb, 128), f32),
            pltpu.VMEM((zs // 2, xs - 1, 2, sb, 128), f32),
            pltpu.VMEM((zs // 2, 2, sb, 128), f32),
            pltpu.VMEM((zs - 1, sb, 128), f32),
            pltpu.VMEM((secs * sb, 128), f32),
            pltpu.SemaphoreType.DMA(()),
            pltpu.SemaphoreType.DMA((4 * nj + 4,)),
            pltpu.SemaphoreType.DMA((messages,)),
            pltpu.SemaphoreType.DMA((messages,)),
        ],
        compiler_params=pltpu.CompilerParams(
            collective_id=0, has_side_effects=True, vmem_limit_bytes=40 * 1024 * 1024
        ),
    )(
        *[
            pltpu.with_memory_space_constraint(a, pltpu.HBM)
            for a in (state, velocity, limiter, conductance, potential_prior, owner, slot)
        ],
    )
    return pl.pallas_call(
        write_out,
        out_shape=(
            jax.ShapeDtypeStruct(state.shape, f32),
            jax.ShapeDtypeStruct(conductance.shape, f32),
            jax.ShapeDtypeStruct((cx, cy), f32),
        ),
        in_specs=[vmem] * 3,
        out_specs=(any_space,) * 3,
        scratch_shapes=[pltpu.SemaphoreType.DMA((2 * nj + 1,))],
        compiler_params=pltpu.CompilerParams(vmem_limit_bytes=16 * 1024 * 1024),
    )(*[pltpu.with_memory_space_constraint(r, pltpu.VMEM) for r in results])


def solution(mesh):
    in_specs = (
        P(None, "sec", "blk"),
        P(None, "sec", "blk"),
        P("sec", "blk"),
        P("sec", "blk", None, None),
        P("sec", "blk", None, None),
        P("sec", "blk"),
        P("sec", "blk"),
    )
    out_specs = (P(None, "sec", "blk"), P("sec", "blk"), P("sec", "blk"))
    return jax.shard_map(
        on_device, mesh=mesh, in_specs=in_specs, out_specs=out_specs, check_vma=False
    )
```

```python
import jax
import jax.numpy as jnp
from jax import lax
from jax.experimental import pallas as pl
from jax.experimental.pallas import tpu as pltpu
from jax.sharding import PartitionSpec as P

ITERS = 4
CORES = 2
TOP = 16
PAD = 40
GROUPS = 8
MESH = pl.DeviceIdType.MESH


def minmod(a, b):
    return jnp.maximum(jnp.minimum(a, b), jnp.minimum(jnp.maximum(a, b), 0.0))


def lane_next(tiles, lane):
    rolled = [pltpu.roll(t, 127, 1) for t in tiles]
    n = len(tiles)
    return [jnp.where(lane == 127, rolled[(j + 1) % n], rolled[j]) for j in range(n)]


def lane_prev(tiles, lane):
    rolled = [pltpu.roll(t, 1, 1) for t in tiles]
    return [jnp.where(lane == 0, rolled[j - 1], rolled[j]) for j in range(len(tiles))]


def kernel(
    dims,
    state,
    velocity,
    limiter,
    sigma,
    prior,
    owner,
    slot,
    fresh,
    out_phi,
    foot,
    grid,
    flags,
    left_x,
    right_x,
    face_x,
    face_y,
    face_before,
    blocks_to,
    block_at,
    look_at,
    look_up_at,
    packs,
    edges,
    corners,
    packs_o,
    edges_o,
    shell,
    weights,
    dense_sib,
    dense_own,
    got_sib,
    got_x,
    z_part,
    got_z,
    table,
    look_sem,
    load_sem,
    send_sem,
    recv_sem,
):
    zs, xs, secs, blks, nq, cx, cy, lat, lon = dims
    nj = cy // 128
    sb = lat * lon // 128
    me = lax.axis_index("sec")
    col = lax.axis_index("blk")
    core = lax.rem(me, CORES)
    at_x = lax.rem(lax.div(me, CORES), xs)
    at_z = lax.div(me, CORES * xs)

    def sec_of(z, x, c):
        return (z * xs + x) * CORES + c

    up, down = lax.rem(me + secs - 1, secs), lax.rem(me + 1, secs)
    left, right = lax.rem(col + blks - 1, blks), lax.rem(col + 1, blks)
    sibling = (me + 1 - 2 * core, col)
    x_peer = {d: (sec_of(at_z, lax.rem(at_x + d, xs), core), col) for d in range(1, xs)}
    z_peer = {d: (sec_of(lax.rem(at_z + d, zs), at_x, core), col) for d in range(1, zs)}
    compass = {
        (-1, 0): (up, col),
        (1, 0): (down, col),
        (0, -1): (me, left),
        (0, 1): (me, right),
        (-1, -1): (up, left),
        (-1, 1): (up, right),
        (1, -1): (down, left),
        (1, 1): (down, right),
    }

    used = [0]
    sent = []

    def send(src, dst, device):
        n = used[0]
        used[0] += 1
        copy = pltpu.make_async_remote_copy(
            src_ref=src,
            dst_ref=dst,
            send_sem=send_sem.at[n],
            recv_sem=recv_sem.at[n],
            device_id=device,
            device_id_type=MESH,
        )
        copy.start()
        sent.append(copy)
        return copy

    barrier = pltpu.get_barrier_semaphore()
    partners = [*compass.values(), *x_peer.values(), *z_peer.values(), sibling]
    for device in partners:
        pl.semaphore_signal(barrier, inc=1, device_id=device, device_id_type=MESH)

    loads = {}

    def load(name, src, dst):
        copy = pltpu.make_async_copy(src, dst, load_sem.at[len(loads)])
        copy.start()
        loads[name] = copy

    mid = slice(TOP, TOP + cx)
    for j in range(nj):
        lanes = slice(128 * j, 128 * j + 128)
        load(("f", j), state.at[nq - 2 : nq, :, lanes], grid.at[nq - 2 : nq, j, mid, :])
        load(("v", j), velocity.at[:, :, lanes], grid.at[nq : nq + 2, j, mid, :])
        load(("l", j), limiter.at[:, lanes], flags.at[j])
    load("owner", owner, blocks_to.at[0])
    load("slot", slot, blocks_to.at[1])
    load("sigma", sigma, shell.at[0, 8 : 8 + lat, 128 : 128 + lon])
    load("prior", prior, shell.at[1, 8 : 8 + lat, 128 : 128 + lon])
    for j in range(nj):
        lanes = slice(128 * j, 128 * j + 128)
        load(("o", j), state.at[: nq - 2, :, lanes], grid.at[: nq - 2, j, mid, :])

    for j in range(nj):
        for name in ("f", "v", "l"):
            loads[(name, j)].wait()
    for j in range(nj):
        grid[nq + 2, j, mid, :] = 0.5 * flags[j].astype(jnp.float32)
    first = nq - 2
    fields = slice(first, first + 5)
    top, bottom = slice(TOP, TOP + 8), slice(TOP + cx - 8, TOP + cx)
    above, below = slice(TOP - 8, TOP), slice(TOP + cx, TOP + cx + 8)
    rows = cx // GROUPS
    wide = lax.broadcasted_iota(jnp.int32, (rows, 128), 1)

    def pack(base, count, width):
        at_left = jnp.zeros((rows, 128), jnp.float32)
        at_right = jnp.zeros((rows, 128), jnp.float32)
        for g in range(GROUPS):
            here = slice(TOP + g * rows, TOP + (g + 1) * rows)
            for a in range(count):
                at = 16 * g + width * a
                mask = (wide >= at) & (wide < at + width)
                at_left = jnp.where(mask, pltpu.roll(grid[base + a, 0, here, :], at, 1), at_left)
                moved = pltpu.roll(grid[base + a, nj - 1, here, :], (at + width) % 128, 1)
                at_right = jnp.where(mask, moved, at_right)
        return at_left, at_right

    def unpack(base, count, width, from_left, from_right, take, put, size, group):
        side = lax.broadcasted_iota(jnp.int32, (size, 128), 1) < 64
        for a in range(count):
            at = 16 * group + width * a
            r = pltpu.roll(from_right[take, :], (128 - at) % 128, 1)
            l = pltpu.roll(from_left[take, :], (256 - width - at) % 128, 1)
            grid[base + a, nj, put, :] = jnp.where(side, r, l)

    to_left, to_right = pack(first, 5, 3)
    packs[0] = to_left
    packs[1] = to_right
    pl.semaphore_wait(barrier, len(partners))
    halo = []
    halo.append(send(grid.at[fields, 0:nj, bottom, :], grid.at[fields, 0:nj, above, :], (down, col)))
    halo.append(send(grid.at[fields, 0:nj, top, :], grid.at[fields, 0:nj, below, :], (up, col)))
    halo.append(send(packs.at[1], edges.at[0], (me, right)))
    halo.append(send(packs.at[0], edges.at[1], (me, left)))
    halo.append(send(packs.at[1, rows - 8 : rows, :], corners.at[0], (down, right)))
    halo.append(send(packs.at[0, rows - 8 : rows, :], corners.at[1], (down, left)))
    halo.append(send(packs.at[1, 0:8, :], corners.at[2], (up, right)))
    halo.append(send(packs.at[0, 0:8, :], corners.at[3], (up, left)))

    row_src = {0: slice(8, 8 + lat), 1: slice(lat, lat + 8), -1: slice(8, 16)}
    row_dst = {0: slice(8, 8 + lat), 1: slice(0, 8), -1: slice(8 + lat, 16 + lat)}
    lane_src = {0: slice(128, 128 + lon), 1: slice(lon, lon + 128), -1: slice(128, 256)}
    lane_dst = {0: slice(128, 128 + lon), 1: slice(0, 128), -1: slice(128 + lon, 256 + lon)}

    def shell_halo(which):
        return [
            send(
                shell.at[which, row_src[dr], lane_src[dc]],
                shell.at[which, row_dst[dr], lane_dst[dc]],
                device,
            )
            for (dr, dc), device in compass.items()
        ]

    loads["sigma"].wait()
    loads["prior"].wait()
    shell_copies = shell_halo(slice(0, 2))

    per_row = lon // 128
    loads["owner"].wait()
    loads["slot"].wait()
    at_owner, at_slot = blocks_to[0], blocks_to[1]
    look_at[...] = at_owner * sb + at_slot
    look_load = pltpu.make_async_copy(look_at, look_up_at, look_sem)
    look_load.start()
    ordered = (
        ((at_owner % CORES) * zs + at_owner // (CORES * xs)) * xs + (at_owner // CORES) % xs
    ) * sb
    ordered = ordered + (at_slot % per_row) * lat + at_slot // per_row
    to_lane = lax.broadcasted_iota(jnp.int32, (128, 128), 1)
    from_lane = lax.broadcasted_iota(jnp.int32, (128, 128), 0)
    each = 128 // nj
    moved = ((from_lane % nj) * each + from_lane // nj == to_lane).astype(jnp.float32)

    def move(a):
        return jnp.dot(a.astype(jnp.float32), moved, preferred_element_type=jnp.float32).astype(jnp.int32)

    block_at[...] = move(ordered // 64) * 64 + move(ordered % 64)

    for j in range(nj):
        loads[("o", j)].wait()
    others = slice(0, nq - 2)
    halo_o = [
        send(grid.at[others, 0:nj, bottom, :], grid.at[others, 0:nj, above, :], (down, col)),
        send(grid.at[others, 0:nj, top, :], grid.at[others, 0:nj, below, :], (up, col)),
    ]
    to_left, to_right = pack(0, nq - 2, 2)
    packs_o[0] = to_left
    packs_o[1] = to_right
    halo_o.append(send(packs_o.at[1], edges_o.at[0], (me, right)))
    halo_o.append(send(packs_o.at[0], edges_o.at[1], (me, left)))

    for copy in halo:
        copy.wait_recv()
    for g in range(GROUPS):
        here = slice(TOP + g * rows, TOP + (g + 1) * rows)
        unpack(first, 5, 3, edges.at[0], edges.at[1], slice(0, rows), here, rows, g)
    unpack(first, 5, 3, corners.at[0], corners.at[1], slice(0, 8), above, 8, GROUPS - 1)
    unpack(first, 5, 3, corners.at[2], corners.at[3], slice(0, 8), below, 8, 0)

    around_rows = cx + 16
    ring = slice(TOP - 8, TOP + cx + 8)
    lane_r = lax.broadcasted_iota(jnp.int32, (around_rows, 128), 1)
    speed_y = [grid[nq + 1, j, ring, :] for j in range(nj + 1)]
    faces_y = [0.2 * (here + after) for here, after in zip(speed_y, lane_next(speed_y, lane_r))]
    faces_before = lane_prev(faces_y, lane_r)
    for j in range(nj + 1):
        face_y[j, ring, :] = faces_y[j]
        face_before[j, ring, :] = faces_before[j]
        face_x[j, ring, :] = 0.2 * (grid[nq, j, ring, :] + grid[nq, j, TOP - 7 : TOP + cx + 9, :])

    def advect(q, tiles_x, start, high):
        lane_h = lax.broadcasted_iota(jnp.int32, (high, 128), 1)
        deep = 16

        def along_x(k, carry):
            b = pl.multiple_of(TOP - 8 + deep * k, 8)
            for j in range(tiles_x):
                here = grid[q, j, pl.ds(b, deep), :]
                lower = here - grid[q, j, pl.ds(b - 1, deep), :]
                upper = grid[q, j, pl.ds(b + 1, deep), :] - here
                half = minmod(lower, upper) * grid[nq + 2, j, pl.ds(b, deep), :]
                left_x[j, pl.ds(b, deep), :] = here + half
                right_x[j, pl.ds(b, deep), :] = here - half
            return carry

        lax.fori_loop(0, (cx + 16) // deep, along_x, 0)
        at, above, below = (slice(start + n, start + n + high) for n in (0, -1, 1))
        here = [grid[q, j, at, :] for j in range(nj + 1)]
        nexts, befores = lane_next(here, lane_h), lane_prev(here, lane_h)
        half = [
            minmod(h - before, after - h) * grid[nq + 2, j, at, :]
            for j, (h, before, after) in enumerate(zip(here, befores, nexts))
        ]
        left_y = [h + m for h, m in zip(here, half)]
        right_y = [h - m for h, m in zip(here, half)]
        right_next, left_before = lane_next(right_y, lane_h), lane_prev(left_y, lane_h)
        for j in range(tiles_x):
            speed = face_y[j, at, :]
            flux_y = speed * jnp.where(speed > 0.0, left_y[j], right_next[j])
            speed = face_before[j, at, :]
            flux_before = speed * jnp.where(speed > 0.0, left_before[j], right_y[j])
            speed = face_x[j, at, :]
            flux_x = speed * jnp.where(speed > 0.0, left_x[j, at, :], right_x[j, below, :])
            speed = face_x[j, above, :]
            flux_above = speed * jnp.where(speed > 0.0, left_x[j, above, :], right_x[j, at, :])
            fresh[q, j, at, :] = here[j] - ((flux_x - flux_above) + (flux_y - flux_before))

    def field(q, carry):
        advect(q, nj + 1, TOP - 8, cx + 16)
        return carry

    lax.fori_loop(nq - 2, nq, field, 0)
    lane_c = lax.broadcasted_iota(jnp.int32, (cx, 128), 1)
    field_x = [fresh[nq - 2, j, mid, :] for j in range(nj + 1)]
    after, before = lane_next(field_x, lane_c), lane_prev(field_x, lane_c)
    for j in range(nj):
        current = 0.5 * (
            fresh[nq - 1, j, TOP + 1 : TOP + cx + 1, :] - fresh[nq - 1, j, TOP - 1 : TOP + cx - 1, :]
        ) - 0.5 * (after[j] - before[j])
        high = current.astype(jnp.bfloat16)
        low = (current - high.astype(jnp.float32)).astype(jnp.bfloat16)
        for k in range(cx // each):
            part = slice((k * nj + j) * each, (k * nj + j + 1) * each)
            weights[part, 0:128] = high[k * each : (k + 1) * each, :]
            weights[part, 128:256] = low[k * each : (k + 1) * each, :]

    order = sorted(range(zs), key=lambda d: -min(d, zs - d))
    duos = [order[n : n + 2] for n in range(0, zs, 2)]
    per_z = xs * sb
    groups = nj * cx // 128

    def sums(duo, to_core):
        ids = jnp.concatenate(
            [
                lax.broadcasted_iota(jnp.int32, (per_z, 128), 0)
                + (to_core * zs + lax.rem(at_z + d, zs)) * per_z
                for d in duo
            ],
            axis=0,
        )
        chosen = [
            jnp.where(ids == block_at[k : k + 1, :], 1.0, 0.0).astype(jnp.bfloat16)
            for k in range(groups)
        ]
        both = jnp.dot(
            jnp.concatenate(chosen, axis=1), weights[...], preferred_element_type=jnp.float32
        )
        return (both[:, :128] + both[:, 128:]).reshape(2, xs, sb, 128)

    sib_copies, x_copies, z_copies = {}, {}, {}
    order_x = sorted(x_peer, key=lambda d: -min(d, xs - d))

    def for_sibling(n):
        dense_sib[n] = sums(duos[n], 1 - core)
        sib_copies[n] = send(dense_sib.at[n], got_sib.at[n], sibling)

    def for_own(n):
        dense_own[n] = sums(duos[n], core)
        sib_copies[n].wait_recv()
        dense_own[n] = dense_own[n] + got_sib[n]
        last = n == len(duos) - 1
        for h in (slice(0, 1), slice(1, 2)) if last else (slice(0, 2),):
            for d in order_x:
                part = dense_own.at[n, h, lax.rem(at_x + d, xs)]
                copy = send(part, got_x.at[n, d - 1, h], x_peer[d])
                x_copies.setdefault((n, h.start), []).append(copy)

    for_sibling(0)
    for n in range(len(duos)):
        if n + 1 < len(duos):
            for_sibling(n + 1)
        for_own(n)
    for copy in halo_o:
        copy.wait_recv()
    for g in range(GROUPS):
        here = slice(TOP + g * rows, TOP + (g + 1) * rows)
        unpack(0, nq - 2, 2, edges_o.at[0], edges_o.at[1], slice(0, rows), here, rows, g)

    def other(q, carry):
        advect(q, nj, TOP, cx)
        return carry

    def along_z(n):
        for h, d in enumerate(duos[n]):
            for copy in x_copies.get((n, h), []):
                copy.wait_recv()
            part = dense_own[n, h, at_x]
            for e in x_peer:
                part = part + got_x[n, e - 1, h]
            z_part[n, h] = part
            if d:
                z_copies[d] = send(z_part.at[n, h], got_z.at[d - 1], z_peer[d])

    ahead = [nq - 6] + [1] * min(2, len(duos) - 1)
    done = 0
    for n in range(len(duos)):
        if n < len(ahead):
            lax.fori_loop(done, done + ahead[n], other, 0)
            done += ahead[n]
        along_z(n)
    lax.fori_loop(done, nq - 3, other, 0)
    source = z_part[len(duos) - 1, 1]
    for d in order[:-1]:
        z_copies[d].wait_recv()
        source = source + got_z[d - 1]
    for c in range(lon // 128):
        at = 128 + 128 * c
        shell[2, 8 : 8 + lat, at : at + 128] = source[c * lat : (c + 1) * lat, :]
    source_copies = shell_halo(slice(2, 3))
    lax.fori_loop(nq - 3, nq - 2, other, 0)

    for copy in shell_copies:
        copy.wait_recv()
    shape = (lat + 16, lon + 256)
    lat_at = lax.broadcasted_iota(jnp.int32, shape, 0) + (me * lat - 8)
    lon_at = lax.broadcasted_iota(jnp.int32, shape, 1) + (col * lon - 128)
    inside = (lat_at >= 0) & (lat_at < secs * lat) & (lon_at >= 0) & (lon_at < blks * lon)
    sig = jnp.where(inside, shell[0], 0.0)
    phi = jnp.where(inside, shell[1], 0.0)

    def around(a):
        return (
            pltpu.roll(a, 1, 0),
            pltpu.roll(a, lat + 15, 0),
            pltpu.roll(a, 1, 1),
            pltpu.roll(a, lon + 255, 1),
        )

    ways = [0.5 * (sig + other_sig) for other_sig in around(sig)]
    inverse = 1.0 / (ways[0] + ways[1] + ways[2] + ways[3] + 1.0)
    for copy in source_copies:
        copy.wait_recv()
    src = shell[2]
    for _ in range(ITERS):
        n, s, w, e = around(phi)
        total = ways[0] * n + ways[1] * s + ways[2] * w + ways[3] * e + src
        phi = jnp.where(inside, total * inverse, 0.0)
    phi = phi[8 : 8 + lat, 128 : 128 + lon]
    out_phi[...] = phi

    split = sb // 8 * 7

    def piece(z, x, start=0, size=sb):
        at = sec_of(z, x, core) * sb + start
        return table.at[pl.ds(pl.multiple_of(at, 8), size), :]

    mine = pl.multiple_of(me * sb, sb)
    for c in range(per_row):
        table[pl.ds(mine + c, lat, stride=per_row), :] = phi[:, c * 128 : (c + 1) * 128]

    from_z, from_x, first_rows, last_rows, from_sib = {}, {}, {}, {}, []
    own = piece(at_z, at_x)
    nearest = sorted(range(1, zs), key=lambda d: min(d, zs - d))
    for d in nearest[:2]:
        from_z[d] = send(own, own, z_peer[d])
    for d in order_x:
        from_x[d] = send(own, own, x_peer[d])
    for d in nearest[2:]:
        from_z[d] = send(own, own, z_peer[d])

    def share(part):
        from_sib.append(send(part, part, sibling))

    def z_back(d):
        return lax.rem(at_z + zs - d, zs)

    def x_back(d):
        return lax.rem(at_x + xs - d, xs)

    share(own)

    def along_x(d):
        from_z[d].wait_recv()
        part = piece(z_back(d), at_x, 0, split)
        for e in order_x:
            first_rows[d, e] = send(part, part, x_peer[e])
        share(piece(z_back(d), at_x))

    for d in nearest[:2]:
        along_x(d)
    for e in order_x[::-1]:
        from_x[e].wait_recv()
        part = piece(at_z, x_back(e), split, sb - split)
        for d in nearest[::-1]:
            last_rows[d, e] = send(part, part, z_peer[d])
        share(piece(at_z, x_back(e)))
    for d in nearest[2:]:
        along_x(d)
    for d in nearest:
        for e in order_x:
            first_rows[d, e].wait_recv()
            last_rows[d, e].wait_recv()
            share(piece(z_back(d), x_back(e)))
    for copy in from_sib:
        copy.wait_recv()
    look_load.wait()

    def look_up(k, carry):
        b = pl.multiple_of(2 * each * k, 8)
        for n in range(2):
            for r in range(each):
                for j in range(nj):
                    at = look_up_at[2 * k + n, r * nj + j]
                    foot[j, pl.ds(b + n * each + r, 1), :] = table[pl.ds(at, 1), :]
        return carry

    lax.fori_loop(0, cx // (2 * each), look_up, 0)
    for copy in sent:
        copy.wait_send()


def write_out(fresh, phi, foot, out_state, out_phi, out_foot, sem):
    cx = foot.shape[1]
    copies = [pltpu.make_async_copy(phi, out_phi, sem.at[0])]
    for j in range(foot.shape[0]):
        lanes = slice(128 * j, 128 * j + 128)
        mid = fresh.at[:, j, TOP : TOP + cx, :]
        copies.append(pltpu.make_async_copy(mid, out_state.at[:, :, lanes], sem.at[2 * j + 1]))
        copies.append(pltpu.make_async_copy(foot.at[j], out_foot.at[:, lanes], sem.at[2 * j + 2]))
    for copy in copies:
        copy.start()
    for copy in copies:
        copy.wait()


def on_device(
    state, velocity, limiter, footpoint_owner, footpoint_slot, conductance, potential_prior
):
    secs, blks = lax.axis_size("sec"), lax.axis_size("blk")
    xs = 4 if secs % 16 == 0 else 2
    zs = secs // (CORES * xs)
    nq, cx, cy = state.shape
    lat, lon = conductance.shape
    nj = cy // 128
    sb = lat * lon // 128
    blocks = nj * cx
    owner = footpoint_owner.reshape(blocks // 128, 128)
    slot = footpoint_slot.reshape(blocks // 128, 128)
    dims = (zs, xs, secs, blks, nq, cx, cy, lat, lon)
    f32 = jnp.float32
    rows = cx // GROUPS
    messages = 12 + 8 + 8 + zs // 2 + zs // 2 * (xs - 1) + (xs - 1) + 2 * (zs - 1) + (xs - 1) + 2 * (zs - 1) * (xs - 1) + zs * xs
    any_space = pl.BlockSpec(memory_space=pl.ANY)
    vmem = pl.BlockSpec(memory_space=pltpu.VMEM)

    def body(*refs):
        kernel(dims, *refs)

    results = pl.pallas_call(
        body,
        out_shape=(
            pltpu.VMEM((nq, nj + 1, cx + PAD, 128), f32),
            pltpu.VMEM(conductance.shape, f32),
            pltpu.VMEM((nj, cx, 128), f32),
        ),
        in_specs=[pl.BlockSpec(memory_space=pltpu.HBM)] * 7,
        out_specs=(vmem, vmem, vmem),
        scratch_shapes=[
            pltpu.VMEM((nq + 3, nj + 1, cx + PAD, 128), f32),
            pltpu.VMEM((nj, cx, 128), jnp.int32),
            pltpu.VMEM((nj + 1, cx + PAD, 128), f32),
            pltpu.VMEM((nj + 1, cx + PAD, 128), f32),
            pltpu.VMEM((nj + 1, cx + PAD, 128), f32),
            pltpu.VMEM((nj + 1, cx + PAD, 128), f32),
            pltpu.VMEM((nj + 1, cx + PAD, 128), f32),
            pltpu.VMEM((2, blocks // 128, 128), jnp.int32),
            pltpu.VMEM((blocks // 128, 128), jnp.int32),
            pltpu.VMEM((blocks // 128, 128), jnp.int32),
            pltpu.SMEM((blocks // 128, 128), jnp.int32),
            pltpu.VMEM((2, rows, 128), f32),
            pltpu.VMEM((2, rows, 128), f32),
            pltpu.VMEM((4, 8, 128), f32),
            pltpu.VMEM((2, rows, 128), f32),
            pltpu.VMEM((2, rows, 128), f32),
            pltpu.VMEM((3, lat + 16, lon + 256), f32),
            pltpu.VMEM((blocks, 256), jnp.bfloat16),
            pltpu.VMEM((zs // 2, 2, xs, sb, 128), f32),
            pltpu.VMEM((zs // 2, 2, xs, sb, 128), f32),
            pltpu.VMEM((zs // 2, 2, xs, sb, 128), f32),
            pltpu.VMEM((zs // 2, xs - 1, 2, sb, 128), f32),
            pltpu.VMEM((zs // 2, 2, sb, 128), f32),
            pltpu.VMEM((zs - 1, sb, 128), f32),
            pltpu.VMEM((secs * sb, 128), f32),
            pltpu.SemaphoreType.DMA(()),
            pltpu.SemaphoreType.DMA((4 * nj + 4,)),
            pltpu.SemaphoreType.DMA((messages,)),
            pltpu.SemaphoreType.DMA((messages,)),
        ],
        compiler_params=pltpu.CompilerParams(
            collective_id=0, has_side_effects=True, vmem_limit_bytes=40 * 1024 * 1024
        ),
    )(
        *[
            pltpu.with_memory_space_constraint(a, pltpu.HBM)
            for a in (state, velocity, limiter, conductance, potential_prior, owner, slot)
        ],
    )
    return pl.pallas_call(
        write_out,
        out_shape=(
            jax.ShapeDtypeStruct(state.shape, f32),
            jax.ShapeDtypeStruct(conductance.shape, f32),
            jax.ShapeDtypeStruct((cx, cy), f32),
        ),
        in_specs=[vmem] * 3,
        out_specs=(any_space,) * 3,
        scratch_shapes=[pltpu.SemaphoreType.DMA((2 * nj + 1,))],
        compiler_params=pltpu.CompilerParams(vmem_limit_bytes=16 * 1024 * 1024),
    )(*[pltpu.with_memory_space_constraint(r, pltpu.VMEM) for r in results])


def solution(mesh):
    in_specs = (
        P(None, "sec", "blk"),
        P(None, "sec", "blk"),
        P("sec", "blk"),
        P("sec", "blk", None, None),
        P("sec", "blk", None, None),
        P("sec", "blk"),
        P("sec", "blk"),
    )
    out_specs = (P(None, "sec", "blk"), P("sec", "blk"), P("sec", "blk"))
    return jax.shard_map(
        on_device, mesh=mesh, in_specs=in_specs, out_specs=out_specs, check_vma=False
    )
```

```python
import jax
import jax.numpy as jnp
from jax import lax
from jax.experimental import pallas as pl
from jax.experimental.pallas import tpu as pltpu
from jax.sharding import PartitionSpec as P

ITERS = 4
CORES = 2
TOP = 16
PAD = 40
GROUPS = 8
MESH = pl.DeviceIdType.MESH


def minmod(a, b):
    return jnp.maximum(jnp.minimum(a, b), jnp.minimum(jnp.maximum(a, b), 0.0))


def lane_next(tiles, lane):
    rolled = [pltpu.roll(t, 127, 1) for t in tiles]
    n = len(tiles)
    return [jnp.where(lane == 127, rolled[(j + 1) % n], rolled[j]) for j in range(n)]


def lane_prev(tiles, lane):
    rolled = [pltpu.roll(t, 1, 1) for t in tiles]
    return [jnp.where(lane == 0, rolled[j - 1], rolled[j]) for j in range(len(tiles))]


def kernel(
    dims,
    state,
    velocity,
    limiter,
    sigma,
    prior,
    owner,
    slot,
    fresh,
    out_phi,
    foot,
    grid,
    flags,
    left_x,
    right_x,
    face_x,
    face_y,
    face_before,
    blocks_to,
    block_at,
    look_at,
    look_up_at,
    packs,
    edges,
    corners,
    packs_o,
    edges_o,
    shell,
    weights,
    dense_sib,
    dense_own,
    got_sib,
    got_x,
    z_part,
    got_z,
    table,
    look_sem,
    load_sem,
    send_sem,
    recv_sem,
):
    zs, xs, secs, blks, nq, cx, cy, lat, lon = dims
    nj = cy // 128
    sb = lat * lon // 128
    me = lax.axis_index("sec")
    col = lax.axis_index("blk")
    core = lax.rem(me, CORES)
    at_x = lax.rem(lax.div(me, CORES), xs)
    at_z = lax.div(me, CORES * xs)

    def sec_of(z, x, c):
        return (z * xs + x) * CORES + c

    up, down = lax.rem(me + secs - 1, secs), lax.rem(me + 1, secs)
    left, right = lax.rem(col + blks - 1, blks), lax.rem(col + 1, blks)
    sibling = (me + 1 - 2 * core, col)
    x_peer = {d: (sec_of(at_z, lax.rem(at_x + d, xs), core), col) for d in range(1, xs)}
    z_peer = {d: (sec_of(lax.rem(at_z + d, zs), at_x, core), col) for d in range(1, zs)}
    compass = {
        (-1, -1): (up, left),
        (-1, 1): (up, right),
        (1, -1): (down, left),
        (1, 1): (down, right),
        (-1, 0): (up, col),
        (1, 0): (down, col),
        (0, -1): (me, left),
        (0, 1): (me, right),
    }

    used = [0]
    sent = []

    def send(src, dst, device):
        n = used[0]
        used[0] += 1
        copy = pltpu.make_async_remote_copy(
            src_ref=src,
            dst_ref=dst,
            send_sem=send_sem.at[n],
            recv_sem=recv_sem.at[n],
            device_id=device,
            device_id_type=MESH,
        )
        copy.start()
        sent.append(copy)
        return copy

    barrier = pltpu.get_barrier_semaphore()
    far_z = [z_peer[d] for d in sorted(z_peer, key=lambda d: -min(d, zs - d))]
    partners = [*far_z, *compass.values(), *x_peer.values(), sibling]
    for device in partners:
        pl.semaphore_signal(barrier, inc=1, device_id=device, device_id_type=MESH)

    loads = {}

    def load(name, src, dst):
        copy = pltpu.make_async_copy(src, dst, load_sem.at[len(loads)])
        copy.start()
        loads[name] = copy

    mid = slice(TOP, TOP + cx)
    outer, inner = [0, nj - 1], list(range(1, nj - 1))
    for j in outer + inner:
        lanes = slice(128 * j, 128 * j + 128)
        load(("f", j), state.at[nq - 2 : nq, :, lanes], grid.at[nq - 2 : nq, j, mid, :])
        load(("v", j), velocity.at[:, :, lanes], grid.at[nq : nq + 2, j, mid, :])
        load(("l", j), limiter.at[:, lanes], flags.at[j])
    load("owner", owner, blocks_to.at[0])
    load("slot", slot, blocks_to.at[1])
    load("sigma", sigma, shell.at[0, 8 : 8 + lat, 128 : 128 + lon])
    load("prior", prior, shell.at[1, 8 : 8 + lat, 128 : 128 + lon])
    for j in range(nj):
        lanes = slice(128 * j, 128 * j + 128)
        load(("o", j), state.at[: nq - 2, :, lanes], grid.at[: nq - 2, j, mid, :])

    def loaded(j):
        for name in ("f", "v", "l"):
            loads[(name, j)].wait()
        grid[nq + 2, j, mid, :] = 0.5 * flags[j].astype(jnp.float32)

    for j in outer:
        loaded(j)
    first = nq - 2
    fields = slice(first, first + 5)
    top, bottom = slice(TOP, TOP + 8), slice(TOP + cx - 8, TOP + cx)
    above, below = slice(TOP - 8, TOP), slice(TOP + cx, TOP + cx + 8)
    rows = cx // GROUPS
    wide = lax.broadcasted_iota(jnp.int32, (rows, 128), 1)

    def pack(base, count, width):
        at_left = jnp.zeros((rows, 128), jnp.float32)
        at_right = jnp.zeros((rows, 128), jnp.float32)
        for g in range(GROUPS):
            here = slice(TOP + g * rows, TOP + (g + 1) * rows)
            for a in range(count):
                at = 16 * g + width * a
                mask = (wide >= at) & (wide < at + width)
                at_left = jnp.where(mask, pltpu.roll(grid[base + a, 0, here, :], at, 1), at_left)
                moved = pltpu.roll(grid[base + a, nj - 1, here, :], (at + width) % 128, 1)
                at_right = jnp.where(mask, moved, at_right)
        return at_left, at_right

    def unpack(base, count, width, from_left, from_right, take, put, size, group):
        side = lax.broadcasted_iota(jnp.int32, (size, 128), 1) < 64
        for a in range(count):
            at = 16 * group + width * a
            r = pltpu.roll(from_right[take, :], (128 - at) % 128, 1)
            l = pltpu.roll(from_left[take, :], (256 - width - at) % 128, 1)
            grid[base + a, nj, put, :] = jnp.where(side, r, l)

    to_left, to_right = pack(first, 5, 3)
    packs[0] = to_left
    packs[1] = to_right
    for j in inner:
        loaded(j)
    pl.semaphore_wait(barrier, len(partners))
    halo = []
    halo.append(send(packs.at[1, rows - 8 : rows, :], corners.at[0], (down, right)))
    halo.append(send(packs.at[0, rows - 8 : rows, :], corners.at[1], (down, left)))
    halo.append(send(packs.at[1, 0:8, :], corners.at[2], (up, right)))
    halo.append(send(packs.at[0, 0:8, :], corners.at[3], (up, left)))
    halo.append(send(grid.at[fields, 0:nj, bottom, :], grid.at[fields, 0:nj, above, :], (down, col)))
    halo.append(send(grid.at[fields, 0:nj, top, :], grid.at[fields, 0:nj, below, :], (up, col)))
    halo.append(send(packs.at[1], edges.at[0], (me, right)))
    halo.append(send(packs.at[0], edges.at[1], (me, left)))

    row_src = {0: slice(8, 8 + lat), 1: slice(lat, lat + 8), -1: slice(8, 16)}
    row_dst = {0: slice(8, 8 + lat), 1: slice(0, 8), -1: slice(8 + lat, 16 + lat)}
    lane_src = {0: slice(128, 128 + lon), 1: slice(lon, lon + 128), -1: slice(128, 256)}
    lane_dst = {0: slice(128, 128 + lon), 1: slice(0, 128), -1: slice(128 + lon, 256 + lon)}

    def shell_halo(which):
        return [
            send(
                shell.at[which, row_src[dr], lane_src[dc]],
                shell.at[which, row_dst[dr], lane_dst[dc]],
                device,
            )
            for (dr, dc), device in compass.items()
        ]

    loads["sigma"].wait()
    loads["prior"].wait()
    shell_copies = shell_halo(slice(0, 2))

    per_row = lon // 128
    loads["owner"].wait()
    loads["slot"].wait()
    at_owner, at_slot = blocks_to[0], blocks_to[1]
    look_at[...] = at_owner * sb + at_slot
    look_load = pltpu.make_async_copy(look_at, look_up_at, look_sem)
    look_load.start()
    ordered = (
        ((at_owner % CORES) * zs + at_owner // (CORES * xs)) * xs + (at_owner // CORES) % xs
    ) * sb
    ordered = ordered + (at_slot % per_row) * lat + at_slot // per_row
    to_lane = lax.broadcasted_iota(jnp.int32, (128, 128), 1)
    from_lane = lax.broadcasted_iota(jnp.int32, (128, 128), 0)
    each = 128 // nj
    moved = ((from_lane % nj) * each + from_lane // nj == to_lane).astype(jnp.float32)

    def move(a):
        return jnp.dot(a.astype(jnp.float32), moved, preferred_element_type=jnp.float32).astype(jnp.int32)

    block_at[...] = move(ordered // 64) * 64 + move(ordered % 64)

    for j in range(nj):
        loads[("o", j)].wait()
    others = slice(0, nq - 2)
    halo_o = [
        send(grid.at[others, 0:nj, bottom, :], grid.at[others, 0:nj, above, :], (down, col)),
        send(grid.at[others, 0:nj, top, :], grid.at[others, 0:nj, below, :], (up, col)),
    ]
    to_left, to_right = pack(0, nq - 2, 2)
    packs_o[0] = to_left
    packs_o[1] = to_right
    halo_o.append(send(packs_o.at[1], edges_o.at[0], (me, right)))
    halo_o.append(send(packs_o.at[0], edges_o.at[1], (me, left)))

    for copy in halo:
        copy.wait_recv()
    for g in range(GROUPS):
        here = slice(TOP + g * rows, TOP + (g + 1) * rows)
        unpack(first, 5, 3, edges.at[0], edges.at[1], slice(0, rows), here, rows, g)
    unpack(first, 5, 3, corners.at[0], corners.at[1], slice(0, 8), above, 8, GROUPS - 1)
    unpack(first, 5, 3, corners.at[2], corners.at[3], slice(0, 8), below, 8, 0)

    around_rows = cx + 16
    ring = slice(TOP - 8, TOP + cx + 8)
    lane_r = lax.broadcasted_iota(jnp.int32, (around_rows, 128), 1)
    speed_y = [grid[nq + 1, j, ring, :] for j in range(nj + 1)]
    faces_y = [0.2 * (here + after) for here, after in zip(speed_y, lane_next(speed_y, lane_r))]
    faces_before = lane_prev(faces_y, lane_r)
    for j in range(nj + 1):
        face_y[j, ring, :] = faces_y[j]
        face_before[j, ring, :] = faces_before[j]
        face_x[j, ring, :] = 0.2 * (grid[nq, j, ring, :] + grid[nq, j, TOP - 7 : TOP + cx + 9, :])

    def advect(q, tiles_x, start, high):
        lane_h = lax.broadcasted_iota(jnp.int32, (high, 128), 1)
        deep = 16

        def along_x(k, carry):
            b = pl.multiple_of(TOP - 8 + deep * k, 8)
            for j in range(tiles_x):
                here = grid[q, j, pl.ds(b, deep), :]
                lower = here - grid[q, j, pl.ds(b - 1, deep), :]
                upper = grid[q, j, pl.ds(b + 1, deep), :] - here
                half = minmod(lower, upper) * grid[nq + 2, j, pl.ds(b, deep), :]
                left_x[j, pl.ds(b, deep), :] = here + half
                right_x[j, pl.ds(b, deep), :] = here - half
            return carry

        lax.fori_loop(0, (cx + 16) // deep, along_x, 0)
        at, above, below = (slice(start + n, start + n + high) for n in (0, -1, 1))
        here = [grid[q, j, at, :] for j in range(nj + 1)]
        nexts, befores = lane_next(here, lane_h), lane_prev(here, lane_h)
        half = [
            minmod(h - before, after - h) * grid[nq + 2, j, at, :]
            for j, (h, before, after) in enumerate(zip(here, befores, nexts))
        ]
        left_y = [h + m for h, m in zip(here, half)]
        right_y = [h - m for h, m in zip(here, half)]
        right_next, left_before = lane_next(right_y, lane_h), lane_prev(left_y, lane_h)
        for j in range(tiles_x):
            speed = face_y[j, at, :]
            flux_y = speed * jnp.where(speed > 0.0, left_y[j], right_next[j])
            speed = face_before[j, at, :]
            flux_before = speed * jnp.where(speed > 0.0, left_before[j], right_y[j])
            speed = face_x[j, at, :]
            flux_x = speed * jnp.where(speed > 0.0, left_x[j, at, :], right_x[j, below, :])
            speed = face_x[j, above, :]
            flux_above = speed * jnp.where(speed > 0.0, left_x[j, above, :], right_x[j, at, :])
            fresh[q, j, at, :] = here[j] - ((flux_x - flux_above) + (flux_y - flux_before))

    def field(q, carry):
        advect(q, nj + 1, TOP - 8, cx + 16)
        return carry

    lax.fori_loop(nq - 2, nq, field, 0)
    lane_c = lax.broadcasted_iota(jnp.int32, (cx, 128), 1)
    field_x = [fresh[nq - 2, j, mid, :] for j in range(nj + 1)]
    after, before = lane_next(field_x, lane_c), lane_prev(field_x, lane_c)
    for j in range(nj):
        current = 0.5 * (
            fresh[nq - 1, j, TOP + 1 : TOP + cx + 1, :] - fresh[nq - 1, j, TOP - 1 : TOP + cx - 1, :]
        ) - 0.5 * (after[j] - before[j])
        high = current.astype(jnp.bfloat16)
        low = (current - high.astype(jnp.float32)).astype(jnp.bfloat16)
        for k in range(cx // each):
            part = slice((k * nj + j) * each, (k * nj + j + 1) * each)
            weights[part, 0:128] = high[k * each : (k + 1) * each, :]
            weights[part, 128:256] = low[k * each : (k + 1) * each, :]

    order = sorted(range(zs), key=lambda d: -min(d, zs - d))
    duos = [order[n : n + 2] for n in range(0, zs, 2)]
    per_z = xs * sb
    groups = nj * cx // 128

    def sums(duo, to_core):
        ids = jnp.concatenate(
            [
                lax.broadcasted_iota(jnp.int32, (per_z, 128), 0)
                + (to_core * zs + lax.rem(at_z + d, zs)) * per_z
                for d in duo
            ],
            axis=0,
        )
        chosen = [
            jnp.where(ids == block_at[k : k + 1, :], 1.0, 0.0).astype(jnp.bfloat16)
            for k in range(groups)
        ]
        both = jnp.dot(
            jnp.concatenate(chosen, axis=1), weights[...], preferred_element_type=jnp.float32
        )
        return (both[:, :128] + both[:, 128:]).reshape(2, xs, sb, 128)

    sib_copies, x_copies, z_copies = {}, {}, {}
    order_x = sorted(x_peer, key=lambda d: -min(d, xs - d))

    def for_sibling(n):
        dense_sib[n] = sums(duos[n], 1 - core)
        sib_copies[n] = send(dense_sib.at[n], got_sib.at[n], sibling)

    def for_own(n):
        dense_own[n] = sums(duos[n], core)
        sib_copies[n].wait_recv()
        dense_own[n] = dense_own[n] + got_sib[n]
        last = n == len(duos) - 1
        for h in (slice(0, 1), slice(1, 2)) if last else (slice(0, 2),):
            for d in order_x:
                part = dense_own.at[n, h, lax.rem(at_x + d, xs)]
                copy = send(part, got_x.at[n, d - 1, h], x_peer[d])
                x_copies.setdefault((n, h.start), []).append(copy)

    for_sibling(0)
    for n in range(len(duos)):
        if n + 1 < len(duos):
            for_sibling(n + 1)
        for_own(n)
    for copy in halo_o:
        copy.wait_recv()
    for g in range(GROUPS):
        here = slice(TOP + g * rows, TOP + (g + 1) * rows)
        unpack(0, nq - 2, 2, edges_o.at[0], edges_o.at[1], slice(0, rows), here, rows, g)

    def other(q, carry):
        advect(q, nj, TOP, cx)
        return carry

    def along_z(n):
        for h, d in enumerate(duos[n]):
            for copy in x_copies.get((n, h), []):
                copy.wait_recv()
            part = dense_own[n, h, at_x]
            for e in x_peer:
                part = part + got_x[n, e - 1, h]
            z_part[n, h] = part
            if d:
                z_copies[d] = send(z_part.at[n, h], got_z.at[d - 1], z_peer[d])

    ahead = [nq - 6] + [1] * min(2, len(duos) - 1)
    done = 0
    for n in range(len(duos)):
        if n < len(ahead):
            lax.fori_loop(done, done + ahead[n], other, 0)
            done += ahead[n]
        along_z(n)
    lax.fori_loop(done, nq - 3, other, 0)
    source = z_part[len(duos) - 1, 1]
    for d in order[:-1]:
        z_copies[d].wait_recv()
        source = source + got_z[d - 1]
    for c in range(lon // 128):
        at = 128 + 128 * c
        shell[2, 8 : 8 + lat, at : at + 128] = source[c * lat : (c + 1) * lat, :]
    source_copies = shell_halo(slice(2, 3))
    lax.fori_loop(nq - 3, nq - 2, other, 0)

    for copy in shell_copies:
        copy.wait_recv()
    shape = (lat + 16, lon + 256)
    lat_at = lax.broadcasted_iota(jnp.int32, shape, 0) + (me * lat - 8)
    lon_at = lax.broadcasted_iota(jnp.int32, shape, 1) + (col * lon - 128)
    inside = (lat_at >= 0) & (lat_at < secs * lat) & (lon_at >= 0) & (lon_at < blks * lon)
    sig = jnp.where(inside, shell[0], 0.0)
    phi = jnp.where(inside, shell[1], 0.0)

    def around(a):
        return (
            pltpu.roll(a, 1, 0),
            pltpu.roll(a, lat + 15, 0),
            pltpu.roll(a, 1, 1),
            pltpu.roll(a, lon + 255, 1),
        )

    ways = [0.5 * (sig + other_sig) for other_sig in around(sig)]
    inverse = 1.0 / (ways[0] + ways[1] + ways[2] + ways[3] + 1.0)
    for copy in source_copies:
        copy.wait_recv()
    src = shell[2]
    for _ in range(ITERS):
        n, s, w, e = around(phi)
        total = ways[0] * n + ways[1] * s + ways[2] * w + ways[3] * e + src
        phi = jnp.where(inside, total * inverse, 0.0)
    phi = phi[8 : 8 + lat, 128 : 128 + lon]
    out_phi[...] = phi

    split = sb // 8 * 7

    def piece(z, x, start=0, size=sb):
        at = sec_of(z, x, core) * sb + start
        return table.at[pl.ds(pl.multiple_of(at, 8), size), :]

    mine = pl.multiple_of(me * sb, sb)
    for c in range(per_row):
        table[pl.ds(mine + c, lat, stride=per_row), :] = phi[:, c * 128 : (c + 1) * 128]

    from_z, from_x, first_rows, last_rows, from_sib = {}, {}, {}, {}, []
    own = piece(at_z, at_x)
    nearest = sorted(range(1, zs), key=lambda d: min(d, zs - d))
    for d in nearest[:2]:
        from_z[d] = send(own, own, z_peer[d])
    for d in order_x:
        from_x[d] = send(own, own, x_peer[d])
    for d in nearest[2:]:
        from_z[d] = send(own, own, z_peer[d])

    def share(part):
        from_sib.append(send(part, part, sibling))

    def z_back(d):
        return lax.rem(at_z + zs - d, zs)

    def x_back(d):
        return lax.rem(at_x + xs - d, xs)

    share(own)

    def along_x(d):
        from_z[d].wait_recv()
        part = piece(z_back(d), at_x, 0, split)
        for e in order_x:
            first_rows[d, e] = send(part, part, x_peer[e])
        share(piece(z_back(d), at_x))

    for d in nearest[:2]:
        along_x(d)
    for e in order_x[::-1]:
        from_x[e].wait_recv()
        part = piece(at_z, x_back(e), split, sb - split)
        for d in nearest[::-1]:
            last_rows[d, e] = send(part, part, z_peer[d])
        share(piece(at_z, x_back(e)))
    for d in nearest[2:]:
        along_x(d)
    for d in nearest:
        for e in order_x:
            first_rows[d, e].wait_recv()
            last_rows[d, e].wait_recv()
            share(piece(z_back(d), x_back(e)))
    for copy in from_sib:
        copy.wait_recv()
    look_load.wait()

    def look_up(k, carry):
        b = pl.multiple_of(2 * each * k, 8)
        for n in range(2):
            for r in range(each):
                for j in range(nj):
                    at = look_up_at[2 * k + n, r * nj + j]
                    foot[j, pl.ds(b + n * each + r, 1), :] = table[pl.ds(at, 1), :]
        return carry

    lax.fori_loop(0, cx // (2 * each), look_up, 0)
    for copy in sent:
        copy.wait_send()


def write_out(fresh, phi, foot, out_state, out_phi, out_foot, sem):
    cx = foot.shape[1]
    copies = [pltpu.make_async_copy(phi, out_phi, sem.at[0])]
    for j in range(foot.shape[0]):
        lanes = slice(128 * j, 128 * j + 128)
        mid = fresh.at[:, j, TOP : TOP + cx, :]
        copies.append(pltpu.make_async_copy(mid, out_state.at[:, :, lanes], sem.at[2 * j + 1]))
        copies.append(pltpu.make_async_copy(foot.at[j], out_foot.at[:, lanes], sem.at[2 * j + 2]))
    for copy in copies:
        copy.start()
    for copy in copies:
        copy.wait()


def on_device(
    state, velocity, limiter, footpoint_owner, footpoint_slot, conductance, potential_prior
):
    secs, blks = lax.axis_size("sec"), lax.axis_size("blk")
    xs = 4 if secs % 16 == 0 else 2
    zs = secs // (CORES * xs)
    nq, cx, cy = state.shape
    lat, lon = conductance.shape
    nj = cy // 128
    sb = lat * lon // 128
    blocks = nj * cx
    owner = footpoint_owner.reshape(blocks // 128, 128)
    slot = footpoint_slot.reshape(blocks // 128, 128)
    dims = (zs, xs, secs, blks, nq, cx, cy, lat, lon)
    f32 = jnp.float32
    rows = cx // GROUPS
    messages = 12 + 8 + 8 + zs // 2 + zs // 2 * (xs - 1) + (xs - 1) + 2 * (zs - 1) + (xs - 1) + 2 * (zs - 1) * (xs - 1) + zs * xs
    any_space = pl.BlockSpec(memory_space=pl.ANY)
    vmem = pl.BlockSpec(memory_space=pltpu.VMEM)

    def body(*refs):
        kernel(dims, *refs)

    results = pl.pallas_call(
        body,
        out_shape=(
            pltpu.VMEM((nq, nj + 1, cx + PAD, 128), f32),
            pltpu.VMEM(conductance.shape, f32),
            pltpu.VMEM((nj, cx, 128), f32),
        ),
        in_specs=[pl.BlockSpec(memory_space=pltpu.HBM)] * 7,
        out_specs=(vmem, vmem, vmem),
        scratch_shapes=[
            pltpu.VMEM((nq + 3, nj + 1, cx + PAD, 128), f32),
            pltpu.VMEM((nj, cx, 128), jnp.int32),
            pltpu.VMEM((nj + 1, cx + PAD, 128), f32),
            pltpu.VMEM((nj + 1, cx + PAD, 128), f32),
            pltpu.VMEM((nj + 1, cx + PAD, 128), f32),
            pltpu.VMEM((nj + 1, cx + PAD, 128), f32),
            pltpu.VMEM((nj + 1, cx + PAD, 128), f32),
            pltpu.VMEM((2, blocks // 128, 128), jnp.int32),
            pltpu.VMEM((blocks // 128, 128), jnp.int32),
            pltpu.VMEM((blocks // 128, 128), jnp.int32),
            pltpu.SMEM((blocks // 128, 128), jnp.int32),
            pltpu.VMEM((2, rows, 128), f32),
            pltpu.VMEM((2, rows, 128), f32),
            pltpu.VMEM((4, 8, 128), f32),
            pltpu.VMEM((2, rows, 128), f32),
            pltpu.VMEM((2, rows, 128), f32),
            pltpu.VMEM((3, lat + 16, lon + 256), f32),
            pltpu.VMEM((blocks, 256), jnp.bfloat16),
            pltpu.VMEM((zs // 2, 2, xs, sb, 128), f32),
            pltpu.VMEM((zs // 2, 2, xs, sb, 128), f32),
            pltpu.VMEM((zs // 2, 2, xs, sb, 128), f32),
            pltpu.VMEM((zs // 2, xs - 1, 2, sb, 128), f32),
            pltpu.VMEM((zs // 2, 2, sb, 128), f32),
            pltpu.VMEM((zs - 1, sb, 128), f32),
            pltpu.VMEM((secs * sb, 128), f32),
            pltpu.SemaphoreType.DMA(()),
            pltpu.SemaphoreType.DMA((4 * nj + 4,)),
            pltpu.SemaphoreType.DMA((messages,)),
            pltpu.SemaphoreType.DMA((messages,)),
        ],
        compiler_params=pltpu.CompilerParams(
            collective_id=0, has_side_effects=True, vmem_limit_bytes=40 * 1024 * 1024
        ),
    )(
        *[
            pltpu.with_memory_space_constraint(a, pltpu.HBM)
            for a in (state, velocity, limiter, conductance, potential_prior, owner, slot)
        ],
    )
    return pl.pallas_call(
        write_out,
        out_shape=(
            jax.ShapeDtypeStruct(state.shape, f32),
            jax.ShapeDtypeStruct(conductance.shape, f32),
            jax.ShapeDtypeStruct((cx, cy), f32),
        ),
        in_specs=[vmem] * 3,
        out_specs=(any_space,) * 3,
        scratch_shapes=[pltpu.SemaphoreType.DMA((2 * nj + 1,))],
        compiler_params=pltpu.CompilerParams(vmem_limit_bytes=16 * 1024 * 1024),
    )(*[pltpu.with_memory_space_constraint(r, pltpu.VMEM) for r in results])


def solution(mesh):
    in_specs = (
        P(None, "sec", "blk"),
        P(None, "sec", "blk"),
        P("sec", "blk"),
        P("sec", "blk", None, None),
        P("sec", "blk", None, None),
        P("sec", "blk"),
        P("sec", "blk"),
    )
    out_specs = (P(None, "sec", "blk"), P("sec", "blk"), P("sec", "blk"))
    return jax.shard_map(
        on_device, mesh=mesh, in_specs=in_specs, out_specs=out_specs, check_vma=False
    )
```

```python
import jax
import jax.numpy as jnp
from jax import lax
from jax.experimental import pallas as pl
from jax.experimental.pallas import tpu as pltpu
from jax.sharding import PartitionSpec as P

ITERS = 4
CORES = 2
TOP = 16
PAD = 40
GROUPS = 8
MESH = pl.DeviceIdType.MESH


def minmod(a, b):
    return jnp.maximum(jnp.minimum(a, b), jnp.minimum(jnp.maximum(a, b), 0.0))


def lane_next(tiles, lane):
    rolled = [pltpu.roll(t, 127, 1) for t in tiles]
    n = len(tiles)
    return [jnp.where(lane == 127, rolled[(j + 1) % n], rolled[j]) for j in range(n)]


def lane_prev(tiles, lane):
    rolled = [pltpu.roll(t, 1, 1) for t in tiles]
    return [jnp.where(lane == 0, rolled[j - 1], rolled[j]) for j in range(len(tiles))]


def kernel(
    dims,
    state,
    velocity,
    limiter,
    sigma,
    prior,
    owner,
    slot,
    fresh,
    out_phi,
    foot,
    grid,
    flags,
    left_x,
    right_x,
    face_x,
    face_y,
    face_before,
    blocks_to,
    block_at,
    look_at,
    look_up_at,
    packs,
    edges,
    corners,
    packs_o,
    edges_o,
    shell,
    weights,
    dense_sib,
    dense_own,
    got_sib,
    got_x,
    z_part,
    got_z,
    table,
    look_sem,
    load_sem,
    send_sem,
    recv_sem,
):
    zs, xs, secs, blks, nq, cx, cy, lat, lon = dims
    nj = cy // 128
    sb = lat * lon // 128
    me = lax.axis_index("sec")
    col = lax.axis_index("blk")
    core = lax.rem(me, CORES)
    at_x = lax.rem(lax.div(me, CORES), xs)
    at_z = lax.div(me, CORES * xs)

    def sec_of(z, x, c):
        return (z * xs + x) * CORES + c

    up, down = lax.rem(me + secs - 1, secs), lax.rem(me + 1, secs)
    left, right = lax.rem(col + blks - 1, blks), lax.rem(col + 1, blks)
    sibling = (me + 1 - 2 * core, col)
    x_peer = {d: (sec_of(at_z, lax.rem(at_x + d, xs), core), col) for d in range(1, xs)}
    z_peer = {d: (sec_of(lax.rem(at_z + d, zs), at_x, core), col) for d in range(1, zs)}
    compass = {
        (-1, -1): (up, left),
        (-1, 1): (up, right),
        (1, -1): (down, left),
        (1, 1): (down, right),
        (-1, 0): (up, col),
        (1, 0): (down, col),
        (0, -1): (me, left),
        (0, 1): (me, right),
    }

    used = [0]
    sent = []

    def send(src, dst, device):
        n = used[0]
        used[0] += 1
        copy = pltpu.make_async_remote_copy(
            src_ref=src,
            dst_ref=dst,
            send_sem=send_sem.at[n],
            recv_sem=recv_sem.at[n],
            device_id=device,
            device_id_type=MESH,
        )
        copy.start()
        sent.append(copy)
        return copy

    barrier = pltpu.get_barrier_semaphore()
    far_z = [z_peer[d] for d in sorted(z_peer, key=lambda d: -min(d, zs - d))]
    partners = [*far_z, *compass.values(), *x_peer.values(), sibling]
    for device in partners:
        pl.semaphore_signal(barrier, inc=1, device_id=device, device_id_type=MESH)

    loads = {}

    def load(name, src, dst):
        copy = pltpu.make_async_copy(src, dst, load_sem.at[len(loads)])
        copy.start()
        loads[name] = copy

    mid = slice(TOP, TOP + cx)
    outer, inner = [0, nj - 1], list(range(1, nj - 1))
    for j in outer + inner:
        lanes = slice(128 * j, 128 * j + 128)
        load(("f", j), state.at[nq - 2 : nq, :, lanes], grid.at[nq - 2 : nq, j, mid, :])
        load(("v", j), velocity.at[:, :, lanes], grid.at[nq : nq + 2, j, mid, :])
        load(("l", j), limiter.at[:, lanes], flags.at[j])
    load("owner", owner, blocks_to.at[0])
    load("slot", slot, blocks_to.at[1])
    load("sigma", sigma, shell.at[0, 8 : 8 + lat, 128 : 128 + lon])
    load("prior", prior, shell.at[1, 8 : 8 + lat, 128 : 128 + lon])
    for j in range(nj):
        lanes = slice(128 * j, 128 * j + 128)
        load(("o", j), state.at[: nq - 2, :, lanes], grid.at[: nq - 2, j, mid, :])

    def loaded(j):
        for name in ("f", "v", "l"):
            loads[(name, j)].wait()
        grid[nq + 2, j, mid, :] = 0.5 * flags[j].astype(jnp.float32)

    for j in outer:
        loaded(j)
    first = nq - 2
    fields = slice(first, first + 5)
    top, bottom = slice(TOP, TOP + 8), slice(TOP + cx - 8, TOP + cx)
    above, below = slice(TOP - 8, TOP), slice(TOP + cx, TOP + cx + 8)
    rows = cx // GROUPS
    wide = lax.broadcasted_iota(jnp.int32, (rows, 128), 1)

    def pack(base, count, width):
        at_left = jnp.zeros((rows, 128), jnp.float32)
        at_right = jnp.zeros((rows, 128), jnp.float32)
        for g in range(GROUPS):
            here = slice(TOP + g * rows, TOP + (g + 1) * rows)
            for a in range(count):
                at = 16 * g + width * a
                mask = (wide >= at) & (wide < at + width)
                at_left = jnp.where(mask, pltpu.roll(grid[base + a, 0, here, :], at, 1), at_left)
                moved = pltpu.roll(grid[base + a, nj - 1, here, :], (at + width) % 128, 1)
                at_right = jnp.where(mask, moved, at_right)
        return at_left, at_right

    def unpack(base, count, width, from_left, from_right, take, put, size, group):
        side = lax.broadcasted_iota(jnp.int32, (size, 128), 1) < 64
        for a in range(count):
            at = 16 * group + width * a
            r = pltpu.roll(from_right[take, :], (128 - at) % 128, 1)
            l = pltpu.roll(from_left[take, :], (256 - width - at) % 128, 1)
            grid[base + a, nj, put, :] = jnp.where(side, r, l)

    to_left, to_right = pack(first, 5, 3)
    packs[0] = to_left
    packs[1] = to_right
    for j in inner:
        loaded(j)
    pl.semaphore_wait(barrier, len(partners))
    halo = []
    halo.append(send(packs.at[1, rows - 8 : rows, :], corners.at[0], (down, right)))
    halo.append(send(packs.at[0, rows - 8 : rows, :], corners.at[1], (down, left)))
    halo.append(send(packs.at[1, 0:8, :], corners.at[2], (up, right)))
    halo.append(send(packs.at[0, 0:8, :], corners.at[3], (up, left)))
    halo.append(send(grid.at[fields, 0:nj, bottom, :], grid.at[fields, 0:nj, above, :], (down, col)))
    halo.append(send(grid.at[fields, 0:nj, top, :], grid.at[fields, 0:nj, below, :], (up, col)))
    halo.append(send(packs.at[1], edges.at[0], (me, right)))
    halo.append(send(packs.at[0], edges.at[1], (me, left)))

    row_src = {0: slice(8, 8 + lat), 1: slice(lat, lat + 8), -1: slice(8, 16)}
    row_dst = {0: slice(8, 8 + lat), 1: slice(0, 8), -1: slice(8 + lat, 16 + lat)}
    lane_src = {0: slice(128, 128 + lon), 1: slice(lon, lon + 128), -1: slice(128, 256)}
    lane_dst = {0: slice(128, 128 + lon), 1: slice(0, 128), -1: slice(128 + lon, 256 + lon)}

    def shell_halo(which):
        return [
            send(
                shell.at[which, row_src[dr], lane_src[dc]],
                shell.at[which, row_dst[dr], lane_dst[dc]],
                device,
            )
            for (dr, dc), device in compass.items()
        ]

    loads["sigma"].wait()
    loads["prior"].wait()
    shell_copies = shell_halo(slice(0, 2))

    per_row = lon // 128
    loads["owner"].wait()
    loads["slot"].wait()
    at_owner, at_slot = blocks_to[0], blocks_to[1]
    look_at[...] = at_owner * sb + at_slot
    look_load = pltpu.make_async_copy(look_at, look_up_at, look_sem)
    look_load.start()
    ordered = (
        ((at_owner % CORES) * zs + at_owner // (CORES * xs)) * xs + (at_owner // CORES) % xs
    ) * sb
    ordered = ordered + (at_slot % per_row) * lat + at_slot // per_row
    to_lane = lax.broadcasted_iota(jnp.int32, (128, 128), 1)
    from_lane = lax.broadcasted_iota(jnp.int32, (128, 128), 0)
    each = 128 // nj
    moved = ((from_lane % nj) * each + from_lane // nj == to_lane).astype(jnp.float32)

    def move(a):
        return jnp.dot(a.astype(jnp.float32), moved, preferred_element_type=jnp.float32).astype(jnp.int32)

    block_at[...] = move(ordered // 64) * 64 + move(ordered % 64)

    for j in range(nj):
        loads[("o", j)].wait()
    others = slice(0, nq - 2)
    halo_o = [
        send(grid.at[others, 0:nj, bottom, :], grid.at[others, 0:nj, above, :], (down, col)),
        send(grid.at[others, 0:nj, top, :], grid.at[others, 0:nj, below, :], (up, col)),
    ]
    to_left, to_right = pack(0, nq - 2, 2)
    packs_o[0] = to_left
    packs_o[1] = to_right
    halo_o.append(send(packs_o.at[1], edges_o.at[0], (me, right)))
    halo_o.append(send(packs_o.at[0], edges_o.at[1], (me, left)))

    for copy in halo:
        copy.wait_recv()
    for g in range(GROUPS):
        here = slice(TOP + g * rows, TOP + (g + 1) * rows)
        unpack(first, 5, 3, edges.at[0], edges.at[1], slice(0, rows), here, rows, g)
    unpack(first, 5, 3, corners.at[0], corners.at[1], slice(0, 8), above, 8, GROUPS - 1)
    unpack(first, 5, 3, corners.at[2], corners.at[3], slice(0, 8), below, 8, 0)

    around_rows = cx + 16
    ring = slice(TOP - 8, TOP + cx + 8)
    lane_r = lax.broadcasted_iota(jnp.int32, (around_rows, 128), 1)
    speed_y = [grid[nq + 1, j, ring, :] for j in range(nj + 1)]
    faces_y = [0.2 * (here + after) for here, after in zip(speed_y, lane_next(speed_y, lane_r))]
    faces_before = lane_prev(faces_y, lane_r)
    for j in range(nj + 1):
        face_y[j, ring, :] = faces_y[j]
        face_before[j, ring, :] = faces_before[j]
        face_x[j, ring, :] = 0.2 * (grid[nq, j, ring, :] + grid[nq, j, TOP - 7 : TOP + cx + 9, :])

    def advect(q, tiles_x, start, high):
        lane_h = lax.broadcasted_iota(jnp.int32, (high, 128), 1)
        deep = 16

        def along_x(k, carry):
            b = pl.multiple_of(TOP - 8 + deep * k, 8)
            for j in range(tiles_x):
                here = grid[q, j, pl.ds(b, deep), :]
                lower = here - grid[q, j, pl.ds(b - 1, deep), :]
                upper = grid[q, j, pl.ds(b + 1, deep), :] - here
                half = minmod(lower, upper) * grid[nq + 2, j, pl.ds(b, deep), :]
                left_x[j, pl.ds(b, deep), :] = here + half
                right_x[j, pl.ds(b, deep), :] = here - half
            return carry

        lax.fori_loop(0, (cx + 16) // deep, along_x, 0)
        at, above, below = (slice(start + n, start + n + high) for n in (0, -1, 1))
        here = [grid[q, j, at, :] for j in range(nj + 1)]
        nexts, befores = lane_next(here, lane_h), lane_prev(here, lane_h)
        half = [
            minmod(h - before, after - h) * grid[nq + 2, j, at, :]
            for j, (h, before, after) in enumerate(zip(here, befores, nexts))
        ]
        left_y = [h + m for h, m in zip(here, half)]
        right_y = [h - m for h, m in zip(here, half)]
        right_next, left_before = lane_next(right_y, lane_h), lane_prev(left_y, lane_h)
        for j in range(tiles_x):
            speed = face_y[j, at, :]
            flux_y = speed * jnp.where(speed > 0.0, left_y[j], right_next[j])
            speed = face_before[j, at, :]
            flux_before = speed * jnp.where(speed > 0.0, left_before[j], right_y[j])
            speed = face_x[j, at, :]
            flux_x = speed * jnp.where(speed > 0.0, left_x[j, at, :], right_x[j, below, :])
            speed = face_x[j, above, :]
            flux_above = speed * jnp.where(speed > 0.0, left_x[j, above, :], right_x[j, at, :])
            fresh[q, j, at, :] = here[j] - ((flux_x - flux_above) + (flux_y - flux_before))

    advect(nq - 2, nj + 1, TOP - 8, cx + 16)
    advect(nq - 1, nj + 1, TOP - 8, cx + 16)
    lane_c = lax.broadcasted_iota(jnp.int32, (cx, 128), 1)
    field_x = [fresh[nq - 2, j, mid, :] for j in range(nj + 1)]
    after, before = lane_next(field_x, lane_c), lane_prev(field_x, lane_c)
    for j in range(nj):
        current = 0.5 * (
            fresh[nq - 1, j, TOP + 1 : TOP + cx + 1, :] - fresh[nq - 1, j, TOP - 1 : TOP + cx - 1, :]
        ) - 0.5 * (after[j] - before[j])
        high = current.astype(jnp.bfloat16)
        low = (current - high.astype(jnp.float32)).astype(jnp.bfloat16)
        for k in range(cx // each):
            part = slice((k * nj + j) * each, (k * nj + j + 1) * each)
            weights[part, 0:128] = high[k * each : (k + 1) * each, :]
            weights[part, 128:256] = low[k * each : (k + 1) * each, :]

    order = sorted(range(zs), key=lambda d: -min(d, zs - d))
    duos = [order[n : n + 2] for n in range(0, zs, 2)]
    per_z = xs * sb
    groups = nj * cx // 128

    def sums(duo, to_core):
        ids = jnp.concatenate(
            [
                lax.broadcasted_iota(jnp.int32, (per_z, 128), 0)
                + (to_core * zs + lax.rem(at_z + d, zs)) * per_z
                for d in duo
            ],
            axis=0,
        )
        chosen = [
            jnp.where(ids == block_at[k : k + 1, :], 1.0, 0.0).astype(jnp.bfloat16)
            for k in range(groups)
        ]
        both = jnp.dot(
            jnp.concatenate(chosen, axis=1), weights[...], preferred_element_type=jnp.float32
        )
        return (both[:, :128] + both[:, 128:]).reshape(2, xs, sb, 128)

    sib_copies, x_copies, z_copies = {}, {}, {}
    order_x = sorted(x_peer, key=lambda d: -min(d, xs - d))

    def for_sibling(n):
        dense_sib[n] = sums(duos[n], 1 - core)
        sib_copies[n] = send(dense_sib.at[n], got_sib.at[n], sibling)

    def for_own(n):
        dense_own[n] = sums(duos[n], core)
        sib_copies[n].wait_recv()
        dense_own[n] = dense_own[n] + got_sib[n]
        last = n == len(duos) - 1
        for h in (slice(0, 1), slice(1, 2)) if last else (slice(0, 2),):
            for d in order_x:
                part = dense_own.at[n, h, lax.rem(at_x + d, xs)]
                copy = send(part, got_x.at[n, d - 1, h], x_peer[d])
                x_copies.setdefault((n, h.start), []).append(copy)

    for_sibling(0)
    for n in range(len(duos)):
        if n + 1 < len(duos):
            for_sibling(n + 1)
        for_own(n)
    for copy in halo_o:
        copy.wait_recv()
    for g in range(GROUPS):
        here = slice(TOP + g * rows, TOP + (g + 1) * rows)
        unpack(0, nq - 2, 2, edges_o.at[0], edges_o.at[1], slice(0, rows), here, rows, g)

    def other(q, carry):
        advect(q, nj, TOP, cx)
        return carry

    def along_z(n):
        for h, d in enumerate(duos[n]):
            for copy in x_copies.get((n, h), []):
                copy.wait_recv()
            part = dense_own[n, h, at_x]
            for e in x_peer:
                part = part + got_x[n, e - 1, h]
            z_part[n, h] = part
            if d:
                z_copies[d] = send(z_part.at[n, h], got_z.at[d - 1], z_peer[d])

    ahead = [1, nq - 6, 1][: len(duos)]
    done = 0
    for n in range(len(duos)):
        if n < len(ahead):
            lax.fori_loop(done, done + ahead[n], other, 0)
            done += ahead[n]
        along_z(n)
    lax.fori_loop(done, nq - 3, other, 0)
    source = z_part[len(duos) - 1, 1]
    for d in order[:-1]:
        z_copies[d].wait_recv()
        source = source + got_z[d - 1]
    for c in range(lon // 128):
        at = 128 + 128 * c
        shell[2, 8 : 8 + lat, at : at + 128] = source[c * lat : (c + 1) * lat, :]
    source_copies = shell_halo(slice(2, 3))
    lax.fori_loop(nq - 3, nq - 2, other, 0)

    for copy in shell_copies:
        copy.wait_recv()
    shape = (lat + 16, lon + 256)
    lat_at = lax.broadcasted_iota(jnp.int32, shape, 0) + (me * lat - 8)
    lon_at = lax.broadcasted_iota(jnp.int32, shape, 1) + (col * lon - 128)
    inside = (lat_at >= 0) & (lat_at < secs * lat) & (lon_at >= 0) & (lon_at < blks * lon)
    sig = jnp.where(inside, shell[0], 0.0)
    phi = jnp.where(inside, shell[1], 0.0)

    def around(a):
        return (
            pltpu.roll(a, 1, 0),
            pltpu.roll(a, lat + 15, 0),
            pltpu.roll(a, 1, 1),
            pltpu.roll(a, lon + 255, 1),
        )

    ways = [0.5 * (sig + other_sig) for other_sig in around(sig)]
    inverse = 1.0 / (ways[0] + ways[1] + ways[2] + ways[3] + 1.0)
    for copy in source_copies:
        copy.wait_recv()
    src = shell[2]
    for _ in range(ITERS):
        n, s, w, e = around(phi)
        total = ways[0] * n + ways[1] * s + ways[2] * w + ways[3] * e + src
        phi = jnp.where(inside, total * inverse, 0.0)
    phi = phi[8 : 8 + lat, 128 : 128 + lon]
    out_phi[...] = phi

    split = sb // 8 * 7

    def piece(z, x, start=0, size=sb):
        at = sec_of(z, x, core) * sb + start
        return table.at[pl.ds(pl.multiple_of(at, 8), size), :]

    mine = pl.multiple_of(me * sb, sb)
    for c in range(per_row):
        table[pl.ds(mine + c, lat, stride=per_row), :] = phi[:, c * 128 : (c + 1) * 128]

    from_z, from_x, first_rows, last_rows, from_sib = {}, {}, {}, {}, []
    own = piece(at_z, at_x)
    nearest = sorted(range(1, zs), key=lambda d: min(d, zs - d))
    for d in nearest[:2]:
        from_z[d] = send(own, own, z_peer[d])
    for d in order_x:
        from_x[d] = send(own, own, x_peer[d])
    for d in nearest[2:]:
        from_z[d] = send(own, own, z_peer[d])

    def share(part):
        from_sib.append(send(part, part, sibling))

    def z_back(d):
        return lax.rem(at_z + zs - d, zs)

    def x_back(d):
        return lax.rem(at_x + xs - d, xs)

    share(own)

    def along_x(d):
        from_z[d].wait_recv()
        part = piece(z_back(d), at_x, 0, split)
        for e in order_x:
            first_rows[d, e] = send(part, part, x_peer[e])
        share(piece(z_back(d), at_x))

    for d in nearest[:2]:
        along_x(d)
    for e in order_x[::-1]:
        from_x[e].wait_recv()
        part = piece(at_z, x_back(e), split, sb - split)
        for d in nearest[::-1]:
            last_rows[d, e] = send(part, part, z_peer[d])
        share(piece(at_z, x_back(e)))
    for d in nearest[2:]:
        along_x(d)
    for d in nearest:
        for e in order_x:
            first_rows[d, e].wait_recv()
            last_rows[d, e].wait_recv()
            share(piece(z_back(d), x_back(e)))
    for copy in from_sib:
        copy.wait_recv()
    look_load.wait()

    def look_up(k, carry):
        b = pl.multiple_of(2 * each * k, 8)
        for n in range(2):
            for r in range(each):
                for j in range(nj):
                    at = look_up_at[2 * k + n, r * nj + j]
                    foot[j, pl.ds(b + n * each + r, 1), :] = table[pl.ds(at, 1), :]
        return carry

    lax.fori_loop(0, cx // (2 * each), look_up, 0)
    for copy in sent:
        copy.wait_send()


def write_out(fresh, phi, foot, out_state, out_phi, out_foot, sem):
    cx = foot.shape[1]
    copies = [pltpu.make_async_copy(phi, out_phi, sem.at[0])]
    for j in range(foot.shape[0]):
        lanes = slice(128 * j, 128 * j + 128)
        mid = fresh.at[:, j, TOP : TOP + cx, :]
        copies.append(pltpu.make_async_copy(mid, out_state.at[:, :, lanes], sem.at[2 * j + 1]))
        copies.append(pltpu.make_async_copy(foot.at[j], out_foot.at[:, lanes], sem.at[2 * j + 2]))
    for copy in copies:
        copy.start()
    for copy in copies:
        copy.wait()


def on_device(
    state, velocity, limiter, footpoint_owner, footpoint_slot, conductance, potential_prior
):
    secs, blks = lax.axis_size("sec"), lax.axis_size("blk")
    xs = 4 if secs % 16 == 0 else 2
    zs = secs // (CORES * xs)
    nq, cx, cy = state.shape
    lat, lon = conductance.shape
    nj = cy // 128
    sb = lat * lon // 128
    blocks = nj * cx
    owner = footpoint_owner.reshape(blocks // 128, 128)
    slot = footpoint_slot.reshape(blocks // 128, 128)
    dims = (zs, xs, secs, blks, nq, cx, cy, lat, lon)
    f32 = jnp.float32
    rows = cx // GROUPS
    messages = 12 + 8 + 8 + zs // 2 + zs // 2 * (xs - 1) + (xs - 1) + 2 * (zs - 1) + (xs - 1) + 2 * (zs - 1) * (xs - 1) + zs * xs
    any_space = pl.BlockSpec(memory_space=pl.ANY)
    vmem = pl.BlockSpec(memory_space=pltpu.VMEM)

    def body(*refs):
        kernel(dims, *refs)

    results = pl.pallas_call(
        body,
        out_shape=(
            pltpu.VMEM((nq, nj + 1, cx + PAD, 128), f32),
            pltpu.VMEM(conductance.shape, f32),
            pltpu.VMEM((nj, cx, 128), f32),
        ),
        in_specs=[pl.BlockSpec(memory_space=pltpu.HBM)] * 7,
        out_specs=(vmem, vmem, vmem),
        scratch_shapes=[
            pltpu.VMEM((nq + 3, nj + 1, cx + PAD, 128), f32),
            pltpu.VMEM((nj, cx, 128), jnp.int32),
            pltpu.VMEM((nj + 1, cx + PAD, 128), f32),
            pltpu.VMEM((nj + 1, cx + PAD, 128), f32),
            pltpu.VMEM((nj + 1, cx + PAD, 128), f32),
            pltpu.VMEM((nj + 1, cx + PAD, 128), f32),
            pltpu.VMEM((nj + 1, cx + PAD, 128), f32),
            pltpu.VMEM((2, blocks // 128, 128), jnp.int32),
            pltpu.VMEM((blocks // 128, 128), jnp.int32),
            pltpu.VMEM((blocks // 128, 128), jnp.int32),
            pltpu.SMEM((blocks // 128, 128), jnp.int32),
            pltpu.VMEM((2, rows, 128), f32),
            pltpu.VMEM((2, rows, 128), f32),
            pltpu.VMEM((4, 8, 128), f32),
            pltpu.VMEM((2, rows, 128), f32),
            pltpu.VMEM((2, rows, 128), f32),
            pltpu.VMEM((3, lat + 16, lon + 256), f32),
            pltpu.VMEM((blocks, 256), jnp.bfloat16),
            pltpu.VMEM((zs // 2, 2, xs, sb, 128), f32),
            pltpu.VMEM((zs // 2, 2, xs, sb, 128), f32),
            pltpu.VMEM((zs // 2, 2, xs, sb, 128), f32),
            pltpu.VMEM((zs // 2, xs - 1, 2, sb, 128), f32),
            pltpu.VMEM((zs // 2, 2, sb, 128), f32),
            pltpu.VMEM((zs - 1, sb, 128), f32),
            pltpu.VMEM((secs * sb, 128), f32),
            pltpu.SemaphoreType.DMA(()),
            pltpu.SemaphoreType.DMA((4 * nj + 4,)),
            pltpu.SemaphoreType.DMA((messages,)),
            pltpu.SemaphoreType.DMA((messages,)),
        ],
        compiler_params=pltpu.CompilerParams(
            collective_id=0, has_side_effects=True, vmem_limit_bytes=40 * 1024 * 1024
        ),
    )(
        *[
            pltpu.with_memory_space_constraint(a, pltpu.HBM)
            for a in (state, velocity, limiter, conductance, potential_prior, owner, slot)
        ],
    )
    return pl.pallas_call(
        write_out,
        out_shape=(
            jax.ShapeDtypeStruct(state.shape, f32),
            jax.ShapeDtypeStruct(conductance.shape, f32),
            jax.ShapeDtypeStruct((cx, cy), f32),
        ),
        in_specs=[vmem] * 3,
        out_specs=(any_space,) * 3,
        scratch_shapes=[pltpu.SemaphoreType.DMA((2 * nj + 1,))],
        compiler_params=pltpu.CompilerParams(vmem_limit_bytes=16 * 1024 * 1024),
    )(*[pltpu.with_memory_space_constraint(r, pltpu.VMEM) for r in results])


def solution(mesh):
    in_specs = (
        P(None, "sec", "blk"),
        P(None, "sec", "blk"),
        P("sec", "blk"),
        P("sec", "blk", None, None),
        P("sec", "blk", None, None),
        P("sec", "blk"),
        P("sec", "blk"),
    )
    out_specs = (P(None, "sec", "blk"), P("sec", "blk"), P("sec", "blk"))
    return jax.shard_map(
        on_device, mesh=mesh, in_specs=in_specs, out_specs=out_specs, check_vma=False
    )
```
